256 devices in a mesh: group: 2 (over core), seq: 32 (over y, z), mp: 4 (over x).
Axes of the slice: x: 4, y: 4, z: 8, core: 2. Of those that a mesh axis runs over, the one named last changes fastest.
Arguments:
- hidden: bfloat16 [2, 4096, 3584], P('group', 'seq', 'mp'), may hold values from -51 to 51
- norm_gain: float32 [2, 3584], P('group'), may hold values from 0.5 to 1.5
- w_q: bfloat16 [2, 3584, 2048], P('group', None, 'mp'), may hold values from -0.09375 to 0.09375
- w_k: bfloat16 [2, 3584, 512], P('group', None, 'mp'), may hold values from -0.09375 to 0.09375
- w_v: bfloat16 [2, 3584, 512], P('group', None, 'mp'), may hold values from -0.09375 to 0.09375
- q_gain: float32 [2, 128], P('group'), may hold values from 0.1 to 1.9
- k_gain: float32 [2, 128], P('group'), may hold values from 0.1 to 1.9
- positions: int32 [2, 4096], P('group', 'seq'), may hold values from 0 to 8191, as said below
- reach: int32 [2, 4096], P('group', 'seq'), may hold values from 0 to 8191, as said below
- grad_out: bfloat16 [2, 4096, 2048], P('group', 'seq', 'mp'), may hold values from -6 to 6
Outputs:
- attended: bfloat16 [2, 4096, 2048], P('group', 'seq', 'mp')
- grad_hidden: bfloat16 [2, 4096, 3584], P('group', 'seq', 'mp')
- grad_w_q: bfloat16 [2, 3584, 2048], P('group', 'seq', 'mp')
- grad_w_k: bfloat16 [2, 3584, 512], P('group', 'seq', 'mp')
- grad_w_v: bfloat16 [2, 3584, 512], P('group', 'seq', 'mp')
The draws below stay inside these ranges and needn't reach their ends.
Inputs may be any that keep to these rules, and one draw needn't show every extreme that they name: Taken over both groups, positions hold each of 0 to 8191 exactly once; within a group they increase along the tokens; all positions of an aligned run of 64 positions belong to one group. A token's reach is at least its own position: it is either its own position (causal text) or the last position of the run of whole blocks that it belongs to (image blocks; every token of group 1 is of this kind).
All inputs are finite; a program needn't handle non-finite values.
Results may differ from the reference program's by a relative error of at most 0.018.
Values may be sent and summed in bfloat16 or wider, within the bound.
No kernel may reach another device: no remote copies, remote signals or barrier semaphores. Data moves between devices by JAX's collectives and lax.ppermute only.
A program may use at most 128 MiB of HBM per device.

```python
import math
import jax
import jax.numpy as jnp
from jax import lax

D = 3584
KVH = 4
HD = 128
QH = 16
BLOCK = 64
G_ROWS = 4096
SEQ_LEN = 8192


def layout(key):
    block_count = SEQ_LEN // BLOCK
    first, second, third = jax.random.split(key, 3)
    order = jax.random.permutation(first, block_count)
    generation = (order < block_count // 2).astype(jnp.int32)
    vision = jax.random.randint(second, (block_count,), 0, 2).astype(jnp.int32)
    renewed = jax.random.randint(third, (block_count,), 0, 4) == 0
    modality = generation * 2 + (1 - generation) * vision
    block_index = jnp.arange(block_count, dtype=jnp.int32)
    previous = jnp.concatenate([jnp.full((1,), -1, jnp.int32), modality[:-1]])
    begins = (modality != previous) | renewed | (block_index == 0)
    marks = jnp.where(begins, block_index, block_count).astype(jnp.int32)
    following = jnp.concatenate([marks[1:], jnp.full((1,), block_count, jnp.int32)])
    next_begin = lax.cummin(following, axis=0, reverse=True)
    last_pos = next_begin * BLOCK - 1
    whole_block = modality > 0
    place = jnp.arange(SEQ_LEN, dtype=jnp.int32)
    block_of = place // BLOCK
    reach_all = jnp.where(whole_block[block_of], last_pos[block_of], place).astype(jnp.int32)
    membership = generation[block_of]
    slots = jnp.argsort(membership, stable=True).astype(jnp.int32)
    return (slots.reshape(2, G_ROWS), reach_all[slots].reshape(2, G_ROWS))


def draw_positions(key, part):
    shared = layout(key)
    return shared[0]


def draw_reach(key, part):
    shared = layout(key)
    return shared[1]


def draw_hidden(key, part):
    key = jax.random.fold_in(key, 7)
    first, second, third = jax.random.split(key, 3)
    feature = jnp.arange(D, dtype=jnp.float32)
    column_scale = jnp.exp(math.log(3.0) * feature / D) * jax.random.uniform(second, (D,), jnp.float32, 0.7, 1.4)
    row_scale = 0.3 * jnp.exp(jax.random.uniform(third, (2, G_ROWS, 1), jnp.float32, 0.0, math.log(10.0)))
    base = jnp.clip(jax.random.normal(first, (2, G_ROWS, D), jnp.float32), -4.0, 4.0)
    return (base * row_scale * column_scale).astype(jnp.bfloat16)


def block_scale(own_key, extent, shards, smallest, largest):
    gain = 1.0
    for dim, blocks in shards:
        heights = jax.random.uniform(jax.random.fold_in(jax.random.fold_in(own_key, 6), dim), (blocks,), jnp.float32, smallest / len(shards), largest / len(shards))
        gain = gain * jnp.repeat(jnp.exp(heights), extent[dim] // blocks).reshape((-1,) + (1,) * (len(extent) - 1 - dim))
    return gain


def noise(key, extent, scale, bound, shards=(), kind=jnp.bfloat16):
    drawn = jax.random.normal(key, extent, jnp.float32) * scale
    if len(shards) > 0:
        drawn = block_scale(key, extent, shards, -0.22, 0.18) * drawn
    return jnp.clip(drawn, min=-bound, max=bound).astype(kind)


def setup_inputs(seed: int = 0) -> dict:
    key_of = jax.random.split(jax.random.key(seed), 11)
    return {
        "hidden": draw_hidden(jax.random.fold_in(key_of[10], 71), 0),
        "norm_gain": jnp.clip(1.0 + 0.1 * jax.random.normal(key_of[1], (2, D), jnp.float32), 0.5, 1.5),
        "w_q": noise(key_of[2], (2, D, QH * HD), D ** -0.5, 0.09375, ((0, 2), (2, 4))),
        "w_k": noise(key_of[3], (2, D, KVH * HD), D ** -0.5, 0.09375, ((0, 2), (2, 4))),
        "w_v": noise(key_of[4], (2, D, KVH * HD), D ** -0.5, 0.09375, ((0, 2), (2, 4))),
        "q_gain": jnp.clip(1.0 + 0.18 * jax.random.normal(key_of[5], (2, HD), jnp.float32), 0.1, 1.9),
        "k_gain": jnp.clip(1.0 + 0.18 * jax.random.normal(key_of[6], (2, HD), jnp.float32), 0.1, 1.9),
        "positions": draw_positions(jax.random.fold_in(key_of[10], 71), 0),
        "reach": draw_reach(jax.random.fold_in(key_of[10], 71), 0),
        "grad_out": noise(key_of[9], (2, G_ROWS, QH * HD), 1.0, 6.0, ((0, 2), (1, 32), (2, 4))),
    }


EPSILON = 1e-06

def normalize(values):
    inverse = lax.rsqrt(lax.optimization_barrier(jnp.mean(values * values, axis=-1, keepdims=True)) + EPSILON)
    return (values * inverse, inverse)

def norm_back(upstream, normal_hat, inverse, weight):
    scaled = weight * upstream
    return inverse * (scaled - normal_hat * lax.optimization_barrier(jnp.mean(scaled * normal_hat, axis=-1, keepdims=True)))

def rounded(values):
    return lax.optimization_barrier(values.astype(jnp.bfloat16)).astype(jnp.float32)

def reference(hidden, norm_gain, w_q, w_k, w_v, q_gain, k_gain, positions, reach, grad_out):
    group_rows = hidden.shape[1]
    head_dim = q_gain.shape[1]
    kv_heads = w_k.shape[2] // head_dim
    per_key = w_q.shape[2] // w_k.shape[2]
    score_scale = head_dim ** (-0.5)
    stored = []
    for member in range(2):
        inputs = hidden[member].astype(jnp.float32)
        input_hat, input_inv = normalize(inputs)
        normed = (input_hat * norm_gain[member]).astype(jnp.bfloat16)
        query_raw = jnp.dot(normed, w_q[member], preferred_element_type=jnp.float32).reshape(group_rows, kv_heads, per_key, head_dim)
        key_raw = jnp.dot(normed, w_k[member], preferred_element_type=jnp.float32).reshape(group_rows, kv_heads, head_dim)
        query_hat, query_inv = normalize(query_raw)
        key_hat, key_inv = normalize(key_raw)
        queries = (query_hat * q_gain[member]).astype(jnp.bfloat16)
        key_rows = (key_hat * k_gain[member]).astype(jnp.bfloat16)
        value_rows = jnp.dot(normed, w_v[member], preferred_element_type=jnp.float32).astype(jnp.bfloat16).reshape(group_rows, kv_heads, head_dim)
        stored.append((input_hat, input_inv, normed, query_hat, query_inv, key_hat, key_inv, queries, key_rows, value_rows))
    key_count = 2 * group_rows
    block_rows = math.gcd(256, key_count)
    block_count = key_count // block_rows
    all_keys = jnp.concatenate([stored[0][8], stored[1][8]]).astype(jnp.float32)
    all_values = jnp.concatenate([stored[0][9], stored[1][9]]).astype(jnp.float32)
    key_pos = positions.reshape(key_count)
    query_blocks = jnp.concatenate([stored[0][7], stored[1][7]]).reshape(block_count, block_rows, kv_heads, per_key, head_dim)
    reach_blocks = reach.reshape(block_count, block_rows)
    grad_blocks = grad_out.reshape(block_count, block_rows, kv_heads, per_key, head_dim)

    def attend(carried, block):
        key_sum, value_sum = carried
        query_tile, reach_tile, grad_tile = block
        query_f = query_tile.astype(jnp.float32)
        grad_f = grad_tile.astype(jnp.float32)
        scores = jnp.einsum('rkqe,jke->rkqj', query_f, all_keys) * score_scale
        visible = (key_pos[None, :] <= reach_tile[:, None])[:, None, None, :]
        weights = jnp.where(visible, jnp.exp(scores), 0.0)
        totals = lax.optimization_barrier(jnp.sum(weights, axis=-1))
        output = jnp.einsum('rkqj,jke->rkqe', rounded(weights), all_values) / totals[..., None]
        row_delta = lax.optimization_barrier(jnp.sum(grad_f * output, axis=-1))
        prob_grad = jnp.einsum('rkqe,jke->rkqj', grad_f, all_values)
        probabilities = weights / totals[..., None]
        score_grad = rounded(probabilities * (prob_grad - row_delta[..., None]) * score_scale)
        query_grad = jnp.einsum('rkqj,jke->rkqe', score_grad, all_keys)
        key_sum = key_sum + jnp.einsum('rkqj,rkqe->jke', score_grad, query_f)
        value_sum = value_sum + jnp.einsum('rkqj,rkqe->jke', rounded(probabilities), grad_f)
        return ((key_sum, value_sum), (output.astype(jnp.bfloat16), query_grad))
    empty = jnp.zeros((key_count, kv_heads, head_dim), jnp.float32)
    (key_sum, value_sum), (attended, query_grad) = lax.scan(attend, (empty, empty), (query_blocks, reach_blocks, grad_blocks))
    attended = attended.reshape(2, group_rows, kv_heads * per_key * head_dim)
    query_grad = query_grad.reshape(2, group_rows, kv_heads, per_key, head_dim)
    input_grads, grads_q, grads_k, grads_v = ([], [], [], [])
    for member in range(2):
        input_hat, input_inv, normed, query_hat, query_inv, key_hat, key_inv = stored[member][:7]
        lower = member * group_rows
        grad_query = norm_back(query_grad[member], query_hat, query_inv, q_gain[member]).astype(jnp.bfloat16).reshape(group_rows, -1)
        grad_key = norm_back(key_sum[lower:lower + group_rows], key_hat, key_inv, k_gain[member]).astype(jnp.bfloat16).reshape(group_rows, -1)
        grad_value = value_sum[lower:lower + group_rows].astype(jnp.bfloat16).reshape(group_rows, -1)
        feature_grad = jnp.dot(grad_query, w_q[member].T, preferred_element_type=jnp.float32)
        feature_grad = feature_grad + jnp.dot(grad_key, w_k[member].T, preferred_element_type=jnp.float32)
        feature_grad = feature_grad + jnp.dot(grad_value, w_v[member].T, preferred_element_type=jnp.float32)
        input_grads.append(norm_back(feature_grad, input_hat, input_inv, norm_gain[member]).astype(jnp.bfloat16))
        grads_q.append(jnp.dot(normed.T, grad_query, preferred_element_type=jnp.float32).astype(jnp.bfloat16))
        grads_k.append(jnp.dot(normed.T, grad_key, preferred_element_type=jnp.float32).astype(jnp.bfloat16))
        grads_v.append(jnp.dot(normed.T, grad_value, preferred_element_type=jnp.float32).astype(jnp.bfloat16))
    return (attended, jnp.stack(input_grads), jnp.stack(grads_q), jnp.stack(grads_k), jnp.stack(grads_v))
```

```python
import jax
import jax.numpy as jnp
from jax import lax
from jax.experimental import pallas as pl
from jax.experimental.pallas import tpu as pltpu
from jax.sharding import PartitionSpec as P

EPSILON = 1e-06
LOG2E = 1.4426950408889634
F32 = jnp.float32
BF16 = jnp.bfloat16
RING = 8
COLUMN = 4
TAIL = 16
VMEM = pl.BlockSpec(memory_space=pltpu.VMEM)
SMEM = pl.BlockSpec(memory_space=pltpu.SMEM)


def nn(left, right):
    return lax.dot_general(left, right, (((1,), (0,)), ((), ())), preferred_element_type=F32)


def nt(left, right):
    return lax.dot_general(left, right, (((1,), (1,)), ((), ())), preferred_element_type=F32)


def tn(left, right):
    return lax.dot_general(left, right, (((0,), (0,)), ((), ())), preferred_element_type=F32)


def shape(dims, dtype):
    return jax.ShapeDtypeStruct(dims, dtype)


def call(body, out_shape, args, smem=0, aliases=None, scratch=(), flops=0, name=None):
    outs = out_shape if isinstance(out_shape, (list, tuple)) else [out_shape]
    return pl.pallas_call(
        body,
        out_shape=out_shape,
        in_specs=[SMEM] * smem + [VMEM] * (len(args) - smem),
        out_specs=[VMEM] * len(outs) if isinstance(out_shape, (list, tuple)) else VMEM,
        scratch_shapes=list(scratch),
        input_output_aliases=aliases or {},
        compiler_params=pltpu.CompilerParams(vmem_limit_bytes=56 * 1024 * 1024),
        cost_estimate=pl.CostEstimate(
            flops=flops,
            bytes_accessed=sum(a.size * a.dtype.itemsize for a in list(args) + list(outs)),
            transcendentals=0,
        ),
        name=name,
    )(*args)


def lanes_of(columns, rows, width=128):
    lane = lax.broadcasted_iota(jnp.int32, (rows, width), 1)
    packed = jnp.zeros((rows, width), F32)
    for index, column in enumerate(columns):
        packed = jnp.where(lane == index, column, packed)
    return packed


def project_body(full, gain, w_q, w_k, w_v, q_gain, k_gain, pos, normed, block, queries, raw, inverses):
    values = full[...].astype(F32)
    rows, width = values.shape
    head = q_gain.shape[1]
    per_key = w_q.shape[1] // head
    inverse = lax.rsqrt(jnp.sum(values * values, axis=-1, keepdims=True) / width + EPSILON)
    normed[...] = (values * inverse * gain[...]).astype(BF16)
    columns = []
    q_raw = nn(normed[...], w_q[...])
    raw[:, : per_key * head] = q_raw
    for index in range(per_key):
        part = q_raw[:, index * head : (index + 1) * head]
        inv = lax.rsqrt(jnp.mean(part * part, axis=-1, keepdims=True) + EPSILON)
        columns.append(inv)
        queries[:, index * head : (index + 1) * head] = (part * inv * q_gain[...]).astype(BF16)
    k_raw = nn(normed[...], w_k[...])
    raw[:, per_key * head : (per_key + 1) * head] = k_raw
    inv = lax.rsqrt(jnp.mean(k_raw * k_raw, axis=-1, keepdims=True) + EPSILON)
    columns.append(inv)
    block[:rows, :] = (k_raw * inv * k_gain[...]).astype(BF16)
    v_raw = nn(normed[...], w_v[...])
    raw[:, (per_key + 1) * head :] = v_raw
    block[rows : 2 * rows, :] = v_raw.astype(BF16)
    block[2 * rows :, :] = pos[...]
    columns.append(inverse)
    inverses[...] = lanes_of(columns, rows)


def turn_body(place, normed, *outs):
    count = len(outs)
    width = normed.shape[1] // count
    for index, out in enumerate(outs):
        start = pl.multiple_of(lax.rem(place[0] + index, count) * width, 128)
        out[...] = normed[:, pl.ds(start, width)].T


def forward_body(tiles, first, last, queries, reach, *refs):
    refs = list(refs)
    sum_in = None if first else refs.pop(0)
    blocks, refs = refs[:tiles], refs[tiles:]
    sum_out, kept = refs[0], refs[1:]
    rows, width = queries.shape
    head = blocks[0].shape[2]
    token_rows = (blocks[0].shape[1] - TAIL) // 2
    heads = width // head
    scale = head ** (-0.5) * LOG2E
    totals = []
    for index in range(heads):
        cols = slice(index * head, (index + 1) * head)
        query = queries[:, cols]
        summed = jnp.zeros((rows, head), F32) if first else sum_in[:, cols]
        total = (
            jnp.zeros((rows, head), F32)
            if first
            else sum_in[:, width + index * head : width + (index + 1) * head]
        )
        for block, keep in zip(blocks, kept):
            count = block.shape[0]
            keys = jnp.concatenate([block[r, :token_rows, :] for r in range(count)], axis=0)
            values = jnp.concatenate(
                [block[r, token_rows : 2 * token_rows, :] for r in range(count)], axis=0
            )
            places = []
            for r in range(count):
                digits = block[r, 2 * token_rows :, :].astype(F32)
                places.append(digits[0:1] * 64.0 + digits[1:2])
            visible = jnp.concatenate(places, axis=1) <= reach[...]
            weights = jnp.where(visible, jnp.exp2(nt(query, keys) * scale), 0.0)
            for r in range(count * token_rows // head):
                total = total + weights[:, r * head : (r + 1) * head]
            rounded = weights.astype(BF16)
            keep[index] = rounded
            summed = summed + nn(rounded, values)
        sum_out[:, cols] = summed
        if last:
            totals.append(jnp.sum(total, axis=-1, keepdims=True))
        else:
            sum_out[:, width + index * head : width + (index + 1) * head] = total
    if last:
        sum_out[:, width:] = lanes_of(totals, rows)


def forward(queries, reach, sums, blocks, first, last):
    rows, width = queries.shape
    head = blocks[0].shape[2]
    keys = blocks[0].shape[0] * (blocks[0].shape[1] - TAIL) // 2
    heads = width // head
    out = [shape((rows, width + (head if last else width)), F32)]
    out += [shape((heads, rows, keys), BF16) for _ in blocks]
    args = [queries, reach] + ([] if first else [sums]) + blocks

    def body(*refs):
        forward_body(len(blocks), first, last, *refs)

    return call(body, out, args, flops=4 * heads * rows * keys * head * len(blocks), name="forward")


def finish_body(mine, theirs, queries, upstream, attended, q_scaled, up_scaled, stats):
    rows, width = queries.shape
    half = rows // 2
    head = 128
    scale = head ** (-0.5)
    deltas, scales = [], []
    for index in range(width // head):
        cols = slice(index * head, (index + 1) * head)

        def joined(where):
            other = theirs[:, where]
            return mine[:, where] + jnp.concatenate([other[half:], other[:half]], axis=0)

        inverse = 1.0 / joined(slice(width + index, width + index + 1))
        output = joined(cols) * inverse
        attended[:, cols] = output[:half].astype(BF16)
        up = upstream[:, cols].astype(F32)
        deltas.append(jnp.sum(up * output, axis=-1, keepdims=True))
        scales.append(inverse * scale)
        up_scaled[:, cols] = (up * inverse).astype(BF16)
        q_scaled[:, cols] = (queries[:, cols].astype(F32) * (inverse * scale)).astype(BF16)
    stats[...] = lanes_of(deltas + scales, rows)


def backward_body(tiles, first, last, upstream, up_scaled, q_scaled, stats, *refs):
    refs = list(refs)
    grad_in = None if first else refs.pop(0)
    blocks, refs = refs[:tiles], refs[tiles:]
    kept, refs = refs[:tiles], refs[tiles:]
    if last:
        own, other = refs[:2]
        terms = refs[2:]
    else:
        grad_out = refs[0]
        terms = refs[1:]
    rows, width = upstream.shape
    half = rows // 2
    head = blocks[0].shape[2]
    token_rows = (blocks[0].shape[1] - TAIL) // 2
    heads = width // head
    grads = [jnp.zeros((rows, head), F32) if first else grad_in[:, h * head : (h + 1) * head] for h in range(heads)]
    for block, keep, term in zip(blocks, kept, terms):
        count = block.shape[0]
        keys = jnp.concatenate([block[r, :token_rows, :] for r in range(count)], axis=0)
        values = jnp.concatenate(
            [block[r, token_rows : 2 * token_rows, :] for r in range(count)], axis=0
        )
        key_term = jnp.zeros((count * token_rows, head), F32)
        value_term = jnp.zeros((count * token_rows, head), F32)
        for index in range(heads):
            cols = slice(index * head, (index + 1) * head)
            weights = keep[index]
            prob_grad = nt(upstream[:, cols], values)
            score_grad = (
                weights.astype(F32) * (prob_grad - stats[:, index : index + 1])
            ).astype(BF16)
            grads[index] = grads[index] + nn(score_grad, keys)
            key_term = key_term + tn(score_grad, q_scaled[:, cols])
            value_term = value_term + tn(weights, up_scaled[:, cols])
        term[:, :head] = key_term.astype(BF16)
        term[:, head:] = value_term.astype(BF16)
    for index in range(heads):
        cols = slice(index * head, (index + 1) * head)
        if last:
            grad = grads[index] * stats[:, heads + index : heads + index + 1]
            own[:, cols] = grad[:half]
            other[:, cols] = grad[half:]
        else:
            grad_out[:, cols] = grads[index]


def backward(upstream, up_scaled, q_scaled, stats, grad, blocks, kept, first, last):
    rows, width = upstream.shape
    head = blocks[0].shape[2]
    keys = kept[0].shape[2]
    out = [shape((rows // 2, width), F32)] * 2 if last else [shape((rows, width), F32)]
    out = out + [shape((keys, 2 * head), BF16) for _ in blocks]
    args = [upstream, up_scaled, q_scaled, stats] + ([] if first else [grad]) + blocks + kept

    def body(*refs):
        backward_body(len(blocks), first, last, *refs)

    return call(body, out, args, flops=8 * rows * keys * width * len(blocks), name="backward")


def back(upstream, hat, inverse, weight):
    scaled = weight * upstream
    return inverse * (scaled - hat * jnp.mean(scaled * hat, axis=-1, keepdims=True))


def query_back_body(mine, theirs, raw, inverses, q_gain, out):
    head = q_gain.shape[1]
    for index in range(mine.shape[1] // head):
        cols = slice(index * head, (index + 1) * head)
        inv = inverses[:, index : index + 1]
        out[:, cols] = back(
            mine[:, cols] + theirs[:, cols], raw[:, cols] * inv, inv, q_gain[...]
        ).astype(BF16)


def key_back_body(a, b, c, d, raw, inverses, k_gain, out):
    head = k_gain.shape[1]
    heads = raw.shape[1] // head - 2
    total = a[...].astype(F32) + b[...].astype(F32) + c[...].astype(F32) + d[...].astype(F32)
    inv = inverses[:, heads : heads + 1]
    hat = raw[:, heads * head : (heads + 1) * head] * inv
    out[:, :head] = back(total[:, :head], hat, inv, k_gain[...]).astype(BF16)
    out[:, head:] = total[:, head:].astype(BF16)


def feature_body(place, grad_q, grad_kv, raw, w_q, w_k, w_v, *outs):
    count = len(outs)
    rows, width = grad_q.shape
    head = w_k.shape[1]
    features = w_q.shape[0] // count
    dot = jnp.sum(grad_q[...].astype(F32) * raw[:, :width], axis=-1, keepdims=True)
    dot = dot + jnp.sum(grad_kv[...].astype(F32) * raw[:, width:], axis=-1, keepdims=True)
    high = dot.astype(BF16).astype(F32)
    tail = lanes_of([high, dot - high], rows).astype(BF16)
    for index, out in enumerate(outs):
        start = pl.multiple_of(lax.rem(place[0] + index, count) * features, 128)
        part = nt(grad_q[...], w_q[pl.ds(start, features), :])
        part = part + nt(grad_kv[:, :head], w_k[pl.ds(start, features), :])
        part = part + nt(grad_kv[:, head:], w_v[pl.ds(start, features), :])
        out[:, :features] = part.astype(BF16)
        out[:, features:] = tail


def input_back_body(a, b, c, d, hidden, inverses, gain, out):
    features = hidden.shape[1]
    total = a[...].astype(F32) + b[...].astype(F32) + c[...].astype(F32) + d[...].astype(F32)
    dot = total[:, features : features + 1] + total[:, features + 1 : features + 2]
    mean = dot / (features * 4)
    inverse = inverses[:, 5:6]
    hat = hidden[...].astype(F32) * inverse
    out[...] = (inverse * (gain[...] * total[:, :features] - hat * mean)).astype(BF16)


def weight_body(place, turned, a, b, c, d, *refs):
    outs, product = refs[:-1], refs[-1]
    grads = jnp.concatenate([a[...], b[...], c[...], d[...]], axis=0)
    product[...] = nn(turned[...], grads).astype(BF16)
    rows = product.shape[0] // RING
    for index, out in enumerate(outs):
        start = pl.multiple_of(lax.rem(place[0] + index, RING) * rows, 16)
        out[...] = product[pl.ds(start, rows), :]


def weight_terms(place, turned, grads):
    rows, columns = turned.shape[0], grads[0].shape[1]
    return call(
        weight_body,
        [shape((rows // RING, columns), BF16)] * RING,
        [place, turned] + grads,
        smem=1,
        scratch=[pltpu.VMEM((rows, columns), BF16)],
        flops=2 * rows * columns * turned.shape[1],
        name="weight_terms",
    )


def along_z(value, step):
    pairs = [
        (y * RING + z, y * RING + (z + step) % RING) for y in range(COLUMN) for z in range(RING)
    ]
    return lax.ppermute(value, "seq", pairs)


def along_y(value, step):
    pairs = [
        (y * RING + z, (y + step) % COLUMN * RING + z) for y in range(COLUMN) for z in range(RING)
    ]
    return lax.ppermute(value, "seq", pairs)


def along_x(value, step):
    return lax.ppermute(value, "mp", [(x, (x + step) % 4) for x in range(4)])


def swapped(value):
    return lax.ppermute(value, "group", [(0, 1), (1, 0)])


def plus(*parts):
    total = parts[0].astype(F32)
    for part in parts[1:]:
        total = total + part.astype(F32)
    return total.astype(BF16)


def ring_sum(terms):
    up, down = terms[4], terms[5]
    for step in range(4):
        up = along_z(up, 1)
        if step < 3:
            up = plus(up, terms[3 - step])
        if step < 3:
            down = along_z(down, -1)
            if step < 2:
                down = plus(down, terms[6 + step])
    return up, down


def on_device(hidden, norm_gain, w_q, w_k, w_v, q_gain, k_gain, positions, reach, grad_out):
    place_x = lax.axis_index("mp").astype(jnp.int32)
    place = lax.axis_index("seq").astype(jnp.int32)
    place_y, place_z = place // RING, lax.rem(place, RING)
    rows, features = hidden.shape[1:]
    width = features * 4
    head = q_gain.shape[1]
    columns = w_q.shape[2]
    gain = norm_gain[0].reshape(1, width)
    local_gain = lax.dynamic_slice(gain, (0, place_x * features), (1, features))
    own_up = grad_out[0]
    upstream = jnp.concatenate([own_up, swapped(own_up)], axis=0)
    all_reach = jnp.concatenate([reach[0], swapped(reach)[0]]).astype(F32).reshape(2 * rows, 1)
    high = positions[0] // 64
    digits = jnp.stack([high, positions[0] - high * 64] + [high] * (TAIL - 2)).astype(BF16)
    full = lax.all_gather(hidden[0], "mp", axis=1, tiled=True)
    normed, block, queries, raw, inverses = call(
        project_body,
        [
            shape((rows, width), BF16),
            shape((2 * rows + TAIL, head), BF16),
            shape((rows, columns), BF16),
            shape((rows, columns + 2 * head), F32),
            shape((rows, 128), F32),
        ],
        [full, gain, w_q[0], w_k[0], w_v[0], q_gain, k_gain, digits],
        flops=2 * rows * width * (columns + 2 * head),
        name="project",
    )
    stack = jnp.stack([block] + [along_y(block, step) for step in range(1, COLUMN)])
    all_queries = jnp.concatenate([queries, swapped(queries)], axis=0)
    blocks = {0: stack}
    up = down = stack
    for step in range(1, 5):
        up = along_z(up, 1)
        blocks[-step] = up
        if step < 4:
            down = along_z(down, -1)
            blocks[step] = down
    turned = call(
        turn_body,
        [shape((features, rows), BF16)] * COLUMN,
        [place_y.reshape(1), normed],
        smem=1,
        name="turn",
    )
    turned = jnp.concatenate(
        [turned[0]] + [along_y(turned[step], step) for step in range(1, COLUMN)], axis=1
    )

    kept = {}
    sums = None
    order = [(0,), (-1, 1), (-2, 2), (-3, 3), (-4,)]
    for number, group in enumerate(order):
        outs = forward(
            all_queries,
            all_reach,
            sums,
            [blocks[k] for k in group],
            number == 0,
            number == len(order) - 1,
        )
        sums = outs[0]
        for k, keep in zip(group, outs[1:]):
            kept[k] = keep
    attended, q_scaled, up_scaled, stats = call(
        finish_body,
        [
            shape((rows, columns), BF16),
            shape((2 * rows, columns), BF16),
            shape((2 * rows, columns), BF16),
            shape((2 * rows, 128), F32),
        ],
        [sums, swapped(sums), all_queries, upstream],
        name="finish",
    )
    terms = {}
    grad = None
    order = [(-4, -3), (3, -2), (2, -1), (1, 0)]
    for number, group in enumerate(order):
        last = number == len(order) - 1
        outs = backward(
            upstream,
            up_scaled,
            q_scaled,
            stats,
            grad,
            [blocks[k] for k in group],
            [kept[k] for k in group],
            number == 0,
            last,
        )
        if last:
            grad_own, grad_other = outs[:2]
            outs = outs[2:]
        else:
            grad, outs = outs[0], outs[1:]
        for k, term in zip(group, outs):
            terms[k % RING] = term
    grad_q = call(
        query_back_body,
        shape((rows, columns), BF16),
        [grad_own, swapped(grad_other), raw, inverses, q_gain],
        name="query_back",
    )
    up, down = ring_sum([terms[k] for k in range(RING)])
    own_terms = plus(terms[0], up, down).reshape(COLUMN, rows, 2 * head)
    parts = [own_terms[0]] + [along_y(own_terms[step], -step) for step in range(1, COLUMN)]
    grad_kv = call(
        key_back_body,
        shape((rows, 2 * head), BF16),
        parts + [raw, inverses, k_gain],
        name="key_back",
    )
    z_index = place_z.reshape(1)
    query_terms = weight_terms(
        z_index, turned, [grad_q] + [along_y(grad_q, step) for step in range(1, COLUMN)]
    )
    up, down = ring_sum(query_terms)
    grad_wq = plus(query_terms[0], up, down)
    key_terms = weight_terms(
        z_index, turned, [grad_kv] + [along_y(grad_kv, step) for step in range(1, COLUMN)]
    )
    up, down = ring_sum(key_terms)
    grad_wkv = plus(key_terms[0], up, down)
    feature_parts = call(
        feature_body,
        [shape((rows, features + 128), BF16)] * 4,
        [place_x.reshape(1), grad_q, grad_kv, raw, w_q[0], w_k[0], w_v[0]],
        smem=1,
        flops=2 * rows * width * (columns + 2 * head),
        name="feature",
    )
    feature_parts = [feature_parts[0]] + [along_x(feature_parts[k], k) for k in range(1, 4)]
    input_grad = call(
        input_back_body,
        shape((rows, features), BF16),
        feature_parts + [hidden[0], inverses, local_gain],
        name="input_back",
    )
    return (
        attended[None],
        input_grad[None],
        grad_wq[None],
        grad_wkv[None, :, :head],
        grad_wkv[None, :, head:],
    )


def solution(mesh):
    return jax.shard_map(
        on_device,
        mesh=mesh,
        in_specs=(
            P("group", "seq", "mp"),
            P("group", None),
            P("group", None, "mp"),
            P("group", None, "mp"),
            P("group", None, "mp"),
            P("group", None),
            P("group", None),
            P("group", "seq"),
            P("group", "seq"),
            P("group", "seq", "mp"),
        ),
        out_specs=(P("group", "seq", "mp"),) * 5,
        check_vma=False,
    )
```

```python
import jax
import jax.numpy as jnp
from jax import lax
from jax.experimental import pallas as pl
from jax.experimental.pallas import tpu as pltpu
from jax.sharding import PartitionSpec as P

EPSILON = 1e-06
LOG2E = 1.4426950408889634
F32 = jnp.float32
BF16 = jnp.bfloat16
RING = 8
COLUMN = 4
TAIL = 16
VMEM = pl.BlockSpec(memory_space=pltpu.VMEM)
SMEM = pl.BlockSpec(memory_space=pltpu.SMEM)


def nn(left, right):
    return lax.dot_general(left, right, (((1,), (0,)), ((), ())), preferred_element_type=F32)


def nt(left, right):
    return lax.dot_general(left, right, (((1,), (1,)), ((), ())), preferred_element_type=F32)


def tn(left, right):
    return lax.dot_general(left, right, (((0,), (0,)), ((), ())), preferred_element_type=F32)


def shape(dims, dtype):
    return jax.ShapeDtypeStruct(dims, dtype)


def call(body, out_shape, args, smem=0, aliases=None, scratch=(), micros=2.0, name=None):
    outs = out_shape if isinstance(out_shape, (list, tuple)) else [out_shape]
    return pl.pallas_call(
        body,
        out_shape=out_shape,
        in_specs=[SMEM] * smem + [VMEM] * (len(args) - smem),
        out_specs=[VMEM] * len(outs) if isinstance(out_shape, (list, tuple)) else VMEM,
        scratch_shapes=list(scratch),
        input_output_aliases=aliases or {},
        compiler_params=pltpu.CompilerParams(vmem_limit_bytes=24 * 1024 * 1024),
        cost_estimate=pl.CostEstimate(
            flops=int(micros * 1.15e9),
            bytes_accessed=0,
            transcendentals=0,
        ),
        name=name,
    )(*args)


def lanes_of(columns, rows, width=128):
    lane = lax.broadcasted_iota(jnp.int32, (rows, width), 1)
    packed = jnp.zeros((rows, width), F32)
    for index, column in enumerate(columns):
        packed = jnp.where(lane == index, column, packed)
    return packed


def project_body(full, gain, w_q, w_k, w_v, q_gain, k_gain, pos, normed, block, queries, raw, inverses):
    values = full[...].astype(F32)
    rows, width = values.shape
    head = q_gain.shape[1]
    per_key = w_q.shape[1] // head
    inverse = lax.rsqrt(jnp.sum(values * values, axis=-1, keepdims=True) / width + EPSILON)
    normed[...] = (values * inverse * gain[...]).astype(BF16)
    columns = []
    q_raw = nn(normed[...], w_q[...])
    raw[:, : per_key * head] = q_raw
    for index in range(per_key):
        part = q_raw[:, index * head : (index + 1) * head]
        inv = lax.rsqrt(jnp.mean(part * part, axis=-1, keepdims=True) + EPSILON)
        columns.append(inv)
        queries[:, index * head : (index + 1) * head] = (part * inv * q_gain[...]).astype(BF16)
    k_raw = nn(normed[...], w_k[...])
    raw[:, per_key * head : (per_key + 1) * head] = k_raw
    inv = lax.rsqrt(jnp.mean(k_raw * k_raw, axis=-1, keepdims=True) + EPSILON)
    columns.append(inv)
    block[:rows, :] = (k_raw * inv * k_gain[...]).astype(BF16)
    v_raw = nn(normed[...], w_v[...])
    raw[:, (per_key + 1) * head :] = v_raw
    block[rows : 2 * rows, :] = v_raw.astype(BF16)
    high = lax.shift_right_logical(pos[...], 6)
    row = lax.broadcasted_iota(jnp.int32, (TAIL, rows), 0)
    digits = jnp.where(row == 0, high, jnp.where(row == 1, pos[...] - high * 64, 0))
    block[2 * rows :, :] = digits.astype(F32).astype(BF16)
    columns.append(inverse)
    inverses[...] = lanes_of(columns, rows)


def turn_body(place, normed, *outs):
    count = len(outs)
    width = normed.shape[1] // count
    for index, out in enumerate(outs):
        start = pl.multiple_of(lax.rem(place[0] + index, count) * width, 128)
        out[...] = normed[:, pl.ds(start, width)].T


def forward_body(tiles, first, last, queries, reach, *refs):
    refs = list(refs)
    sum_in = None if first else refs.pop(0)
    blocks, refs = refs[:tiles], refs[tiles:]
    sum_out, kept = refs[0], refs[1:]
    rows, width = queries.shape
    head = blocks[0].shape[2]
    token_rows = (blocks[0].shape[1] - TAIL) // 2
    heads = width // head
    scale = head ** (-0.5) * LOG2E
    totals = []
    for index in range(heads):
        cols = slice(index * head, (index + 1) * head)
        query = queries[:, cols]
        summed = jnp.zeros((rows, head), F32) if first else sum_in[:, cols]
        total = (
            jnp.zeros((rows, head), F32)
            if first
            else sum_in[:, width + index * head : width + (index + 1) * head]
        )
        for block, keep in zip(blocks, kept):
            count = block.shape[0]
            keys = jnp.concatenate([block[r, :token_rows, :] for r in range(count)], axis=0)
            values = jnp.concatenate(
                [block[r, token_rows : 2 * token_rows, :] for r in range(count)], axis=0
            )
            places = []
            for r in range(count):
                digits = block[r, 2 * token_rows :, :].astype(F32)
                places.append(digits[0:1] * 64.0 + digits[1:2])
            visible = jnp.concatenate(places, axis=1) <= reach[...]
            weights = jnp.where(visible, jnp.exp2(nt(query, keys) * scale), 0.0)
            for r in range(count * token_rows // head):
                total = total + weights[:, r * head : (r + 1) * head]
            rounded = weights.astype(BF16)
            keep[index] = rounded
            summed = summed + nn(rounded, values)
        sum_out[:, cols] = summed
        if last:
            totals.append(jnp.sum(total, axis=-1, keepdims=True))
        else:
            sum_out[:, width + index * head : width + (index + 1) * head] = total
    if last:
        sum_out[:, width:] = lanes_of(totals, rows)


def forward(queries, reach, sums, blocks, first, last):
    rows, width = queries.shape
    head = blocks[0].shape[2]
    keys = blocks[0].shape[0] * (blocks[0].shape[1] - TAIL) // 2
    heads = width // head
    out = [shape((rows, width + (head if last else width)), F32)]
    out += [shape((heads, rows, keys), BF16) for _ in blocks]
    args = [queries, reach] + ([] if first else [sums]) + blocks

    def body(*refs):
        forward_body(len(blocks), first, last, *refs)

    return call(body, out, args, micros=2.2 * len(blocks), name="forward")


def finish_body(mine, theirs, queries, upstream, attended, q_scaled, up_scaled, stats):
    rows, width = queries.shape
    half = rows // 2
    head = 128
    scale = head ** (-0.5)
    deltas, scales = [], []
    for index in range(width // head):
        cols = slice(index * head, (index + 1) * head)

        def joined(where):
            other = theirs[:, where]
            return mine[:, where] + jnp.concatenate([other[half:], other[:half]], axis=0)

        inverse = 1.0 / joined(slice(width + index, width + index + 1))
        output = joined(cols) * inverse
        attended[:, cols] = output[:half].astype(BF16)
        up = upstream[:, cols].astype(F32)
        deltas.append(jnp.sum(up * output, axis=-1, keepdims=True))
        scales.append(inverse * scale)
        up_scaled[:, cols] = (up * inverse).astype(BF16)
        q_scaled[:, cols] = (queries[:, cols].astype(F32) * (inverse * scale)).astype(BF16)
    stats[...] = lanes_of(deltas + scales, rows)


def backward_body(tiles, first, last, upstream, up_scaled, q_scaled, stats, *refs):
    refs = list(refs)
    grad_in = None if first else refs.pop(0)
    blocks, refs = refs[:tiles], refs[tiles:]
    kept, refs = refs[:tiles], refs[tiles:]
    if last:
        own, other = refs[:2]
        terms = refs[2:]
    else:
        grad_out = refs[0]
        terms = refs[1:]
    rows, width = upstream.shape
    half = rows // 2
    head = blocks[0].shape[2]
    token_rows = (blocks[0].shape[1] - TAIL) // 2
    heads = width // head
    grads = [jnp.zeros((rows, head), F32) if first else grad_in[:, h * head : (h + 1) * head] for h in range(heads)]
    for block, keep, term in zip(blocks, kept, terms):
        count = block.shape[0]
        keys = jnp.concatenate([block[r, :token_rows, :] for r in range(count)], axis=0)
        values = jnp.concatenate(
            [block[r, token_rows : 2 * token_rows, :] for r in range(count)], axis=0
        )
        key_term = jnp.zeros((count * token_rows, head), F32)
        value_term = jnp.zeros((count * token_rows, head), F32)
        for index in range(heads):
            cols = slice(index * head, (index + 1) * head)
            weights = keep[index]
            prob_grad = nt(upstream[:, cols], values)
            score_grad = (
                weights.astype(F32) * (prob_grad - stats[:, index : index + 1])
            ).astype(BF16)
            grads[index] = grads[index] + nn(score_grad, keys)
            key_term = key_term + tn(score_grad, q_scaled[:, cols])
            value_term = value_term + tn(weights, up_scaled[:, cols])
        term[:, :head] = key_term.astype(BF16)
        term[:, head:] = value_term.astype(BF16)
    for index in range(heads):
        cols = slice(index * head, (index + 1) * head)
        if last:
            grad = grads[index] * stats[:, heads + index : heads + index + 1]
            own[:, cols] = grad[:half]
            other[:, cols] = grad[half:]
        else:
            grad_out[:, cols] = grads[index]


def backward(upstream, up_scaled, q_scaled, stats, grad, blocks, kept, first, last):
    rows, width = upstream.shape
    head = blocks[0].shape[2]
    keys = kept[0].shape[2]
    out = [shape((rows // 2, width), F32)] * 2 if last else [shape((rows, width), F32)]
    out = out + [shape((keys, 2 * head), BF16) for _ in blocks]
    args = [upstream, up_scaled, q_scaled, stats] + ([] if first else [grad]) + blocks + kept

    def body(*refs):
        backward_body(len(blocks), first, last, *refs)

    return call(body, out, args, micros=2.5 * len(blocks), name="backward")


def back(upstream, hat, inverse, weight):
    scaled = weight * upstream
    return inverse * (scaled - hat * jnp.mean(scaled * hat, axis=-1, keepdims=True))


def query_back_body(mine, theirs, raw, inverses, q_gain, out):
    head = q_gain.shape[1]
    for index in range(mine.shape[1] // head):
        cols = slice(index * head, (index + 1) * head)
        inv = inverses[:, index : index + 1]
        out[:, cols] = back(
            mine[:, cols] + theirs[:, cols], raw[:, cols] * inv, inv, q_gain[...]
        ).astype(BF16)


def key_back_body(a, b, c, d, raw, inverses, k_gain, out):
    head = k_gain.shape[1]
    heads = raw.shape[1] // head - 2
    total = a[...].astype(F32) + b[...].astype(F32) + c[...].astype(F32) + d[...].astype(F32)
    inv = inverses[:, heads : heads + 1]
    hat = raw[:, heads * head : (heads + 1) * head] * inv
    out[:, :head] = back(total[:, :head], hat, inv, k_gain[...]).astype(BF16)
    out[:, head:] = total[:, head:].astype(BF16)


def feature_body(place, grad_q, grad_kv, raw, w_q, w_k, w_v, *outs):
    count = len(outs)
    rows, width = grad_q.shape
    head = w_k.shape[1]
    features = w_q.shape[0] // count
    dot = jnp.sum(grad_q[...].astype(F32) * raw[:, :width], axis=-1, keepdims=True)
    dot = dot + jnp.sum(grad_kv[...].astype(F32) * raw[:, width:], axis=-1, keepdims=True)
    high = dot.astype(BF16).astype(F32)
    tail = lanes_of([high, dot - high], rows).astype(BF16)
    for index, out in enumerate(outs):
        start = pl.multiple_of(lax.rem(place[0] + index, count) * features, 128)
        part = nt(grad_q[...], w_q[pl.ds(start, features), :])
        part = part + nt(grad_kv[:, :head], w_k[pl.ds(start, features), :])
        part = part + nt(grad_kv[:, head:], w_v[pl.ds(start, features), :])
        out[:, :features] = part.astype(BF16)
        out[:, features:] = tail


def input_back_body(a, b, c, d, hidden, inverses, gain, out):
    features = hidden.shape[1]
    total = a[...].astype(F32) + b[...].astype(F32) + c[...].astype(F32) + d[...].astype(F32)
    dot = total[:, features : features + 1] + total[:, features + 1 : features + 2]
    mean = dot / (features * 4)
    inverse = inverses[:, 5:6]
    hat = hidden[...].astype(F32) * inverse
    out[...] = (inverse * (gain[...] * total[:, :features] - hat * mean)).astype(BF16)


def weight_body(*refs):
    turned = jnp.concatenate([ref[...] for ref in refs[:COLUMN]], axis=1)
    grads = jnp.concatenate([ref[...] for ref in refs[COLUMN:-1]], axis=0)
    refs[-1][...] = nn(turned, grads).astype(BF16)


def weight_sum(turned, grads):
    rows, columns = turned[0].shape[0], grads[0].shape[1]
    terms = call(
        weight_body, shape((rows, columns), BF16), turned + grads, name="weight_terms"
    )
    rings = [[y * RING + z for z in range(RING)] for y in range(COLUMN)]
    terms = lax.all_to_all(terms, "seq", 0, 0, axis_index_groups=rings, tiled=True)
    terms = terms.reshape(RING, rows // RING, columns)
    return plus(*[terms[k] for k in range(RING)])


def along_z(value, step):
    pairs = [
        (y * RING + z, y * RING + (z + step) % RING) for y in range(COLUMN) for z in range(RING)
    ]
    return lax.ppermute(value, "seq", pairs)


def along_y(value, step):
    pairs = [
        (y * RING + z, (y + step) % COLUMN * RING + z) for y in range(COLUMN) for z in range(RING)
    ]
    return lax.ppermute(value, "seq", pairs)


def along_x(value, step):
    return lax.ppermute(value, "mp", [(x, (x + step) % 4) for x in range(4)])


def swapped(value):
    return lax.ppermute(value, "group", [(0, 1), (1, 0)])


def plus(*parts):
    total = parts[0].astype(F32)
    for part in parts[1:]:
        total = total + part.astype(F32)
    return total.astype(BF16)


def on_device(hidden, norm_gain, w_q, w_k, w_v, q_gain, k_gain, positions, reach, grad_out):
    place_x = lax.axis_index("mp").astype(jnp.int32)
    place = lax.axis_index("seq").astype(jnp.int32)
    place_y = place // RING
    rows, features = hidden.shape[1:]
    width = features * 4
    head = q_gain.shape[1]
    columns = w_q.shape[2]
    gain = norm_gain[0].reshape(1, width)
    local_gain = lax.dynamic_slice(gain, (0, place_x * features), (1, features))
    full = lax.all_gather(hidden[0], "mp", axis=1, tiled=True)
    full, other_up, other_reach = lax.optimization_barrier(
        (full, swapped(grad_out[0]), swapped(reach))
    )
    upstream = jnp.concatenate([grad_out[0], other_up], axis=0)
    all_reach = jnp.concatenate([reach[0], other_reach[0]]).astype(F32).reshape(2 * rows, 1)
    normed, block, queries, raw, inverses = call(
        project_body,
        [
            shape((rows, width), BF16),
            shape((2 * rows + TAIL, head), BF16),
            shape((rows, columns), BF16),
            shape((rows, columns + 2 * head), F32),
            shape((rows, 128), F32),
        ],
        [full, gain, w_q[0], w_k[0], w_v[0], q_gain, k_gain, positions],
        micros=4.0,
        name="project",
    )
    stack = jnp.stack([block] + [along_y(block, step) for step in range(1, COLUMN)])
    all_queries = jnp.concatenate([queries, swapped(queries)], axis=0)
    blocks = {0: stack}
    up = down = stack
    for step in range(1, 5):
        up = along_z(up, 1)
        blocks[-step] = up
        if step < 4:
            down = along_z(down, -1)
            blocks[step] = down
    kept = {}
    sums = None
    order = [(0,), (-1, 1), (-2, 2), (-3, 3), (-4,)]
    for number, group in enumerate(order):
        if number == 1:
            sums, normed = lax.optimization_barrier((sums, normed))
            turned = call(
                turn_body,
                [shape((features, rows), BF16)] * COLUMN,
                [place_y.reshape(1), normed],
                smem=1,
                name="turn",
            )
            turned = [turned[0]] + [along_y(turned[step], step) for step in range(1, COLUMN)]
        if number == 3:
            sums, turned = lax.optimization_barrier((sums, turned))
        outs = forward(
            all_queries,
            all_reach,
            sums,
            [blocks[k] for k in group],
            number == 0,
            number == len(order) - 1,
        )
        sums = outs[0]
        for k, keep in zip(group, outs[1:]):
            kept[k] = keep
    attended, q_scaled, up_scaled, stats = call(
        finish_body,
        [
            shape((rows, columns), BF16),
            shape((2 * rows, columns), BF16),
            shape((2 * rows, columns), BF16),
            shape((2 * rows, 128), F32),
        ],
        [sums, swapped(sums), all_queries, upstream],
        name="finish",
    )
    terms = {}
    grad = None
    order = [(-4, -3), (3, -2), (2, -1), (1, 0)]
    up = down = None
    for number, group in enumerate(order):
        last = number == len(order) - 1
        if number == 1:
            up, down = along_z(terms[4], 1), along_z(terms[5], -1)
        if number > 1:
            grad, up, down = lax.optimization_barrier((grad, up, down))
            up = along_z(plus(up, terms[5 - number]), 1)
            down = along_z(plus(down, terms[4 + number]), -1)
        outs = backward(
            upstream,
            up_scaled,
            q_scaled,
            stats,
            grad,
            [blocks[k] for k in group],
            [kept[k] for k in group],
            number == 0,
            last,
        )
        if last:
            grad_own, grad_other = outs[:2]
            outs = outs[2:]
        else:
            grad, outs = outs[0], outs[1:]
        for k, term in zip(group, outs):
            terms[k % RING] = term
    grad_q = call(
        query_back_body,
        shape((rows, columns), BF16),
        [grad_own, swapped(grad_other), raw, inverses, q_gain],
        name="query_back",
    )
    up = along_z(plus(up, terms[1]), 1)
    own_terms = plus(terms[0], up, down).reshape(COLUMN, rows, 2 * head)
    parts = [own_terms[0]] + [along_y(own_terms[step], -step) for step in range(1, COLUMN)]
    grad_kv = call(
        key_back_body,
        shape((rows, 2 * head), BF16),
        parts + [raw, inverses, k_gain],
        name="key_back",
    )
    query_grads = [grad_q] + [along_y(grad_q, step) for step in range(1, COLUMN)]
    grad_wq = weight_sum(turned, query_grads)
    key_grads = [along_y(grad_kv, step) for step in range(1, COLUMN)]
    feature_parts = call(
        feature_body,
        [shape((rows, features + 128), BF16)] * 4,
        [place_x.reshape(1), grad_q, grad_kv, raw, w_q[0], w_k[0], w_v[0]],
        smem=1,
        micros=5.0,
        name="feature",
    )
    feature_parts, key_grads = lax.optimization_barrier((feature_parts, key_grads))
    grad_wkv = weight_sum(turned, [grad_kv] + key_grads)
    feature_parts = [feature_parts[0]] + [along_x(feature_parts[k], k) for k in range(1, 4)]
    input_grad = call(
        input_back_body,
        shape((rows, features), BF16),
        feature_parts + [hidden[0], inverses, local_gain],
        name="input_back",
    )
    return (
        attended[None],
        input_grad[None],
        grad_wq[None],
        grad_wkv[None, :, :head],
        grad_wkv[None, :, head:],
    )


def solution(mesh):
    return jax.shard_map(
        on_device,
        mesh=mesh,
        in_specs=(
            P("group", "seq", "mp"),
            P("group", None),
            P("group", None, "mp"),
            P("group", None, "mp"),
            P("group", None, "mp"),
            P("group", None),
            P("group", None),
            P("group", "seq"),
            P("group", "seq"),
            P("group", "seq", "mp"),
        ),
        out_specs=(P("group", "seq", "mp"),) * 5,
        check_vma=False,
    )
```

```python
import jax
import jax.numpy as jnp
from jax import lax
from jax.experimental import pallas as pl
from jax.experimental.pallas import tpu as pltpu
from jax.sharding import PartitionSpec as P

EPSILON = 1e-06
LOG2E = 1.4426950408889634
F32 = jnp.float32
BF16 = jnp.bfloat16
RING = 8
COLUMN = 4
TAIL = 16
VMEM = pl.BlockSpec(memory_space=pltpu.VMEM)
SMEM = pl.BlockSpec(memory_space=pltpu.SMEM)
FAR = pl.BlockSpec(memory_space=pltpu.HBM)


def nn(left, right):
    return lax.dot_general(left, right, (((1,), (0,)), ((), ())), preferred_element_type=F32)


def nt(left, right):
    return lax.dot_general(left, right, (((1,), (1,)), ((), ())), preferred_element_type=F32)


def tn(left, right):
    return lax.dot_general(left, right, (((0,), (0,)), ((), ())), preferred_element_type=F32)


def shape(dims, dtype):
    return jax.ShapeDtypeStruct(dims, dtype)


def call(body, out_shape, args, smem=0, far=(), scratch=(), micros=2.0, name=None):
    outs = out_shape if isinstance(out_shape, (list, tuple)) else [out_shape]
    return pl.pallas_call(
        body,
        out_shape=out_shape,
        in_specs=[
            SMEM if index < smem else FAR if index in far else VMEM for index in range(len(args))
        ],
        out_specs=[VMEM] * len(outs) if isinstance(out_shape, (list, tuple)) else VMEM,
        scratch_shapes=list(scratch),
        compiler_params=pltpu.CompilerParams(vmem_limit_bytes=14 * 1024 * 1024),
        cost_estimate=pl.CostEstimate(
            flops=int(micros * 1.15e9),
            bytes_accessed=0,
            transcendentals=0,
        ),
        name=name,
    )(*args)


def lanes_of(columns, rows, width=128):
    lane = lax.broadcasted_iota(jnp.int32, (rows, width), 1)
    packed = jnp.zeros((rows, width), F32)
    for index, column in enumerate(columns):
        packed = jnp.where(lane == index, column, packed)
    return packed


def project_body(full, gain, far_q, far_k, far_v, q_gain, k_gain, pos, *refs):
    normed, block, queries, raw, inverses, w_q, w_k, w_v, sems = refs
    copies = [
        pltpu.make_async_copy(source, target, sems.at[index])
        for index, (source, target) in enumerate(((far_k, w_k), (far_v, w_v), (far_q, w_q)))
    ]
    for copy in copies:
        copy.start()
    values = full[...].astype(F32)
    rows, width = values.shape
    head = q_gain.shape[1]
    per_key = w_q.shape[1] // head
    inverse = lax.rsqrt(jnp.sum(values * values, axis=-1, keepdims=True) / width + EPSILON)
    normed[...] = (values * inverse * gain[...]).astype(BF16)
    columns = []
    for copy in copies:
        copy.wait()
    q_raw = nn(normed[...], w_q[...])
    raw[:, : per_key * head] = q_raw
    for index in range(per_key):
        part = q_raw[:, index * head : (index + 1) * head]
        inv = lax.rsqrt(jnp.mean(part * part, axis=-1, keepdims=True) + EPSILON)
        columns.append(inv)
        queries[:, index * head : (index + 1) * head] = (part * inv * q_gain[...]).astype(BF16)
    k_raw = nn(normed[...], w_k[...])
    raw[:, per_key * head : (per_key + 1) * head] = k_raw
    inv = lax.rsqrt(jnp.mean(k_raw * k_raw, axis=-1, keepdims=True) + EPSILON)
    columns.append(inv)
    block[:rows, :] = (k_raw * inv * k_gain[...]).astype(BF16)
    v_raw = nn(normed[...], w_v[...])
    raw[:, (per_key + 1) * head :] = v_raw
    block[rows : 2 * rows, :] = v_raw.astype(BF16)
    high = lax.shift_right_logical(pos[...], 6)
    row = lax.broadcasted_iota(jnp.int32, (TAIL, rows), 0)
    digits = jnp.where(row == 0, high, jnp.where(row == 1, pos[...] - high * 64, 0))
    block[2 * rows :, :] = digits.astype(F32).astype(BF16)
    columns.append(inverse)
    inverses[...] = lanes_of(columns, rows)


def turn_body(place, normed, *outs):
    count = len(outs)
    width = normed.shape[1] // count
    for index, out in enumerate(outs):
        start = pl.multiple_of(lax.rem(place[0] + index, count) * width, 128)
        out[...] = normed[:, pl.ds(start, width)].T


def forward_body(tiles, first, last, queries, reach, *refs):
    refs = list(refs)
    sum_in = None if first else refs.pop(0)
    blocks, refs = refs[:tiles], refs[tiles:]
    sum_out, kept = refs[0], refs[1:]
    rows, width = queries.shape
    head = blocks[0].shape[2]
    token_rows = (blocks[0].shape[1] - TAIL) // 2
    heads = width // head
    scale = head ** (-0.5) * LOG2E
    totals = []
    for index in range(heads):
        cols = slice(index * head, (index + 1) * head)
        query = queries[:, cols]
        summed = jnp.zeros((rows, head), F32) if first else sum_in[:, cols]
        total = (
            jnp.zeros((rows, head), F32)
            if first
            else sum_in[:, width + index * head : width + (index + 1) * head]
        )
        for block, keep in zip(blocks, kept):
            count = block.shape[0]
            keys = jnp.concatenate([block[r, :token_rows, :] for r in range(count)], axis=0)
            values = jnp.concatenate(
                [block[r, token_rows : 2 * token_rows, :] for r in range(count)], axis=0
            )
            places = []
            for r in range(count):
                digits = block[r, 2 * token_rows :, :].astype(F32)
                places.append(digits[0:1] * 64.0 + digits[1:2])
            visible = jnp.concatenate(places, axis=1) <= reach[...]
            weights = jnp.where(visible, jnp.exp2(nt(query, keys) * scale), 0.0)
            for r in range(count * token_rows // head):
                total = total + weights[:, r * head : (r + 1) * head]
            rounded = weights.astype(BF16)
            keep[index] = rounded
            summed = summed + nn(rounded, values)
        sum_out[:, cols] = summed
        if last:
            totals.append(jnp.sum(total, axis=-1, keepdims=True))
        else:
            sum_out[:, width + index * head : width + (index + 1) * head] = total
    if last:
        sum_out[:, width:] = lanes_of(totals, rows)


def forward(queries, reach, sums, blocks, first, last):
    rows, width = queries.shape
    head = blocks[0].shape[2]
    keys = blocks[0].shape[0] * (blocks[0].shape[1] - TAIL) // 2
    heads = width // head
    out = [shape((rows, width + (head if last else width)), F32)]
    out += [shape((heads, rows, keys), BF16) for _ in blocks]
    args = [queries, reach] + ([] if first else [sums]) + blocks

    def body(*refs):
        forward_body(len(blocks), first, last, *refs)

    return call(body, out, args, micros=0.6 * len(blocks), name="forward")


def finish_body(mine, theirs, queries, upstream, attended, q_scaled, up_scaled, stats):
    rows, width = queries.shape
    half = rows // 2
    head = 128
    scale = head ** (-0.5)
    deltas, scales = [], []
    for index in range(width // head):
        cols = slice(index * head, (index + 1) * head)

        def joined(where):
            other = theirs[:, where]
            return mine[:, where] + jnp.concatenate([other[half:], other[:half]], axis=0)

        inverse = 1.0 / joined(slice(width + index, width + index + 1))
        output = joined(cols) * inverse
        attended[:, cols] = output[:half].astype(BF16)
        up = upstream[:, cols].astype(F32)
        deltas.append(jnp.sum(up * output, axis=-1, keepdims=True))
        scales.append(inverse * scale)
        up_scaled[:, cols] = (up * inverse).astype(BF16)
        q_scaled[:, cols] = (queries[:, cols].astype(F32) * (inverse * scale)).astype(BF16)
    stats[...] = lanes_of(deltas + scales, rows)


def backward_body(tiles, first, last, upstream, up_scaled, q_scaled, stats, *refs):
    refs = list(refs)
    grad_in = None if first else refs.pop(0)
    blocks, refs = refs[:tiles], refs[tiles:]
    kept, refs = refs[:tiles], refs[tiles:]
    if last:
        own, other = refs[:2]
        terms = refs[2:]
    else:
        grad_out = refs[0]
        terms = refs[1:]
    rows, width = upstream.shape
    half = rows // 2
    head = blocks[0].shape[2]
    token_rows = (blocks[0].shape[1] - TAIL) // 2
    heads = width // head
    grads = [jnp.zeros((rows, head), F32) if first else grad_in[:, h * head : (h + 1) * head] for h in range(heads)]
    for block, keep, term in zip(blocks, kept, terms):
        count = block.shape[0]
        keys = jnp.concatenate([block[r, :token_rows, :] for r in range(count)], axis=0)
        values = jnp.concatenate(
            [block[r, token_rows : 2 * token_rows, :] for r in range(count)], axis=0
        )
        key_term = jnp.zeros((count * token_rows, head), F32)
        value_term = jnp.zeros((count * token_rows, head), F32)
        for index in range(heads):
            cols = slice(index * head, (index + 1) * head)
            weights = keep[index]
            prob_grad = nt(upstream[:, cols], values)
            score_grad = (
                weights.astype(F32) * (prob_grad - stats[:, index : index + 1])
            ).astype(BF16)
            grads[index] = grads[index] + nn(score_grad, keys)
            key_term = key_term + tn(score_grad, q_scaled[:, cols])
            value_term = value_term + tn(weights, up_scaled[:, cols])
        term[:, :head] = key_term.astype(BF16)
        term[:, head:] = value_term.astype(BF16)
    for index in range(heads):
        cols = slice(index * head, (index + 1) * head)
        if last:
            grad = grads[index] * stats[:, heads + index : heads + index + 1]
            own[:, cols] = grad[:half]
            other[:, cols] = grad[half:]
        else:
            grad_out[:, cols] = grads[index]


def backward(upstream, up_scaled, q_scaled, stats, grad, blocks, kept, first, last):
    rows, width = upstream.shape
    head = blocks[0].shape[2]
    keys = kept[0].shape[2]
    out = [shape((rows // 2, width), F32)] * 2 if last else [shape((rows, width), F32)]
    out = out + [shape((keys, 2 * head), BF16) for _ in blocks]
    args = [upstream, up_scaled, q_scaled, stats] + ([] if first else [grad]) + blocks + kept

    def body(*refs):
        backward_body(len(blocks), first, last, *refs)

    return call(body, out, args, micros=0.8 * len(blocks), name="backward")


def back(upstream, hat, inverse, weight):
    scaled = weight * upstream
    return inverse * (scaled - hat * jnp.mean(scaled * hat, axis=-1, keepdims=True))


def query_back_body(mine, theirs, raw, inverses, q_gain, out):
    head = q_gain.shape[1]
    for index in range(mine.shape[1] // head):
        cols = slice(index * head, (index + 1) * head)
        inv = inverses[:, index : index + 1]
        out[:, cols] = back(
            mine[:, cols] + theirs[:, cols], raw[:, cols] * inv, inv, q_gain[...]
        ).astype(BF16)


def join_body(*refs):
    rows = refs[-1].shape[0]
    for half in range(2):
        own, up, down = refs[3 * half : 3 * half + 3]
        total = (own[...].astype(F32) + up[...].astype(F32) + down[...].astype(F32)).astype(BF16)
        for index in range(2):
            refs[6 + 2 * half + index][...] = total[index * rows : (index + 1) * rows]


def key_back_body(a, b, c, d, raw, inverses, k_gain, out):
    head = k_gain.shape[1]
    heads = raw.shape[1] // head - 2
    total = a[...].astype(F32) + b[...].astype(F32) + c[...].astype(F32) + d[...].astype(F32)
    inv = inverses[:, heads : heads + 1]
    hat = raw[:, heads * head : (heads + 1) * head] * inv
    out[:, :head] = back(total[:, :head], hat, inv, k_gain[...]).astype(BF16)
    out[:, head:] = total[:, head:].astype(BF16)


def feature_body(place, grad_q, grad_kv, raw, w_q, w_k, w_v, *outs):
    count = len(outs)
    rows, width = grad_q.shape
    head = w_k.shape[1]
    features = w_q.shape[0] // count
    dot = jnp.sum(grad_q[...].astype(F32) * raw[:, :width], axis=-1, keepdims=True)
    dot = dot + jnp.sum(grad_kv[...].astype(F32) * raw[:, width:], axis=-1, keepdims=True)
    high = dot.astype(BF16).astype(F32)
    tail = lanes_of([high, dot - high], rows).astype(BF16)
    for index, out in enumerate(outs):
        start = pl.multiple_of(lax.rem(place[0] + index, count) * features, 128)
        part = nt(grad_q[...], w_q[pl.ds(start, features), :])
        part = part + nt(grad_kv[:, :head], w_k[pl.ds(start, features), :])
        part = part + nt(grad_kv[:, head:], w_v[pl.ds(start, features), :])
        out[:, :features] = part.astype(BF16)
        out[:, features:] = tail


def input_back_body(a, b, c, d, hidden, inverses, gain, out):
    features = hidden.shape[1]
    total = a[...].astype(F32) + b[...].astype(F32) + c[...].astype(F32) + d[...].astype(F32)
    dot = total[:, features : features + 1] + total[:, features + 1 : features + 2]
    mean = dot / (features * 4)
    inverse = inverses[:, 5:6]
    hat = hidden[...].astype(F32) * inverse
    out[...] = (inverse * (gain[...] * total[:, :features] - hat * mean)).astype(BF16)


def weight_body(*refs):
    turned = jnp.concatenate([ref[...] for ref in refs[:COLUMN]], axis=1)
    grads = jnp.concatenate([ref[...] for ref in refs[COLUMN:-1]], axis=0)
    refs[-1][...] = nn(turned, grads).astype(BF16)


def weight_terms(turned, grads):
    out = shape((turned[0].shape[0], grads[0].shape[1]), BF16)
    return call(weight_body, out, turned + grads, name="weight_terms")


def across_z(terms):
    rows, columns = terms.shape
    rings = [[y * RING + z for z in range(RING)] for y in range(COLUMN)]
    terms = lax.all_to_all(terms, "seq", 0, 0, axis_index_groups=rings, tiled=True)
    return terms.reshape(RING, rows // RING, columns)


def along_z(value, step):
    pairs = [
        (y * RING + z, y * RING + (z + step) % RING) for y in range(COLUMN) for z in range(RING)
    ]
    return lax.ppermute(value, "seq", pairs)


def along_y(value, step):
    pairs = [
        (y * RING + z, (y + step) % COLUMN * RING + z) for y in range(COLUMN) for z in range(RING)
    ]
    return lax.ppermute(value, "seq", pairs)


def along_x(value, step):
    return lax.ppermute(value, "mp", [(x, (x + step) % 4) for x in range(4)])


def swapped(value):
    return lax.ppermute(value, "group", [(0, 1), (1, 0)])


def plus(*parts):
    total = parts[0].astype(F32)
    for part in parts[1:]:
        total = total + part.astype(F32)
    return total.astype(BF16)


def on_device(hidden, norm_gain, w_q, w_k, w_v, q_gain, k_gain, positions, reach, grad_out):
    place_x = lax.axis_index("mp").astype(jnp.int32)
    place = lax.axis_index("seq").astype(jnp.int32)
    place_y = place // RING
    rows, features = hidden.shape[1:]
    width = features * 4
    head = q_gain.shape[1]
    columns = w_q.shape[2]
    gain = norm_gain[0].reshape(1, width)
    local_gain = lax.dynamic_slice(gain, (0, place_x * features), (1, features))
    full = lax.all_gather(hidden[0], "mp", axis=1, tiled=True)
    full, other_up, other_reach = lax.optimization_barrier(
        (full, swapped(grad_out[0]), swapped(reach))
    )
    upstream = jnp.concatenate([grad_out[0], other_up], axis=0)
    all_reach = jnp.concatenate([reach[0], other_reach[0]]).astype(F32).reshape(2 * rows, 1)
    normed, block, queries, raw, inverses = call(
        project_body,
        [
            shape((rows, width), BF16),
            shape((2 * rows + TAIL, head), BF16),
            shape((rows, columns), BF16),
            shape((rows, columns + 2 * head), F32),
            shape((rows, 128), F32),
        ],
        [full, gain]
        + [pltpu.with_memory_space_constraint(w[0], pltpu.HBM) for w in (w_q, w_k, w_v)]
        + [q_gain, k_gain, positions],
        far=(2, 3, 4),
        scratch=[
            pltpu.VMEM((width, columns), BF16),
            pltpu.VMEM((width, head), BF16),
            pltpu.VMEM((width, head), BF16),
            pltpu.SemaphoreType.DMA((3,)),
        ],
        micros=4.0,
        name="project",
    )
    near = [block] + [along_y(block, step) for step in range(1, COLUMN)]
    pairs = [jnp.stack(near[:2]), jnp.stack(near[2:])]
    all_queries = jnp.concatenate([queries, swapped(queries)], axis=0)
    blocks = {(half, 0): pairs[half] for half in range(2)}
    for half in range(2):
        up = down = pairs[half]
        for step in range(1, 5):
            up = along_z(up, 1)
            blocks[half, -step] = up
            if step < 4:
                down = along_z(down, -1)
                blocks[half, step] = down
    kept = {}
    sums = None
    order = [((0, 0), (1, 0))]
    order += [((half, -step), (half, step)) for step in range(1, 4) for half in range(2)]
    order += [((0, -4), (1, -4))]
    for number, group in enumerate(order):
        if number == 1:
            sums, normed = lax.optimization_barrier((sums, normed))
            turned = call(
                turn_body,
                [shape((features, rows), BF16)] * COLUMN,
                [place_y.reshape(1), normed],
                smem=1,
                name="turn",
            )
            turned = [turned[0]] + [along_y(turned[step], step) for step in range(1, COLUMN)]
        if number == 5:
            sums, turned = lax.optimization_barrier((sums, turned))
        outs = forward(
            all_queries,
            all_reach,
            sums,
            [blocks[k] for k in group],
            number == 0,
            number == len(order) - 1,
        )
        sums = outs[0]
        for k, keep in zip(group, outs[1:]):
            kept[k] = keep
    attended, q_scaled, up_scaled, stats = call(
        finish_body,
        [
            shape((rows, columns), BF16),
            shape((2 * rows, columns), BF16),
            shape((2 * rows, columns), BF16),
            shape((2 * rows, 128), F32),
        ],
        [sums, swapped(sums), all_queries, upstream],
        name="finish",
    )
    terms = {}
    grad = None
    order = [
        (half, pair) for pair in ((-4, -3), (3, -2), (2, -1), (1, 0)) for half in range(2)
    ]
    ups, downs = [None, None], [None, None]
    for number, (half, pair) in enumerate(order):
        stage = number // 2
        last = number == len(order) - 1
        if stage > 1:
            grad, ups[half], downs[half] = lax.optimization_barrier(
                (grad, ups[half], downs[half])
            )
            ups[half] = along_z(plus(ups[half], terms[half, 5 - stage]), 1)
            downs[half] = along_z(plus(downs[half], terms[half, 4 + stage]), -1)
        outs = backward(
            upstream,
            up_scaled,
            q_scaled,
            stats,
            grad,
            [blocks[half, k] for k in pair],
            [kept[half, k] for k in pair],
            number == 0,
            last,
        )
        if last:
            grad_own, grad_other = outs[:2]
            outs = outs[2:]
        else:
            grad, outs = outs[0], outs[1:]
        for k, term in zip(pair, outs):
            terms[half, k % RING] = term
        if stage == 0:
            ups[half], downs[half] = along_z(terms[half, 4], 1), along_z(terms[half, 5], -1)
    grad_q = call(
        query_back_body,
        shape((rows, columns), BF16),
        [grad_own, swapped(grad_other), raw, inverses, q_gain],
        name="query_back",
    )
    query_grads = [grad_q] + [along_y(grad_q, step) for step in range(1, COLUMN)]
    query_terms = weight_terms(turned, query_grads)
    own_terms = []
    for half in range(2):
        up = along_z(plus(ups[half], terms[half, 1]), 1)
        own_terms += [terms[half, 0], up, downs[half]]
    own_terms = call(
        join_body, [shape((rows, 2 * head), BF16)] * COLUMN, own_terms, name="join"
    )
    own_terms = [own_terms[0]] + [along_y(own_terms[step], -step) for step in range(1, COLUMN)]
    own_terms, query_terms = lax.optimization_barrier((own_terms, query_terms))
    query_terms = across_z(query_terms)
    grad_kv = call(
        key_back_body,
        shape((rows, 2 * head), BF16),
        own_terms + [raw, inverses, k_gain],
        name="key_back",
    )
    key_grads = [along_y(grad_kv, step) for step in range(1, COLUMN)]
    feature_parts = call(
        feature_body,
        [shape((rows, features + 128), BF16)] * 4,
        [place_x.reshape(1), grad_q, grad_kv, raw, w_q[0], w_k[0], w_v[0]],
        smem=1,
        micros=5.0,
        name="feature",
    )
    near_part, key_grads, query_terms = lax.optimization_barrier(
        (feature_parts[0], key_grads, query_terms)
    )
    grad_wq = plus(*[query_terms[k] for k in range(RING)])
    key_terms = across_z(weight_terms(turned, [grad_kv] + key_grads))
    grad_wkv = plus(*[key_terms[k] for k in range(RING)])
    feature_parts = [near_part] + [along_x(feature_parts[k], k) for k in range(1, 4)]
    input_grad = call(
        input_back_body,
        shape((rows, features), BF16),
        feature_parts + [hidden[0], inverses, local_gain],
        micros=8.0,
        name="input_back",
    )
    return (
        attended[None],
        input_grad[None],
        grad_wq[None],
        grad_wkv[None, :, :head],
        grad_wkv[None, :, head:],
    )


def solution(mesh):
    return jax.shard_map(
        on_device,
        mesh=mesh,
        in_specs=(
            P("group", "seq", "mp"),
            P("group", None),
            P("group", None, "mp"),
            P("group", None, "mp"),
            P("group", None, "mp"),
            P("group", None),
            P("group", None),
            P("group", "seq"),
            P("group", "seq"),
            P("group", "seq", "mp"),
        ),
        out_specs=(P("group", "seq", "mp"),) * 5,
        check_vma=False,
    )
```

```python
import jax
import jax.numpy as jnp
from jax import lax
from jax.experimental import pallas as pl
from jax.experimental.pallas import tpu as pltpu
from jax.sharding import PartitionSpec as P

EPSILON = 1e-06
LOG2E = 1.4426950408889634
F32 = jnp.float32
BF16 = jnp.bfloat16
RING = 8
COLUMN = 4
TAIL = 16
VMEM = pl.BlockSpec(memory_space=pltpu.VMEM)
SMEM = pl.BlockSpec(memory_space=pltpu.SMEM)
FAR = pl.BlockSpec(memory_space=pltpu.HBM)


def nn(left, right):
    return lax.dot_general(left, right, (((1,), (0,)), ((), ())), preferred_element_type=F32)


def nt(left, right):
    return lax.dot_general(left, right, (((1,), (1,)), ((), ())), preferred_element_type=F32)


def tn(left, right):
    return lax.dot_general(left, right, (((0,), (0,)), ((), ())), preferred_element_type=F32)


def shape(dims, dtype):
    return jax.ShapeDtypeStruct(dims, dtype)


def call(body, out_shape, args, smem=0, far=(), scratch=(), micros=2.0, name=None):
    outs = out_shape if isinstance(out_shape, (list, tuple)) else [out_shape]
    return pl.pallas_call(
        body,
        out_shape=out_shape,
        in_specs=[
            SMEM if index < smem else FAR if index in far else VMEM for index in range(len(args))
        ],
        out_specs=[VMEM] * len(outs) if isinstance(out_shape, (list, tuple)) else VMEM,
        scratch_shapes=list(scratch),
        compiler_params=pltpu.CompilerParams(vmem_limit_bytes=20 * 1024 * 1024),
        cost_estimate=pl.CostEstimate(
            flops=int(micros * 1.15e9),
            bytes_accessed=0,
            transcendentals=0,
        ),
        name=name,
    )(*args)


def lanes_of(columns, rows, width=128):
    lane = lax.broadcasted_iota(jnp.int32, (rows, width), 1)
    packed = jnp.zeros((rows, width), F32)
    for index, column in enumerate(columns):
        packed = jnp.where(lane == index, column, packed)
    return packed


def project_body(full, *refs):
    far, near, refs = refs[:8], refs[-9:-1], list(refs[8:-9]) + [refs[-1]]
    normed, blocks, queries, raw, inverses, sems = refs
    gain, pos, reach, k_gain, q_gain, w_k, w_v, w_q = near
    copies = [
        pltpu.make_async_copy(source, target, sems.at[index])
        for index, (source, target) in enumerate(zip(far, near))
    ]
    for copy in copies:
        copy.start()
    values = full[...].astype(F32)
    rows, width = values.shape
    head = q_gain.shape[1]
    per_key = w_q.shape[1] // head
    inverse = lax.rsqrt(jnp.sum(values * values, axis=-1, keepdims=True) / width + EPSILON)
    for copy in copies[:5]:
        copy.wait()
    normed[...] = (values * inverse * gain[...]).astype(BF16)
    for copy in copies[5:]:
        copy.wait()
    k_raw = nn(normed[...], w_k[...])
    raw[:, per_key * head : (per_key + 1) * head] = k_raw
    k_inv = lax.rsqrt(jnp.mean(k_raw * k_raw, axis=-1, keepdims=True) + EPSILON)
    key_rows = (k_raw * k_inv * k_gain[...]).astype(BF16)
    v_raw = nn(normed[...], w_v[...])
    raw[:, (per_key + 1) * head :] = v_raw
    high = lax.shift_right_logical(pos[...], 6)
    row = lax.broadcasted_iota(jnp.int32, (TAIL, rows), 0)
    digits = jnp.where(row == 0, high, jnp.where(row == 1, pos[...] - high * 64, 0))
    for index in range(RING):
        blocks[index, :rows, :] = key_rows
        blocks[index, rows : 2 * rows, :] = v_raw.astype(BF16)
        blocks[index, 2 * rows :, :] = digits.astype(F32).astype(BF16)
    columns = []
    q_raw = nn(normed[...], w_q[...])
    raw[:, : per_key * head] = q_raw
    for index in range(per_key):
        part = q_raw[:, index * head : (index + 1) * head]
        inv = lax.rsqrt(jnp.mean(part * part, axis=-1, keepdims=True) + EPSILON)
        columns.append(inv)
        queries[:, index * head : (index + 1) * head] = (part * inv * q_gain[...]).astype(BF16)
    high = lax.shift_right_logical(reach[...], 6)
    row = lax.broadcasted_iota(jnp.int32, (rows, rows), 0)
    digits = jnp.where(row == 0, high, jnp.where(row == 1, reach[...] - high * 64, 0))
    queries[:, per_key * head :] = digits.astype(F32).T.astype(BF16)
    inverses[...] = lanes_of(columns + [k_inv, inverse], rows)


def turn_body(place, normed, *outs):
    count = len(outs)
    width = normed.shape[1] // count
    for index, out in enumerate(outs):
        start = pl.multiple_of(lax.rem(place[0] + index, count) * width, 128)
        out[...] = normed[:, pl.ds(start, width)].T


def stacked(refs, cols):
    return jnp.concatenate([ref[:, cols] for ref in refs], axis=0)


def key_tiles(blocks):
    token_rows = (blocks.shape[1] - TAIL) // 2
    for first in range(0, blocks.shape[0], 2):
        pair = range(first, first + 2)
        keys = jnp.concatenate([blocks[r, :token_rows, :] for r in pair], axis=0)
        values = jnp.concatenate([blocks[r, token_rows : 2 * token_rows, :] for r in pair], axis=0)
        places = []
        for r in pair:
            digits = blocks[r, 2 * token_rows :, :].astype(F32)
            places.append(digits[0:1] * 64.0 + digits[1:2])
        yield slice(first * token_rows, (first + 2) * token_rows), keys, values, jnp.concatenate(
            places, axis=1
        )


def forward_body(first, blocks, *refs):
    queries, refs = refs[:COLUMN], list(refs[COLUMN:])
    head = blocks.shape[2]
    width = queries[0].shape[1] - head
    rows = queries[0].shape[0] * COLUMN
    if first:
        sum_out, kept = refs
    else:
        ups, (sum_in, sum_out, stats, kept) = refs[:COLUMN], refs[COLUMN:]
    heads = width // head
    scale = head ** (-0.5) * LOG2E
    reach = stacked(queries, slice(width, width + head)).astype(F32)
    reach = reach[:, 0:1] * 64.0 + reach[:, 1:2]
    totals, dots = [], []
    for index in range(heads):
        cols = slice(index * head, (index + 1) * head)
        total_cols = slice(width + index * head, width + (index + 1) * head)
        query = stacked(queries, cols)
        summed = jnp.zeros((rows, head), F32) if first else sum_in[:, cols]
        total = jnp.zeros((rows, head), F32) if first else sum_in[:, total_cols]
        for span, keys, values, places in key_tiles(blocks):
            weights = jnp.where(places <= reach, jnp.exp2(nt(query, keys) * scale), 0.0)
            for r in range(weights.shape[1] // head):
                total = total + weights[:, r * head : (r + 1) * head]
            rounded = weights.astype(BF16)
            kept[index, :, span] = rounded
            summed = summed + nn(rounded, values)
        sum_out[:, cols] = summed
        if first:
            sum_out[:, total_cols] = total
        else:
            totals.append(jnp.sum(total, axis=-1, keepdims=True))
            up = stacked(ups, cols).astype(F32)
            dots.append(jnp.sum(up * summed, axis=-1, keepdims=True))
    if not first:
        stats[...] = lanes_of(dots + totals, rows).T[: 2 * heads]


def forward(blocks, queries, ups, sums):
    rows = queries[0].shape[0] * COLUMN
    head = blocks.shape[2]
    width = queries[0].shape[1] - head
    heads = width // head
    kept = shape((heads, rows, blocks.shape[0] * (blocks.shape[1] - TAIL) // 2), BF16)
    first = sums is None
    if first:
        out = [shape((rows, 2 * width), F32), kept]
        args = [blocks] + queries
    else:
        out = [shape((rows, width), F32), shape((2 * heads, rows), F32), kept]
        args = [blocks] + queries + ups + [sums]

    def body(*refs):
        forward_body(first, *refs)

    return call(body, out, args, micros=4.0, name="forward")


def finish_body(summed, *refs):
    stats, refs = refs[:COLUMN], refs[COLUMN:]
    queries, ups, refs = refs[:COLUMN], refs[COLUMN : 2 * COLUMN], refs[2 * COLUMN :]
    q_scaled, up_scaled, terms, outs = refs[0], refs[1], refs[2], refs[3:]
    rows, width = summed.shape
    part = rows // COLUMN
    heads = stats[0].shape[0] // 2
    head = width // heads
    scale = head ** (-0.5)
    joined = stats[0][...]
    for step in range(1, COLUMN):
        other = stats[step][...]
        cut = rows - step * part
        joined = joined + jnp.concatenate([other[:, cut:], other[:, :cut]], axis=1)
    fill = jnp.zeros((128 - 2 * heads, rows), F32)
    joined = jnp.concatenate([joined, fill], axis=0).T
    deltas, scales = [], []
    for index in range(heads):
        cols = slice(index * head, (index + 1) * head)
        inverse = 1.0 / joined[:, heads + index : heads + index + 1]
        deltas.append(joined[:, index : index + 1] * inverse)
        scales.append(inverse * scale)
        output = (summed[:, cols] * inverse).astype(BF16)
        for step, out in enumerate(outs):
            out[:, cols] = output[step * part : (step + 1) * part]
        up_scaled[:, cols] = (stacked(ups, cols).astype(F32) * inverse).astype(BF16)
        q_scaled[:, cols] = (stacked(queries, cols).astype(F32) * (inverse * scale)).astype(BF16)
    terms[...] = lanes_of(deltas + scales, rows)


def backward_body(last, blocks, kept, up_scaled, q_scaled, stats, *refs):
    ups, refs = refs[:COLUMN], list(refs[COLUMN:])
    grad_in = refs.pop(0) if last else None
    term, grad_out = refs[0], refs[1:]
    rows, width = q_scaled.shape
    part = rows // COLUMN
    head = blocks.shape[2]
    heads = width // head
    grads = [
        grad_in[:, h * head : (h + 1) * head] if last else jnp.zeros((rows, head), F32)
        for h in range(heads)
    ]
    for span, keys, values, _ in key_tiles(blocks):
        key_term = jnp.zeros((keys.shape[0], head), F32)
        value_term = jnp.zeros((keys.shape[0], head), F32)
        for index in range(heads):
            cols = slice(index * head, (index + 1) * head)
            weights = kept[index, :, span]
            prob_grad = nt(stacked(ups, cols), values)
            score_grad = (
                weights.astype(F32) * (prob_grad - stats[:, index : index + 1])
            ).astype(BF16)
            grads[index] = grads[index] + nn(score_grad, keys)
            key_term = key_term + tn(score_grad, q_scaled[:, cols])
            value_term = value_term + tn(weights, up_scaled[:, cols])
        term[span, :head] = key_term.astype(BF16)
        term[span, head:] = value_term.astype(BF16)
    for index in range(heads):
        cols = slice(index * head, (index + 1) * head)
        if last:
            grad = grads[index] * stats[:, heads + index : heads + index + 1]
            for step, out in enumerate(grad_out):
                out[:, cols] = grad[step * part : (step + 1) * part].astype(out.dtype)
        else:
            grad_out[0][:, cols] = grads[index]


def backward(blocks, kept, up_scaled, q_scaled, stats, ups, grad):
    rows, width = q_scaled.shape
    out = [shape((kept.shape[2], 2 * blocks.shape[2]), BF16)]
    last = grad is not None
    if last:
        out += [shape((rows // COLUMN, width), F32 if step == 0 else BF16) for step in range(COLUMN)]
    else:
        out += [shape((rows, width), F32)]
    args = [blocks, kept, up_scaled, q_scaled, stats] + ups + ([grad] if last else [])

    def body(*refs):
        backward_body(last, *refs)

    return call(body, out, args, micros=6.5, name="backward")


def back(upstream, hat, inverse, weight):
    scaled = weight * upstream
    return inverse * (scaled - hat * jnp.mean(scaled * hat, axis=-1, keepdims=True))


def query_back_body(a, b, c, d, raw, inverses, q_gain, out):
    head = q_gain.shape[1]
    for index in range(a.shape[1] // head):
        cols = slice(index * head, (index + 1) * head)
        inv = inverses[:, index : index + 1]
        total = a[:, cols] + b[:, cols].astype(F32)
        total = total + c[:, cols].astype(F32) + d[:, cols].astype(F32)
        out[:, cols] = back(total, raw[:, cols] * inv, inv, q_gain[...]).astype(BF16)


def key_back_body(terms, raw, inverses, k_gain, out):
    head = k_gain.shape[1]
    heads = raw.shape[1] // head - 2
    total = terms[0].astype(F32)
    for index in range(1, RING):
        total = total + terms[index].astype(F32)
    inv = inverses[:, heads : heads + 1]
    hat = raw[:, heads * head : (heads + 1) * head] * inv
    out[:, :head] = back(total[:, :head], hat, inv, k_gain[...]).astype(BF16)
    out[:, head:] = total[:, head:].astype(BF16)


def feature_body(place, grad_q, grad_kv, raw, w_q, w_k, w_v, *outs):
    count = len(outs)
    rows, width = grad_q.shape
    head = w_k.shape[1]
    features = w_q.shape[0] // count
    dot = jnp.sum(grad_q[...].astype(F32) * raw[:, :width], axis=-1, keepdims=True)
    dot = dot + jnp.sum(grad_kv[...].astype(F32) * raw[:, width:], axis=-1, keepdims=True)
    high = dot.astype(BF16).astype(F32)
    tail = lanes_of([high, dot - high], rows).astype(BF16)
    for index, out in enumerate(outs):
        start = pl.multiple_of(lax.rem(place[0] + index, count) * features, 128)
        part = nt(grad_q[...], w_q[pl.ds(start, features), :])
        part = part + nt(grad_kv[:, :head], w_k[pl.ds(start, features), :])
        part = part + nt(grad_kv[:, head:], w_v[pl.ds(start, features), :])
        out[:, :features] = part.astype(BF16)
        out[:, features:] = tail


def input_back_body(a, b, c, d, hidden, inverses, gain, out):
    features = hidden.shape[1]
    total = a[...].astype(F32) + b[...].astype(F32) + c[...].astype(F32) + d[...].astype(F32)
    dot = total[:, features : features + 1] + total[:, features + 1 : features + 2]
    mean = dot / (features * 4)
    inverse = inverses[:, 5:6]
    hat = hidden[...].astype(F32) * inverse
    out[...] = (inverse * (gain[...] * total[:, :features] - hat * mean)).astype(BF16)


def weight_body(*refs):
    turned = jnp.concatenate([ref[...] for ref in refs[:COLUMN]], axis=1)
    grads = jnp.concatenate([ref[...] for ref in refs[COLUMN:-1]], axis=0)
    refs[-1][...] = nn(turned, grads).astype(BF16)


def weight_terms(turned, grads):
    out = shape((turned[0].shape[0], grads[0].shape[1]), BF16)
    return call(weight_body, out, turned + grads, name="weight_terms")


def across_z(terms):
    rows, columns = terms.shape
    rings = [[y * RING + z for z in range(RING)] for y in range(COLUMN)]
    terms = lax.all_to_all(terms, "seq", 0, 0, axis_index_groups=rings, tiled=True)
    return terms.reshape(RING, rows // RING, columns)


def along_z(value, step):
    pairs = [
        (y * RING + z, y * RING + (z + step) % RING) for y in range(COLUMN) for z in range(RING)
    ]
    return lax.ppermute(value, "seq", pairs)


def along_y(value, step):
    pairs = [
        (y * RING + z, (y + step) % COLUMN * RING + z) for y in range(COLUMN) for z in range(RING)
    ]
    return lax.ppermute(value, "seq", pairs)


def along_x(value, step):
    return lax.ppermute(value, "mp", [(x, (x + step) % 4) for x in range(4)])


def swapped(value):
    return lax.ppermute(value, "group", [(0, 1), (1, 0)])


def plus(*parts):
    total = parts[0].astype(F32)
    for part in parts[1:]:
        total = total + part.astype(F32)
    return total.astype(BF16)


def on_device(hidden, norm_gain, w_q, w_k, w_v, q_gain, k_gain, positions, reach, grad_out):
    place_x = lax.axis_index("mp").astype(jnp.int32)
    place = lax.axis_index("seq").astype(jnp.int32)
    place_y = place // RING
    rows, features = hidden.shape[1:]
    width = features * 4
    head = q_gain.shape[1]
    columns = w_q.shape[2]
    gain = norm_gain[0].reshape(1, width)
    local_gain = lax.dynamic_slice(gain, (0, place_x * features), (1, features))
    full = lax.all_gather(hidden[0], "mp", axis=1, tiled=True)
    sources = [gain, positions, reach, k_gain, q_gain, w_k[0], w_v[0], w_q[0]]
    normed, blocks, queries, raw, inverses = call(
        project_body,
        [
            shape((rows, width), BF16),
            shape((RING, 2 * rows + TAIL, head), BF16),
            shape((rows, columns + head), BF16),
            shape((rows, columns + 2 * head), F32),
            shape((rows, 128), F32),
        ],
        [full] + [pltpu.with_memory_space_constraint(value, pltpu.HBM) for value in sources],
        far=range(1, 9),
        scratch=[pltpu.VMEM(value.shape, value.dtype) for value in sources]
        + [pltpu.SemaphoreType.DMA((8,))],
        micros=4.0,
        name="project",
    )
    own_blocks = across_z(blocks.reshape(-1, head)).reshape(blocks.shape)
    queries = [queries] + [along_y(queries, step) for step in range(1, COLUMN)]
    ups = [grad_out[0]] + [along_y(grad_out[0], step) for step in range(1, COLUMN)]
    other_blocks = swapped(own_blocks)
    ups, normed = lax.optimization_barrier((ups, normed))
    turned = call(
        turn_body,
        [shape((features, rows), BF16)] * COLUMN,
        [place_y.reshape(1), normed],
        smem=1,
        name="turn",
    )
    turned = [turned[0]] + [along_y(turned[step], step) for step in range(1, COLUMN)]
    sums, own_kept = forward(own_blocks, queries, ups, None)
    sums, turned = lax.optimization_barrier((sums, turned))
    summed, stats, other_kept = forward(other_blocks, queries, ups, sums)
    finished = call(
        finish_body,
        [
            shape((COLUMN * rows, columns), BF16),
            shape((COLUMN * rows, columns), BF16),
            shape((COLUMN * rows, 128), F32),
        ]
        + [shape((rows, columns), BF16)] * COLUMN,
        [summed, stats] + [along_y(stats, step) for step in range(1, COLUMN)] + queries + ups,
        name="finish",
    )
    q_scaled, up_scaled, stats = finished[:3]
    outputs = finished[3:]
    other_terms, grad = backward(
        other_blocks, other_kept, up_scaled, q_scaled, stats, ups, None
    )
    outputs = [outputs[0]] + [along_y(outputs[step], -step) for step in range(1, COLUMN)]
    grad, outputs = lax.optimization_barrier((grad, outputs))
    attended = plus(*outputs)
    outs = backward(own_blocks, own_kept, up_scaled, q_scaled, stats, ups, grad)
    own_terms, query_grad = outs[0], list(outs[1:])
    own_terms = across_z(plus(own_terms, swapped(other_terms)))
    query_grad = [query_grad[0]] + [along_y(query_grad[step], -step) for step in range(1, COLUMN)]
    grad_q = call(
        query_back_body,
        shape((rows, columns), BF16),
        query_grad + [raw, inverses, q_gain],
        name="query_back",
    )
    query_grads = [grad_q] + [along_y(grad_q, step) for step in range(1, COLUMN)]
    query_terms = weight_terms(turned, query_grads)
    own_terms, query_terms = lax.optimization_barrier((own_terms, query_terms))
    query_terms = across_z(query_terms)
    grad_kv = call(
        key_back_body,
        shape((rows, 2 * head), BF16),
        [own_terms, raw, inverses, k_gain],
        name="key_back",
    )
    key_grads = [along_y(grad_kv, step) for step in range(1, COLUMN)]
    feature_parts = call(
        feature_body,
        [shape((rows, features + 128), BF16)] * 4,
        [place_x.reshape(1), grad_q, grad_kv, raw, w_q[0], w_k[0], w_v[0]],
        smem=1,
        micros=5.0,
        name="feature",
    )
    near_part, key_grads, query_terms = lax.optimization_barrier(
        (feature_parts[0], key_grads, query_terms)
    )
    grad_wq = plus(*[query_terms[k] for k in range(RING)])
    key_terms = across_z(weight_terms(turned, [grad_kv] + key_grads))
    grad_wkv = plus(*[key_terms[k] for k in range(RING)])
    feature_parts = [near_part] + [along_x(feature_parts[k], k) for k in range(1, 4)]
    input_grad = call(
        input_back_body,
        shape((rows, features), BF16),
        feature_parts + [hidden[0], inverses, local_gain],
        micros=8.0,
        name="input_back",
    )
    return (
        attended[None],
        input_grad[None],
        grad_wq[None],
        grad_wkv[None, :, :head],
        grad_wkv[None, :, head:],
    )


def solution(mesh):
    return jax.shard_map(
        on_device,
        mesh=mesh,
        in_specs=(
            P("group", "seq", "mp"),
            P("group", None),
            P("group", None, "mp"),
            P("group", None, "mp"),
            P("group", None, "mp"),
            P("group", None),
            P("group", None),
            P("group", "seq"),
            P("group", "seq"),
            P("group", "seq", "mp"),
        ),
        out_specs=(P("group", "seq", "mp"),) * 5,
        check_vma=False,
    )
```

```python
import jax
import jax.numpy as jnp
from jax import lax
from jax.experimental import pallas as pl
from jax.experimental.pallas import tpu as pltpu
from jax.sharding import PartitionSpec as P

EPSILON = 1e-06
LOG2E = 1.4426950408889634
F32 = jnp.float32
BF16 = jnp.bfloat16
RING = 8
COLUMN = 4
TAIL = 16
VMEM = pl.BlockSpec(memory_space=pltpu.VMEM)
SMEM = pl.BlockSpec(memory_space=pltpu.SMEM)
FAR = pl.BlockSpec(memory_space=pltpu.HBM)


def nn(left, right):
    return lax.dot_general(left, right, (((1,), (0,)), ((), ())), preferred_element_type=F32)


def nt(left, right):
    return lax.dot_general(left, right, (((1,), (1,)), ((), ())), preferred_element_type=F32)


def tn(left, right):
    return lax.dot_general(left, right, (((0,), (0,)), ((), ())), preferred_element_type=F32)


def shape(dims, dtype):
    return jax.ShapeDtypeStruct(dims, dtype)


def call(body, out_shape, args, smem=0, far=(), scratch=(), micros=2.0, name=None):
    outs = out_shape if isinstance(out_shape, (list, tuple)) else [out_shape]
    return pl.pallas_call(
        body,
        out_shape=out_shape,
        in_specs=[
            SMEM if index < smem else FAR if index in far else VMEM for index in range(len(args))
        ],
        out_specs=[VMEM] * len(outs) if isinstance(out_shape, (list, tuple)) else VMEM,
        scratch_shapes=list(scratch),
        compiler_params=pltpu.CompilerParams(vmem_limit_bytes=16 * 1024 * 1024),
        cost_estimate=pl.CostEstimate(
            flops=int(micros * 1.15e9),
            bytes_accessed=0,
            transcendentals=0,
        ),
        name=name,
    )(*args)


def lanes_of(columns, rows, width=128):
    lane = lax.broadcasted_iota(jnp.int32, (rows, width), 1)
    packed = jnp.zeros((rows, width), F32)
    for index, column in enumerate(columns):
        packed = jnp.where(lane == index, column, packed)
    return packed


def project_body(full, *refs):
    far, near, refs = refs[:8], refs[-9:-1], list(refs[8:-9]) + [refs[-1]]
    normed, blocks, queries, raw, inverses, sems = refs
    gain, pos, reach, k_gain, q_gain, w_k, w_v, w_q = near
    copies = [
        pltpu.make_async_copy(source, target, sems.at[index])
        for index, (source, target) in enumerate(zip(far, near))
    ]
    for copy in copies:
        copy.start()
    values = full[...].astype(F32)
    rows, width = values.shape
    head = q_gain.shape[1]
    per_key = w_q.shape[1] // head
    inverse = lax.rsqrt(jnp.sum(values * values, axis=-1, keepdims=True) / width + EPSILON)
    for copy in copies[:5]:
        copy.wait()
    normed[...] = (values * inverse * gain[...]).astype(BF16)
    for copy in copies[5:]:
        copy.wait()
    k_raw = nn(normed[...], w_k[...])
    raw[:, per_key * head : (per_key + 1) * head] = k_raw
    k_inv = lax.rsqrt(jnp.mean(k_raw * k_raw, axis=-1, keepdims=True) + EPSILON)
    key_rows = (k_raw * k_inv * k_gain[...]).astype(BF16)
    v_raw = nn(normed[...], w_v[...])
    raw[:, (per_key + 1) * head :] = v_raw
    high = lax.shift_right_logical(pos[...], 6)
    row = lax.broadcasted_iota(jnp.int32, (TAIL, rows), 0)
    digits = jnp.where(row == 0, high, jnp.where(row == 1, pos[...] - high * 64, 0))
    for index in range(RING):
        blocks[index, :rows, :] = key_rows
        blocks[index, rows : 2 * rows, :] = v_raw.astype(BF16)
        blocks[index, 2 * rows :, :] = digits.astype(F32).astype(BF16)
    columns = []
    q_raw = nn(normed[...], w_q[...])
    raw[:, : per_key * head] = q_raw
    for index in range(per_key):
        part = q_raw[:, index * head : (index + 1) * head]
        inv = lax.rsqrt(jnp.mean(part * part, axis=-1, keepdims=True) + EPSILON)
        columns.append(inv)
        queries[:, index * head : (index + 1) * head] = (part * inv * q_gain[...]).astype(BF16)
    high = lax.shift_right_logical(reach[...], 6)
    row = lax.broadcasted_iota(jnp.int32, (rows, rows), 0)
    digits = jnp.where(row == 0, high, jnp.where(row == 1, reach[...] - high * 64, 0))
    queries[:, per_key * head :] = digits.astype(F32).T.astype(BF16)
    inverses[...] = lanes_of(columns + [k_inv, inverse], rows)


def turn_body(place, normed, *outs):
    count = len(outs)
    width = normed.shape[1] // count
    for index, out in enumerate(outs):
        start = pl.multiple_of(lax.rem(place[0] + index, count) * width, 128)
        out[...] = normed[:, pl.ds(start, width)].T


def stacked(refs, cols):
    return jnp.concatenate([ref[:, cols] for ref in refs], axis=0)


def key_tiles(blocks):
    token_rows = (blocks.shape[1] - TAIL) // 2
    for first in range(0, blocks.shape[0], 2):
        pair = range(first, first + 2)
        keys = jnp.concatenate([blocks[r, :token_rows, :] for r in pair], axis=0)
        values = jnp.concatenate([blocks[r, token_rows : 2 * token_rows, :] for r in pair], axis=0)
        places = []
        for r in pair:
            digits = blocks[r, 2 * token_rows :, :].astype(F32)
            places.append(digits[0:1] * 64.0 + digits[1:2])
        yield slice(first * token_rows, (first + 2) * token_rows), keys, values, jnp.concatenate(
            places, axis=1
        )


def forward_body(first, blocks, *refs):
    queries, refs = refs[:COLUMN], list(refs[COLUMN:])
    head = blocks.shape[2]
    width = queries[0].shape[1] - head
    rows = queries[0].shape[0] * COLUMN
    if first:
        sum_out, kept = refs
    else:
        ups, (sum_in, sum_out, stats, kept) = refs[:COLUMN], refs[COLUMN:]
    heads = width // head
    scale = head ** (-0.5) * LOG2E
    reach = stacked(queries, slice(width, width + head)).astype(F32)
    reach = reach[:, 0:1] * 64.0 + reach[:, 1:2]
    totals, dots = [], []
    for index in range(heads):
        cols = slice(index * head, (index + 1) * head)
        total_cols = slice(width + index * head, width + (index + 1) * head)
        query = stacked(queries, cols)
        summed = jnp.zeros((rows, head), F32) if first else sum_in[:, cols]
        total = jnp.zeros((rows, head), F32) if first else sum_in[:, total_cols]
        for span, keys, values, places in key_tiles(blocks):
            weights = jnp.where(places <= reach, jnp.exp2(nt(query, keys) * scale), 0.0)
            for r in range(weights.shape[1] // head):
                total = total + weights[:, r * head : (r + 1) * head]
            rounded = weights.astype(BF16)
            kept[index, :, span] = rounded
            summed = summed + nn(rounded, values)
        sum_out[:, cols] = summed
        if first:
            sum_out[:, total_cols] = total
        else:
            totals.append(jnp.sum(total, axis=-1, keepdims=True))
            up = stacked(ups, cols).astype(F32)
            dots.append(jnp.sum(up * summed, axis=-1, keepdims=True))
    if not first:
        stats[...] = lanes_of(dots + totals, rows).T[: 2 * heads]


def forward(blocks, queries, ups, sums):
    rows = queries[0].shape[0] * COLUMN
    head = blocks.shape[2]
    width = queries[0].shape[1] - head
    heads = width // head
    kept = shape((heads, rows, blocks.shape[0] * (blocks.shape[1] - TAIL) // 2), BF16)
    first = sums is None
    if first:
        out = [shape((rows, 2 * width), F32), kept]
        args = [blocks] + queries
    else:
        out = [shape((rows, width), F32), shape((2 * heads, rows), F32), kept]
        args = [blocks] + queries + ups + [sums]

    def body(*refs):
        forward_body(first, *refs)

    return call(body, out, args, micros=4.0, name="forward")


def finish_body(summed, *refs):
    stats, refs = refs[:COLUMN], refs[COLUMN:]
    queries, ups, refs = refs[:COLUMN], refs[COLUMN : 2 * COLUMN], refs[2 * COLUMN :]
    q_scaled, up_scaled, terms, outs = refs[0], refs[1], refs[2], refs[3:]
    rows, width = summed.shape
    part = rows // COLUMN
    heads = stats[0].shape[0] // 2
    head = width // heads
    scale = head ** (-0.5)
    joined = stats[0][...]
    for step in range(1, COLUMN):
        other = stats[step][...]
        cut = rows - step * part
        joined = joined + jnp.concatenate([other[:, cut:], other[:, :cut]], axis=1)
    fill = jnp.zeros((128 - 2 * heads, rows), F32)
    joined = jnp.concatenate([joined, fill], axis=0).T
    deltas, scales = [], []
    for index in range(heads):
        cols = slice(index * head, (index + 1) * head)
        inverse = 1.0 / joined[:, heads + index : heads + index + 1]
        deltas.append(joined[:, index : index + 1] * inverse)
        scales.append(inverse * scale)
        output = (summed[:, cols] * inverse).astype(BF16)
        for step, out in enumerate(outs):
            out[:, cols] = output[step * part : (step + 1) * part]
        up_scaled[:, cols] = (stacked(ups, cols).astype(F32) * inverse).astype(BF16)
        q_scaled[:, cols] = (stacked(queries, cols).astype(F32) * (inverse * scale)).astype(BF16)
    terms[...] = lanes_of(deltas + scales, rows)


def backward_body(last, blocks, kept, up_scaled, q_scaled, stats, *refs):
    ups, refs = refs[:COLUMN], list(refs[COLUMN:])
    grad_in = refs.pop(0) if last else None
    term, grad_out = refs[0], refs[1:]
    rows, width = q_scaled.shape
    part = rows // COLUMN
    head = blocks.shape[2]
    heads = width // head
    grads = [
        grad_in[:, h * head : (h + 1) * head] if last else jnp.zeros((rows, head), F32)
        for h in range(heads)
    ]
    for span, keys, values, _ in key_tiles(blocks):
        key_term = jnp.zeros((keys.shape[0], head), F32)
        value_term = jnp.zeros((keys.shape[0], head), F32)
        for index in range(heads):
            cols = slice(index * head, (index + 1) * head)
            weights = kept[index, :, span]
            prob_grad = nt(stacked(ups, cols), values)
            score_grad = (
                weights.astype(F32) * (prob_grad - stats[:, index : index + 1])
            ).astype(BF16)
            grads[index] = grads[index] + nn(score_grad, keys)
            key_term = key_term + tn(score_grad, q_scaled[:, cols])
            value_term = value_term + tn(weights, up_scaled[:, cols])
        term[span, :head] = key_term.astype(BF16)
        term[span, head:] = value_term.astype(BF16)
    for index in range(heads):
        cols = slice(index * head, (index + 1) * head)
        if last:
            grad = grads[index] * stats[:, heads + index : heads + index + 1]
            for step, out in enumerate(grad_out):
                out[:, cols] = grad[step * part : (step + 1) * part].astype(out.dtype)
        else:
            grad_out[0][:, cols] = grads[index]


def backward(blocks, kept, up_scaled, q_scaled, stats, ups, grad):
    rows, width = q_scaled.shape
    out = [shape((kept.shape[2], 2 * blocks.shape[2]), BF16)]
    last = grad is not None
    if last:
        out += [shape((rows // COLUMN, width), F32 if step == 0 else BF16) for step in range(COLUMN)]
    else:
        out += [shape((rows, width), F32)]
    args = [blocks, kept, up_scaled, q_scaled, stats] + ups + ([grad] if last else [])

    def body(*refs):
        backward_body(last, *refs)

    return call(body, out, args, micros=6.5, name="backward")


def back(upstream, hat, inverse, weight):
    scaled = weight * upstream
    return inverse * (scaled - hat * jnp.mean(scaled * hat, axis=-1, keepdims=True))


def grads_body(a, b, c, d, terms, raw, inverses, q_gain, k_gain, out):
    head = q_gain.shape[1]
    width = a.shape[1]
    heads = width // head
    for index in range(heads):
        cols = slice(index * head, (index + 1) * head)
        inv = inverses[:, index : index + 1]
        total = a[:, cols] + b[:, cols].astype(F32)
        total = total + c[:, cols].astype(F32) + d[:, cols].astype(F32)
        out[:, cols] = back(total, raw[:, cols] * inv, inv, q_gain[...]).astype(BF16)
    total = terms[0].astype(F32)
    for index in range(1, RING):
        total = total + terms[index].astype(F32)
    inv = inverses[:, heads : heads + 1]
    hat = raw[:, width : width + head] * inv
    out[:, width : width + head] = back(total[:, :head], hat, inv, k_gain[...]).astype(BF16)
    out[:, width + head :] = total[:, head:].astype(BF16)


def feature_body(place, grads, raw, w_q, w_k, w_v, *outs):
    count = len(outs)
    rows = grads.shape[0]
    head, width = w_k.shape[1], w_q.shape[1]
    features = w_q.shape[0] // count
    dot = jnp.sum(grads[...].astype(F32) * raw[...], axis=-1, keepdims=True)
    high = dot.astype(BF16).astype(F32)
    tail = lanes_of([high, dot - high], rows).astype(BF16)
    for index, out in enumerate(outs):
        start = pl.multiple_of(lax.rem(place[0] + index, count) * features, 128)
        part = nt(grads[:, :width], w_q[pl.ds(start, features), :])
        part = part + nt(grads[:, width : width + head], w_k[pl.ds(start, features), :])
        part = part + nt(grads[:, width + head :], w_v[pl.ds(start, features), :])
        out[:, :features] = part.astype(BF16)
        out[:, features:] = tail


def input_back_body(a, b, c, d, hidden, inverses, gain, out):
    features = hidden.shape[1]
    total = a[...].astype(F32) + b[...].astype(F32) + c[...].astype(F32) + d[...].astype(F32)
    dot = total[:, features : features + 1] + total[:, features + 1 : features + 2]
    mean = dot / (features * 4)
    inverse = inverses[:, 5:6]
    hat = hidden[...].astype(F32) * inverse
    out[...] = (inverse * (gain[...] * total[:, :features] - hat * mean)).astype(BF16)


def weight_body(*refs):
    turned = jnp.concatenate([ref[...] for ref in refs[:COLUMN]], axis=1)
    grads = jnp.concatenate([ref[...] for ref in refs[COLUMN:-1]], axis=0)
    refs[-1][...] = nn(turned, grads).astype(BF16)


def weight_terms(turned, grads):
    out = shape((turned[0].shape[0], grads[0].shape[1]), BF16)
    return call(weight_body, out, turned + grads, name="weight_terms")


def collect_body(terms, *outs):
    total = terms[0].astype(F32)
    for index in range(1, RING):
        total = total + terms[index].astype(F32)
    start = 0
    for out in outs:
        out[...] = total[:, start : start + out.shape[1]].astype(BF16)
        start += out.shape[1]


def across_z(terms):
    rows, columns = terms.shape
    rings = [[y * RING + z for z in range(RING)] for y in range(COLUMN)]
    terms = lax.all_to_all(terms, "seq", 0, 0, axis_index_groups=rings, tiled=True)
    return terms.reshape(RING, rows // RING, columns)


def along_z(value, step):
    pairs = [
        (y * RING + z, y * RING + (z + step) % RING) for y in range(COLUMN) for z in range(RING)
    ]
    return lax.ppermute(value, "seq", pairs)


def along_y(value, step):
    pairs = [
        (y * RING + z, (y + step) % COLUMN * RING + z) for y in range(COLUMN) for z in range(RING)
    ]
    return lax.ppermute(value, "seq", pairs)


def along_x(value, step):
    return lax.ppermute(value, "mp", [(x, (x + step) % 4) for x in range(4)])


def swapped(value):
    return lax.ppermute(value, "group", [(0, 1), (1, 0)])


def plus(*parts):
    total = parts[0].astype(F32)
    for part in parts[1:]:
        total = total + part.astype(F32)
    return total.astype(BF16)


def on_device(hidden, norm_gain, w_q, w_k, w_v, q_gain, k_gain, positions, reach, grad_out):
    place_x = lax.axis_index("mp").astype(jnp.int32)
    place = lax.axis_index("seq").astype(jnp.int32)
    place_y = place // RING
    rows, features = hidden.shape[1:]
    width = features * 4
    head = q_gain.shape[1]
    columns = w_q.shape[2]
    gain = norm_gain[0].reshape(1, width)
    local_gain = lax.dynamic_slice(gain, (0, place_x * features), (1, features))
    full = lax.all_gather(hidden[0], "mp", axis=1, tiled=True)
    sources = [gain, positions, reach, k_gain, q_gain, w_k[0], w_v[0], w_q[0]]
    normed, blocks, queries, raw, inverses = call(
        project_body,
        [
            shape((rows, width), BF16),
            shape((RING, 2 * rows + TAIL, head), BF16),
            shape((rows, columns + head), BF16),
            shape((rows, columns + 2 * head), F32),
            shape((rows, 128), F32),
        ],
        [full] + [pltpu.with_memory_space_constraint(value, pltpu.HBM) for value in sources],
        far=range(1, 9),
        scratch=[pltpu.VMEM(value.shape, value.dtype) for value in sources]
        + [pltpu.SemaphoreType.DMA((8,))],
        micros=4.0,
        name="project",
    )
    own_blocks = across_z(blocks.reshape(-1, head)).reshape(blocks.shape)
    queries = [queries] + [along_y(queries, step) for step in range(1, COLUMN)]
    ups = [grad_out[0]] + [along_y(grad_out[0], step) for step in range(1, COLUMN)]
    other_blocks = swapped(own_blocks)
    sums, own_kept = forward(own_blocks, queries, ups, None)
    summed, stats, other_kept = forward(other_blocks, queries, ups, sums)
    finished = call(
        finish_body,
        [
            shape((COLUMN * rows, columns), BF16),
            shape((COLUMN * rows, columns), BF16),
            shape((COLUMN * rows, 128), F32),
        ]
        + [shape((rows, columns), BF16)] * COLUMN,
        [summed, stats] + [along_y(stats, step) for step in range(1, COLUMN)] + queries + ups,
        name="finish",
    )
    q_scaled, up_scaled, stats = finished[:3]
    outputs = finished[3:]
    other_terms, grad = backward(
        other_blocks, other_kept, up_scaled, q_scaled, stats, ups, None
    )
    outs = backward(own_blocks, own_kept, up_scaled, q_scaled, stats, ups, grad)
    own_terms, query_grad = outs[0], list(outs[1:])
    query_grad[0], normed = lax.optimization_barrier((query_grad[0], normed))
    turned = call(
        turn_body,
        [shape((features, rows), BF16)] * COLUMN,
        [place_y.reshape(1), normed],
        smem=1,
        name="turn",
    )
    turned = [turned[0]] + [along_y(turned[step], step) for step in range(1, COLUMN)]
    own_terms = across_z(plus(own_terms, swapped(other_terms)))
    query_grad = [query_grad[0]] + [along_y(query_grad[step], -step) for step in range(1, COLUMN)]
    query_grad, own_terms, turned = lax.optimization_barrier((query_grad, own_terms, turned))
    grads = call(
        grads_body,
        shape((rows, columns + 2 * head), BF16),
        query_grad + [own_terms, raw, inverses, q_gain, k_gain],
        name="grads",
    )
    all_grads = [grads] + [along_y(grads, step) for step in range(1, COLUMN)]
    feature_parts = call(
        feature_body,
        [shape((rows, features + 128), BF16)] * 4,
        [place_x.reshape(1), grads, raw, w_q[0], w_k[0], w_v[0]],
        smem=1,
        micros=5.0,
        name="feature",
    )
    first_part, all_grads = lax.optimization_barrier((feature_parts[0], all_grads))
    terms = weight_terms(turned, all_grads)
    terms, sent, outputs = lax.optimization_barrier((terms, list(feature_parts[1:]), outputs))
    terms = across_z(terms)
    feature_parts = [first_part] + [along_x(sent[k - 1], k) for k in range(1, 4)]
    attended = plus(outputs[0], *[along_y(outputs[step], -step) for step in range(1, COLUMN)])
    input_grad = call(
        input_back_body,
        shape((rows, features), BF16),
        feature_parts + [hidden[0], inverses, local_gain],
        micros=8.0,
        name="input_back",
    )
    weight_rows = terms.shape[1]
    grad_wq, grad_wk, grad_wv = call(
        collect_body,
        [shape((weight_rows, size), BF16) for size in (columns, head, head)],
        [terms],
        name="collect",
    )
    return (attended[None], input_grad[None], grad_wq[None], grad_wk[None], grad_wv[None])


def solution(mesh):
    return jax.shard_map(
        on_device,
        mesh=mesh,
        in_specs=(
            P("group", "seq", "mp"),
            P("group", None),
            P("group", None, "mp"),
            P("group", None, "mp"),
            P("group", None, "mp"),
            P("group", None),
            P("group", None),
            P("group", "seq"),
            P("group", "seq"),
            P("group", "seq", "mp"),
        ),
        out_specs=(P("group", "seq", "mp"),) * 5,
        check_vma=False,
    )
```

```python
import jax
import jax.numpy as jnp
from jax import lax
from jax.experimental import pallas as pl
from jax.experimental.pallas import tpu as pltpu
from jax.sharding import PartitionSpec as P

EPSILON = 1e-06
LOG2E = 1.4426950408889634
F32 = jnp.float32
BF16 = jnp.bfloat16
RING = 8
COLUMN = 4
TAIL = 16
VMEM = pl.BlockSpec(memory_space=pltpu.VMEM)
SMEM = pl.BlockSpec(memory_space=pltpu.SMEM)
FAR = pl.BlockSpec(memory_space=pltpu.HBM)


def nn(left, right):
    return lax.dot_general(left, right, (((1,), (0,)), ((), ())), preferred_element_type=F32)


def nt(left, right):
    return lax.dot_general(left, right, (((1,), (1,)), ((), ())), preferred_element_type=F32)


def tn(left, right):
    return lax.dot_general(left, right, (((0,), (0,)), ((), ())), preferred_element_type=F32)


def shape(dims, dtype):
    return jax.ShapeDtypeStruct(dims, dtype)


def call(body, out_shape, args, smem=0, far=(), scratch=(), micros=2.0, name=None):
    outs = out_shape if isinstance(out_shape, (list, tuple)) else [out_shape]
    return pl.pallas_call(
        body,
        out_shape=out_shape,
        in_specs=[
            SMEM if index < smem else FAR if index in far else VMEM for index in range(len(args))
        ],
        out_specs=[VMEM] * len(outs) if isinstance(out_shape, (list, tuple)) else VMEM,
        scratch_shapes=list(scratch),
        compiler_params=pltpu.CompilerParams(vmem_limit_bytes=16 * 1024 * 1024),
        cost_estimate=pl.CostEstimate(
            flops=int(micros * 1.15e9),
            bytes_accessed=0,
            transcendentals=0,
        ),
        name=name,
    )(*args)


def lanes_of(columns, rows, width=128):
    lane = lax.broadcasted_iota(jnp.int32, (rows, width), 1)
    packed = jnp.zeros((rows, width), F32)
    for index, column in enumerate(columns):
        packed = jnp.where(lane == index, column, packed)
    return packed


def project_body(full, *refs):
    far, near, refs = refs[:8], refs[-9:-1], list(refs[8:-9]) + [refs[-1]]
    normed, blocks, queries, raw, inverses, sems = refs
    gain, pos, reach, k_gain, q_gain, w_k, w_v, w_q = near
    copies = [
        pltpu.make_async_copy(source, target, sems.at[index])
        for index, (source, target) in enumerate(zip(far, near))
    ]
    for copy in copies:
        copy.start()
    values = full[...].astype(F32)
    rows, width = values.shape
    head = q_gain.shape[1]
    per_key = w_q.shape[1] // head
    inverse = lax.rsqrt(jnp.sum(values * values, axis=-1, keepdims=True) / width + EPSILON)
    for copy in copies[:5]:
        copy.wait()
    normed[...] = (values * inverse * gain[...]).astype(BF16)
    for copy in copies[5:]:
        copy.wait()
    k_raw = nn(normed[...], w_k[...])
    raw[:, per_key * head : (per_key + 1) * head] = k_raw
    k_inv = lax.rsqrt(jnp.mean(k_raw * k_raw, axis=-1, keepdims=True) + EPSILON)
    key_rows = (k_raw * k_inv * k_gain[...]).astype(BF16)
    v_raw = nn(normed[...], w_v[...])
    raw[:, (per_key + 1) * head :] = v_raw
    high = lax.shift_right_logical(pos[...], 6)
    row = lax.broadcasted_iota(jnp.int32, (TAIL, rows), 0)
    digits = jnp.where(row == 0, high, jnp.where(row == 1, pos[...] - high * 64, 0))
    for index in range(RING):
        blocks[index, :rows, :] = key_rows
        blocks[index, rows : 2 * rows, :] = v_raw.astype(BF16)
        blocks[index, 2 * rows :, :] = digits.astype(F32).astype(BF16)
    columns = []
    q_raw = nn(normed[...], w_q[...])
    raw[:, : per_key * head] = q_raw
    for index in range(per_key):
        part = q_raw[:, index * head : (index + 1) * head]
        inv = lax.rsqrt(jnp.mean(part * part, axis=-1, keepdims=True) + EPSILON)
        columns.append(inv)
        queries[:, index * head : (index + 1) * head] = (part * inv * q_gain[...]).astype(BF16)
    high = lax.shift_right_logical(reach[...], 6)
    row = lax.broadcasted_iota(jnp.int32, (rows, rows), 0)
    digits = jnp.where(row == 0, high, jnp.where(row == 1, reach[...] - high * 64, 0))
    queries[:, per_key * head :] = digits.astype(F32).T.astype(BF16)
    inverses[...] = lanes_of(columns + [k_inv, inverse], rows)


def turn_body(place, normed, *outs):
    count = len(outs)
    width = normed.shape[1] // count
    for index, out in enumerate(outs):
        start = pl.multiple_of(lax.rem(place[0] + index, count) * width, 128)
        out[...] = normed[:, pl.ds(start, width)].T


def stacked(refs, cols):
    return jnp.concatenate([ref[:, cols] for ref in refs], axis=0)


def key_tiles(blocks):
    token_rows = (blocks.shape[1] - TAIL) // 2
    for first in range(0, blocks.shape[0], 2):
        pair = range(first, first + 2)
        keys = jnp.concatenate([blocks[r, :token_rows, :] for r in pair], axis=0)
        values = jnp.concatenate([blocks[r, token_rows : 2 * token_rows, :] for r in pair], axis=0)
        places = []
        for r in pair:
            digits = blocks[r, 2 * token_rows :, :].astype(F32)
            places.append(digits[0:1] * 64.0 + digits[1:2])
        yield slice(first * token_rows, (first + 2) * token_rows), keys, values, jnp.concatenate(
            places, axis=1
        )


def forward_body(first, blocks, *refs):
    queries, refs = refs[:COLUMN], list(refs[COLUMN:])
    head = blocks.shape[2]
    width = queries[0].shape[1] - head
    rows = queries[0].shape[0] * COLUMN
    if first:
        sum_out, kept = refs
    else:
        ups, (sum_in, sum_out, stats, kept) = refs[:COLUMN], refs[COLUMN:]
    heads = width // head
    scale = head ** (-0.5) * LOG2E
    reach = stacked(queries, slice(width, width + head)).astype(F32)
    reach = reach[:, 0:1] * 64.0 + reach[:, 1:2]
    totals, dots = [], []
    for index in range(heads):
        cols = slice(index * head, (index + 1) * head)
        total_cols = slice(width + index * head, width + (index + 1) * head)
        query = stacked(queries, cols)
        summed = jnp.zeros((rows, head), F32) if first else sum_in[:, cols]
        total = jnp.zeros((rows, head), F32) if first else sum_in[:, total_cols]
        for span, keys, values, places in key_tiles(blocks):
            weights = jnp.where(places <= reach, jnp.exp2(nt(query, keys) * scale), 0.0)
            for r in range(weights.shape[1] // head):
                total = total + weights[:, r * head : (r + 1) * head]
            rounded = weights.astype(BF16)
            kept[index, :, span] = rounded
            summed = summed + nn(rounded, values)
        sum_out[:, cols] = summed
        if first:
            sum_out[:, total_cols] = total
        else:
            totals.append(jnp.sum(total, axis=-1, keepdims=True))
            up = stacked(ups, cols).astype(F32)
            dots.append(jnp.sum(up * summed, axis=-1, keepdims=True))
    if not first:
        stats[...] = lanes_of(dots + totals, rows).T[: 2 * heads]


def forward(blocks, queries, ups, sums):
    rows = queries[0].shape[0] * COLUMN
    head = blocks.shape[2]
    width = queries[0].shape[1] - head
    heads = width // head
    kept = shape((heads, rows, blocks.shape[0] * (blocks.shape[1] - TAIL) // 2), BF16)
    first = sums is None
    if first:
        out = [shape((rows, 2 * width), F32), kept]
        args = [blocks] + queries
    else:
        out = [shape((rows, width), F32), shape((2 * heads, rows), F32), kept]
        args = [blocks] + queries + ups + [sums]

    def body(*refs):
        forward_body(first, *refs)

    return call(body, out, args, micros=4.0, name="forward")


def finish_body(summed, *refs):
    stats, refs = refs[:COLUMN], refs[COLUMN:]
    queries, ups, refs = refs[:COLUMN], refs[COLUMN : 2 * COLUMN], refs[2 * COLUMN :]
    q_scaled, up_scaled, terms, outs = refs[0], refs[1], refs[2], refs[3:]
    rows, width = summed.shape
    part = rows // COLUMN
    heads = stats[0].shape[0] // 2
    head = width // heads
    scale = head ** (-0.5)
    joined = stats[0][...]
    for step in range(1, COLUMN):
        other = stats[step][...]
        cut = rows - step * part
        joined = joined + jnp.concatenate([other[:, cut:], other[:, :cut]], axis=1)
    fill = jnp.zeros((128 - 2 * heads, rows), F32)
    joined = jnp.concatenate([joined, fill], axis=0).T
    deltas, scales = [], []
    for index in range(heads):
        cols = slice(index * head, (index + 1) * head)
        inverse = 1.0 / joined[:, heads + index : heads + index + 1]
        deltas.append(joined[:, index : index + 1] * inverse)
        scales.append(inverse * scale)
        output = (summed[:, cols] * inverse).astype(BF16)
        for step, out in enumerate(outs):
            out[:, cols] = output[step * part : (step + 1) * part]
        up_scaled[:, cols] = (stacked(ups, cols).astype(F32) * inverse).astype(BF16)
        q_scaled[:, cols] = (stacked(queries, cols).astype(F32) * (inverse * scale)).astype(BF16)
    terms[...] = lanes_of(deltas + scales, rows)


def backward_body(last, blocks, kept, up_scaled, q_scaled, stats, *refs):
    ups, refs = refs[:COLUMN], list(refs[COLUMN:])
    grad_in = refs.pop(0) if last else None
    term, grad_out = refs[0], refs[1:]
    rows, width = q_scaled.shape
    part = rows // COLUMN
    head = blocks.shape[2]
    heads = width // head
    grads = [
        grad_in[:, h * head : (h + 1) * head] if last else jnp.zeros((rows, head), F32)
        for h in range(heads)
    ]
    for span, keys, values, _ in key_tiles(blocks):
        key_term = jnp.zeros((keys.shape[0], head), F32)
        value_term = jnp.zeros((keys.shape[0], head), F32)
        for index in range(heads):
            cols = slice(index * head, (index + 1) * head)
            weights = kept[index, :, span]
            prob_grad = nt(stacked(ups, cols), values)
            score_grad = (
                weights.astype(F32) * (prob_grad - stats[:, index : index + 1])
            ).astype(BF16)
            grads[index] = grads[index] + nn(score_grad, keys)
            key_term = key_term + tn(score_grad, q_scaled[:, cols])
            value_term = value_term + tn(weights, up_scaled[:, cols])
        term[span, :head] = key_term.astype(BF16)
        term[span, head:] = value_term.astype(BF16)
    for index in range(heads):
        cols = slice(index * head, (index + 1) * head)
        if last:
            grad = grads[index] * stats[:, heads + index : heads + index + 1]
            for step, out in enumerate(grad_out):
                out[:, cols] = grad[step * part : (step + 1) * part].astype(out.dtype)
        else:
            grad_out[0][:, cols] = grads[index]


def backward(blocks, kept, up_scaled, q_scaled, stats, ups, grad):
    rows, width = q_scaled.shape
    out = [shape((kept.shape[2], 2 * blocks.shape[2]), BF16)]
    last = grad is not None
    if last:
        out += [shape((rows // COLUMN, width), F32 if step == 0 else BF16) for step in range(COLUMN)]
    else:
        out += [shape((rows, width), F32)]
    args = [blocks, kept, up_scaled, q_scaled, stats] + ups + ([grad] if last else [])

    def body(*refs):
        backward_body(last, *refs)

    return call(body, out, args, micros=6.5, name="backward")


def back(upstream, hat, inverse, weight):
    scaled = weight * upstream
    return inverse * (scaled - hat * jnp.mean(scaled * hat, axis=-1, keepdims=True))


def grads_body(a, b, c, d, terms, raw, inverses, q_gain, k_gain, out):
    head = q_gain.shape[1]
    width = a.shape[1]
    heads = width // head
    for index in range(heads):
        cols = slice(index * head, (index + 1) * head)
        inv = inverses[:, index : index + 1]
        total = a[:, cols] + b[:, cols].astype(F32)
        total = total + c[:, cols].astype(F32) + d[:, cols].astype(F32)
        out[:, cols] = back(total, raw[:, cols] * inv, inv, q_gain[...]).astype(BF16)
    total = terms[0].astype(F32)
    for index in range(1, RING):
        total = total + terms[index].astype(F32)
    inv = inverses[:, heads : heads + 1]
    hat = raw[:, width : width + head] * inv
    out[:, width : width + head] = back(total[:, :head], hat, inv, k_gain[...]).astype(BF16)
    out[:, width + head :] = total[:, head:].astype(BF16)


def feature_body(place, grads, raw, w_q, w_k, w_v, *outs):
    count = len(outs)
    rows = grads.shape[0]
    head, width = w_k.shape[1], w_q.shape[1]
    features = w_q.shape[0] // count
    dot = jnp.sum(grads[...].astype(F32) * raw[...], axis=-1, keepdims=True)
    high = dot.astype(BF16).astype(F32)
    tail = lanes_of([high, dot - high], rows).astype(BF16)
    for index, out in enumerate(outs):
        start = pl.multiple_of(lax.rem(place[0] + index, count) * features, 128)
        part = nt(grads[:, :width], w_q[pl.ds(start, features), :])
        part = part + nt(grads[:, width : width + head], w_k[pl.ds(start, features), :])
        part = part + nt(grads[:, width + head :], w_v[pl.ds(start, features), :])
        out[:, :features] = part.astype(BF16)
        out[:, features:] = tail


def input_back_body(a, b, c, d, hidden, inverses, gain, out):
    features = hidden.shape[1]
    total = a[...].astype(F32) + b[...].astype(F32) + c[...].astype(F32) + d[...].astype(F32)
    dot = total[:, features : features + 1] + total[:, features + 1 : features + 2]
    mean = dot / (features * 4)
    inverse = inverses[:, 5:6]
    hat = hidden[...].astype(F32) * inverse
    out[...] = (inverse * (gain[...] * total[:, :features] - hat * mean)).astype(BF16)


def weight_body(*refs):
    turned = jnp.concatenate([ref[...] for ref in refs[:COLUMN]], axis=1)
    grads = jnp.concatenate([ref[...] for ref in refs[COLUMN:-1]], axis=0)
    refs[-1][...] = nn(turned, grads).astype(BF16)


def weight_terms(turned, grads):
    out = shape((turned[0].shape[0], grads[0].shape[1]), BF16)
    return call(weight_body, out, turned + grads, name="weight_terms")


def collect_body(terms, *outs):
    total = terms[0].astype(F32)
    for index in range(1, RING):
        total = total + terms[index].astype(F32)
    start = 0
    for out in outs:
        out[...] = total[:, start : start + out.shape[1]].astype(BF16)
        start += out.shape[1]


def across_z(terms):
    rows, columns = terms.shape
    rings = [[y * RING + z for z in range(RING)] for y in range(COLUMN)]
    terms = lax.all_to_all(terms, "seq", 0, 0, axis_index_groups=rings, tiled=True)
    return terms.reshape(RING, rows // RING, columns)


def along_z(value, step):
    pairs = [
        (y * RING + z, y * RING + (z + step) % RING) for y in range(COLUMN) for z in range(RING)
    ]
    return lax.ppermute(value, "seq", pairs)


def along_y(value, step):
    pairs = [
        (y * RING + z, (y + step) % COLUMN * RING + z) for y in range(COLUMN) for z in range(RING)
    ]
    return lax.ppermute(value, "seq", pairs)


def along_x(value, step):
    return lax.ppermute(value, "mp", [(x, (x + step) % 4) for x in range(4)])


def swapped(value):
    return lax.ppermute(value, "group", [(0, 1), (1, 0)])


def plus(*parts):
    total = parts[0].astype(F32)
    for part in parts[1:]:
        total = total + part.astype(F32)
    return total.astype(BF16)


def on_device(hidden, norm_gain, w_q, w_k, w_v, q_gain, k_gain, positions, reach, grad_out):
    place_x = lax.axis_index("mp").astype(jnp.int32)
    place = lax.axis_index("seq").astype(jnp.int32)
    place_y = place // RING
    rows, features = hidden.shape[1:]
    width = features * 4
    head = q_gain.shape[1]
    columns = w_q.shape[2]
    gain = norm_gain[0].reshape(1, width)
    local_gain = lax.dynamic_slice(gain, (0, place_x * features), (1, features))
    full = lax.all_gather(hidden[0], "mp", axis=1, tiled=True)
    sources = [gain, positions, reach, k_gain, q_gain, w_k[0], w_v[0], w_q[0]]
    normed, blocks, queries, raw, inverses = call(
        project_body,
        [
            shape((rows, width), BF16),
            shape((RING, 2 * rows + TAIL, head), BF16),
            shape((rows, columns + head), BF16),
            shape((rows, columns + 2 * head), F32),
            shape((rows, 128), F32),
        ],
        [full] + [pltpu.with_memory_space_constraint(value, pltpu.HBM) for value in sources],
        far=range(1, 9),
        scratch=[pltpu.VMEM(value.shape, value.dtype) for value in sources]
        + [pltpu.SemaphoreType.DMA((8,))],
        micros=4.0,
        name="project",
    )
    own_blocks = across_z(blocks.reshape(-1, head)).reshape(blocks.shape)
    queries = [queries] + [along_y(queries, step) for step in range(1, COLUMN)]
    ups = [grad_out[0]] + [along_y(grad_out[0], step) for step in range(1, COLUMN)]
    turned = call(
        turn_body,
        [shape((features, rows), BF16)] * COLUMN,
        [place_y.reshape(1), normed],
        smem=1,
        name="turn",
    )
    own_blocks, ups, turned = lax.optimization_barrier((own_blocks, ups, turned))
    other_blocks = swapped(own_blocks)
    sums, own_kept = forward(own_blocks, queries, ups, None)
    summed, stats, other_kept = forward(other_blocks, queries, ups, sums)
    finished = call(
        finish_body,
        [
            shape((COLUMN * rows, columns), BF16),
            shape((COLUMN * rows, columns), BF16),
            shape((COLUMN * rows, 128), F32),
        ]
        + [shape((rows, columns), BF16)] * COLUMN,
        [summed, stats] + [along_y(stats, step) for step in range(1, COLUMN)] + queries + ups,
        name="finish",
    )
    q_scaled, up_scaled, stats = finished[:3]
    outputs = finished[3:]
    stats, turned = lax.optimization_barrier((stats, turned))
    turned = [turned[0]] + [along_y(turned[step], step) for step in range(1, COLUMN)]
    other_terms, grad = backward(
        other_blocks, other_kept, up_scaled, q_scaled, stats, ups, None
    )
    grad, turned = lax.optimization_barrier((grad, turned))
    outs = backward(own_blocks, own_kept, up_scaled, q_scaled, stats, ups, grad)
    own_terms, query_grad = outs[0], list(outs[1:])
    own_terms = across_z(plus(own_terms, swapped(other_terms)))
    query_grad = [query_grad[0]] + [along_y(query_grad[step], -step) for step in range(1, COLUMN)]
    grads = call(
        grads_body,
        shape((rows, columns + 2 * head), BF16),
        query_grad + [own_terms, raw, inverses, q_gain, k_gain],
        name="grads",
    )
    all_grads = [grads] + [along_y(grads, step) for step in range(1, COLUMN)]
    feature_parts = call(
        feature_body,
        [shape((rows, features + 128), BF16)] * 4,
        [place_x.reshape(1), grads, raw, w_q[0], w_k[0], w_v[0]],
        smem=1,
        micros=5.0,
        name="feature",
    )
    first_part, all_grads = lax.optimization_barrier((feature_parts[0], all_grads))
    terms = weight_terms(turned, all_grads)
    terms, sent, outputs = lax.optimization_barrier((terms, list(feature_parts[1:]), outputs))
    terms = across_z(terms)
    feature_parts = [first_part] + [along_x(sent[k - 1], k) for k in range(1, 4)]
    attended = plus(outputs[0], *[along_y(outputs[step], -step) for step in range(1, COLUMN)])
    input_grad = call(
        input_back_body,
        shape((rows, features), BF16),
        feature_parts + [hidden[0], inverses, local_gain],
        micros=8.0,
        name="input_back",
    )
    weight_rows = terms.shape[1]
    grad_wq, grad_wk, grad_wv = call(
        collect_body,
        [shape((weight_rows, size), BF16) for size in (columns, head, head)],
        [terms],
        name="collect",
    )
    return (attended[None], input_grad[None], grad_wq[None], grad_wk[None], grad_wv[None])


def solution(mesh):
    return jax.shard_map(
        on_device,
        mesh=mesh,
        in_specs=(
            P("group", "seq", "mp"),
            P("group", None),
            P("group", None, "mp"),
            P("group", None, "mp"),
            P("group", None, "mp"),
            P("group", None),
            P("group", None),
            P("group", "seq"),
            P("group", "seq"),
            P("group", "seq", "mp"),
        ),
        out_specs=(P("group", "seq", "mp"),) * 5,
        check_vma=False,
    )
```

```python
import jax
import jax.numpy as jnp
from jax import lax
from jax.experimental import pallas as pl
from jax.experimental.pallas import tpu as pltpu
from jax.sharding import PartitionSpec as P

EPSILON = 1e-06
LOG2E = 1.4426950408889634
F32 = jnp.float32
BF16 = jnp.bfloat16
RING = 8
COLUMN = 4
TAIL = 16
VMEM = pl.BlockSpec(memory_space=pltpu.VMEM)
SMEM = pl.BlockSpec(memory_space=pltpu.SMEM)
FAR = pl.BlockSpec(memory_space=pltpu.HBM)


def nn(left, right):
    return lax.dot_general(left, right, (((1,), (0,)), ((), ())), preferred_element_type=F32)


def nt(left, right):
    return lax.dot_general(left, right, (((1,), (1,)), ((), ())), preferred_element_type=F32)


def tn(left, right):
    return lax.dot_general(left, right, (((0,), (0,)), ((), ())), preferred_element_type=F32)


def shape(dims, dtype):
    return jax.ShapeDtypeStruct(dims, dtype)


def call(body, out_shape, args, smem=0, far=(), scratch=(), micros=2.0, name=None):
    outs = out_shape if isinstance(out_shape, (list, tuple)) else [out_shape]
    return pl.pallas_call(
        body,
        out_shape=out_shape,
        in_specs=[
            SMEM if index < smem else FAR if index in far else VMEM for index in range(len(args))
        ],
        out_specs=[VMEM] * len(outs) if isinstance(out_shape, (list, tuple)) else VMEM,
        scratch_shapes=list(scratch),
        compiler_params=pltpu.CompilerParams(vmem_limit_bytes=16 * 1024 * 1024),
        cost_estimate=pl.CostEstimate(
            flops=int(micros * 1.15e9),
            bytes_accessed=0,
            transcendentals=0,
        ),
        name=name,
    )(*args)


def lanes_of(columns, rows, width=128):
    lane = lax.broadcasted_iota(jnp.int32, (rows, width), 1)
    packed = jnp.zeros((rows, width), F32)
    for index, column in enumerate(columns):
        packed = jnp.where(lane == index, column, packed)
    return packed


def project_body(full, *refs):
    far, near, refs = refs[:8], refs[-9:-1], list(refs[8:-9]) + [refs[-1]]
    normed, blocks, queries, raw, inverses, sems = refs
    gain, pos, reach, k_gain, q_gain, w_k, w_v, w_q = near
    copies = [
        pltpu.make_async_copy(source, target, sems.at[index])
        for index, (source, target) in enumerate(zip(far, near))
    ]
    for copy in copies:
        copy.start()
    values = full[...].astype(F32)
    rows, width = values.shape
    head = q_gain.shape[1]
    per_key = w_q.shape[1] // head
    inverse = lax.rsqrt(jnp.sum(values * values, axis=-1, keepdims=True) / width + EPSILON)
    for copy in copies[:5]:
        copy.wait()
    normed[...] = (values * inverse * gain[...]).astype(BF16)
    for copy in copies[5:]:
        copy.wait()
    k_raw = nn(normed[...], w_k[...])
    raw[:, per_key * head : (per_key + 1) * head] = k_raw
    k_inv = lax.rsqrt(jnp.mean(k_raw * k_raw, axis=-1, keepdims=True) + EPSILON)
    key_rows = (k_raw * k_inv * k_gain[...]).astype(BF16)
    v_raw = nn(normed[...], w_v[...])
    raw[:, (per_key + 1) * head :] = v_raw
    high = lax.shift_right_logical(pos[...], 6)
    row = lax.broadcasted_iota(jnp.int32, (TAIL, rows), 0)
    digits = jnp.where(row == 0, high, jnp.where(row == 1, pos[...] - high * 64, 0))
    for index in range(RING):
        blocks[index, :rows, :] = key_rows
        blocks[index, rows : 2 * rows, :] = v_raw.astype(BF16)
        blocks[index, 2 * rows :, :] = digits.astype(F32).astype(BF16)
    columns = []
    q_raw = nn(normed[...], w_q[...])
    raw[:, : per_key * head] = q_raw
    for index in range(per_key):
        part = q_raw[:, index * head : (index + 1) * head]
        inv = lax.rsqrt(jnp.mean(part * part, axis=-1, keepdims=True) + EPSILON)
        columns.append(inv)
        queries[:, index * head : (index + 1) * head] = (part * inv * q_gain[...]).astype(BF16)
    high = lax.shift_right_logical(reach[...], 6)
    row = lax.broadcasted_iota(jnp.int32, (rows, rows), 0)
    digits = jnp.where(row == 0, high, jnp.where(row == 1, reach[...] - high * 64, 0))
    queries[:, per_key * head :] = digits.astype(F32).T.astype(BF16)
    inverses[...] = lanes_of(columns + [k_inv, inverse], rows)


def turn_body(place, normed, *outs):
    count = len(outs)
    width = normed.shape[1] // count
    for index, out in enumerate(outs):
        start = pl.multiple_of(lax.rem(place[0] + index, count) * width, 128)
        out[...] = normed[:, pl.ds(start, width)].T


def stacked(refs, cols):
    return jnp.concatenate([ref[:, cols] for ref in refs], axis=0)


def key_tiles(blocks):
    token_rows = (blocks.shape[1] - TAIL) // 2
    for first in range(0, blocks.shape[0], 2):
        pair = range(first, first + 2)
        keys = jnp.concatenate([blocks[r, :token_rows, :] for r in pair], axis=0)
        values = jnp.concatenate([blocks[r, token_rows : 2 * token_rows, :] for r in pair], axis=0)
        places = []
        for r in pair:
            digits = blocks[r, 2 * token_rows :, :].astype(F32)
            places.append(digits[0:1] * 64.0 + digits[1:2])
        yield slice(first * token_rows, (first + 2) * token_rows), keys, values, jnp.concatenate(
            places, axis=1
        )


def forward_body(first, blocks, *refs):
    queries, refs = refs[:COLUMN], list(refs[COLUMN:])
    head = blocks.shape[2]
    width = queries[0].shape[1] - head
    rows = queries[0].shape[0] * COLUMN
    if first:
        sum_out, kept = refs
    else:
        ups, (sum_in, sum_out, stats, kept) = refs[:COLUMN], refs[COLUMN:]
    heads = width // head
    scale = head ** (-0.5) * LOG2E
    reach = stacked(queries, slice(width, width + head)).astype(F32)
    reach = reach[:, 0:1] * 64.0 + reach[:, 1:2]
    totals, dots = [], []
    for index in range(heads):
        cols = slice(index * head, (index + 1) * head)
        total_cols = slice(width + index * head, width + (index + 1) * head)
        query = stacked(queries, cols)
        summed = jnp.zeros((rows, head), F32) if first else sum_in[:, cols]
        total = jnp.zeros((rows, head), F32) if first else sum_in[:, total_cols]
        for span, keys, values, places in key_tiles(blocks):
            weights = jnp.where(places <= reach, jnp.exp2(nt(query, keys) * scale), 0.0)
            for r in range(weights.shape[1] // head):
                total = total + weights[:, r * head : (r + 1) * head]
            rounded = weights.astype(BF16)
            kept[index, :, span] = rounded
            summed = summed + nn(rounded, values)
        sum_out[:, cols] = summed
        if first:
            sum_out[:, total_cols] = total
        else:
            totals.append(jnp.sum(total, axis=-1, keepdims=True))
            up = stacked(ups, cols).astype(F32)
            dots.append(jnp.sum(up * summed, axis=-1, keepdims=True))
    if not first:
        stats[...] = lanes_of(dots + totals, rows).T[: 2 * heads]


def forward(blocks, queries, ups, sums):
    rows = queries[0].shape[0] * COLUMN
    head = blocks.shape[2]
    width = queries[0].shape[1] - head
    heads = width // head
    kept = shape((heads, rows, blocks.shape[0] * (blocks.shape[1] - TAIL) // 2), BF16)
    first = sums is None
    if first:
        out = [shape((rows, 2 * width), F32), kept]
        args = [blocks] + queries
    else:
        out = [shape((rows, width), F32), shape((2 * heads, rows), F32), kept]
        args = [blocks] + queries + ups + [sums]

    def body(*refs):
        forward_body(first, *refs)

    return call(body, out, args, micros=4.0, name="forward")


def finish_body(summed, *refs):
    stats, refs = refs[:COLUMN], refs[COLUMN:]
    queries, ups, refs = refs[:COLUMN], refs[COLUMN : 2 * COLUMN], refs[2 * COLUMN :]
    q_scaled, up_scaled, terms, outs = refs[0], refs[1], refs[2], refs[3:]
    rows, width = summed.shape
    part = rows // COLUMN
    heads = stats[0].shape[0] // 2
    head = width // heads
    scale = head ** (-0.5)
    joined = stats[0][...]
    for step in range(1, COLUMN):
        other = stats[step][...]
        cut = rows - step * part
        joined = joined + jnp.concatenate([other[:, cut:], other[:, :cut]], axis=1)
    fill = jnp.zeros((128 - 2 * heads, rows), F32)
    joined = jnp.concatenate([joined, fill], axis=0).T
    deltas, scales = [], []
    for index in range(heads):
        cols = slice(index * head, (index + 1) * head)
        inverse = 1.0 / joined[:, heads + index : heads + index + 1]
        deltas.append(joined[:, index : index + 1] * inverse)
        scales.append(inverse * scale)
        output = (summed[:, cols] * inverse).astype(BF16)
        for step, out in enumerate(outs):
            out[:, cols] = output[step * part : (step + 1) * part]
        up_scaled[:, cols] = (stacked(ups, cols).astype(F32) * inverse).astype(BF16)
        q_scaled[:, cols] = (stacked(queries, cols).astype(F32) * (inverse * scale)).astype(BF16)
    terms[...] = lanes_of(deltas + scales, rows)


def backward_body(last, blocks, kept, up_scaled, q_scaled, stats, *refs):
    ups, refs = refs[:COLUMN], list(refs[COLUMN:])
    grad_in = refs.pop(0) if last else None
    term, grad_out = refs[0], refs[1:]
    rows, width = q_scaled.shape
    part = rows // COLUMN
    head = blocks.shape[2]
    heads = width // head
    grads = [
        grad_in[:, h * head : (h + 1) * head] if last else jnp.zeros((rows, head), F32)
        for h in range(heads)
    ]
    for span, keys, values, _ in key_tiles(blocks):
        key_term = jnp.zeros((keys.shape[0], head), F32)
        value_term = jnp.zeros((keys.shape[0], head), F32)
        for index in range(heads):
            cols = slice(index * head, (index + 1) * head)
            weights = kept[index, :, span]
            prob_grad = nt(stacked(ups, cols), values)
            score_grad = (
                weights.astype(F32) * (prob_grad - stats[:, index : index + 1])
            ).astype(BF16)
            grads[index] = grads[index] + nn(score_grad, keys)
            key_term = key_term + tn(score_grad, q_scaled[:, cols])
            value_term = value_term + tn(weights, up_scaled[:, cols])
        term[span, :head] = key_term.astype(BF16)
        term[span, head:] = value_term.astype(BF16)
    for index in range(heads):
        cols = slice(index * head, (index + 1) * head)
        if last:
            grad = grads[index] * stats[:, heads + index : heads + index + 1]
            for step, out in enumerate(grad_out):
                out[:, cols] = grad[step * part : (step + 1) * part].astype(out.dtype)
        else:
            grad_out[0][:, cols] = grads[index]


def backward(blocks, kept, up_scaled, q_scaled, stats, ups, grad):
    rows, width = q_scaled.shape
    out = [shape((kept.shape[2], 2 * blocks.shape[2]), BF16)]
    last = grad is not None
    if last:
        out += [shape((rows // COLUMN, width), F32 if step == 0 else BF16) for step in range(COLUMN)]
    else:
        out += [shape((rows, width), F32)]
    args = [blocks, kept, up_scaled, q_scaled, stats] + ups + ([grad] if last else [])

    def body(*refs):
        backward_body(last, *refs)

    return call(body, out, args, micros=6.5, name="backward")


def back(upstream, hat, inverse, weight):
    scaled = weight * upstream
    return inverse * (scaled - hat * jnp.mean(scaled * hat, axis=-1, keepdims=True))


def grads_body(a, b, c, d, terms, raw, inverses, q_gain, k_gain, out):
    head = q_gain.shape[1]
    width = a.shape[1]
    heads = width // head
    for index in range(heads):
        cols = slice(index * head, (index + 1) * head)
        inv = inverses[:, index : index + 1]
        total = a[:, cols] + b[:, cols].astype(F32)
        total = total + c[:, cols].astype(F32) + d[:, cols].astype(F32)
        out[:, cols] = back(total, raw[:, cols] * inv, inv, q_gain[...]).astype(BF16)
    total = terms[0].astype(F32)
    for index in range(1, RING):
        total = total + terms[index].astype(F32)
    inv = inverses[:, heads : heads + 1]
    hat = raw[:, width : width + head] * inv
    out[:, width : width + head] = back(total[:, :head], hat, inv, k_gain[...]).astype(BF16)
    out[:, width + head :] = total[:, head:].astype(BF16)


def feature_body(place, grads, raw, w_q, w_k, w_v, *outs):
    count = len(outs)
    rows = grads.shape[0]
    head, width = w_k.shape[1], w_q.shape[1]
    features = w_q.shape[0] // count
    dot = jnp.sum(grads[...].astype(F32) * raw[...], axis=-1, keepdims=True)
    high = dot.astype(BF16).astype(F32)
    tail = lanes_of([high, dot - high], rows).astype(BF16)
    for index, out in enumerate(outs):
        start = pl.multiple_of(lax.rem(place[0] + index, count) * features, 128)
        part = nt(grads[:, :width], w_q[pl.ds(start, features), :])
        part = part + nt(grads[:, width : width + head], w_k[pl.ds(start, features), :])
        part = part + nt(grads[:, width + head :], w_v[pl.ds(start, features), :])
        out[:, :features] = part.astype(BF16)
        out[:, features:] = tail


def input_back_body(a, b, c, d, hidden, inverses, gain, out):
    features = hidden.shape[1]
    total = a[...].astype(F32) + b[...].astype(F32) + c[...].astype(F32) + d[...].astype(F32)
    dot = total[:, features : features + 1] + total[:, features + 1 : features + 2]
    mean = dot / (features * 4)
    inverse = inverses[:, 5:6]
    hat = hidden[...].astype(F32) * inverse
    out[...] = (inverse * (gain[...] * total[:, :features] - hat * mean)).astype(BF16)


def weight_body(place, *refs):
    sources, outs, product = refs[: 2 * COLUMN], refs[2 * COLUMN : -1], refs[-1]
    turned = jnp.concatenate([ref[...] for ref in sources[:COLUMN]], axis=1)
    grads = jnp.concatenate([ref[...] for ref in sources[COLUMN:]], axis=0)
    product[...] = nn(turned, grads).astype(BF16)
    rows = product.shape[0] // RING
    for index, out in enumerate(outs):
        start = pl.multiple_of(lax.rem(place[0] + index, RING) * rows, 16)
        out[...] = product[pl.ds(start, rows), :]


def weight_terms(place, turned, grads):
    rows, columns = turned[0].shape[0], grads[0].shape[1]
    return call(
        weight_body,
        [shape((rows // RING, columns), BF16)] * RING,
        [place] + turned + grads,
        smem=1,
        scratch=[pltpu.VMEM((rows, columns), BF16)],
        name="weight_terms",
    )


def ring_sum(terms, later, last):
    up, down = terms[4], terms[5]
    for step in range(4):
        up = along_z(up, 1)
        if step < 3:
            up = plus(up, terms[3 - step])
            down = along_z(down, -1)
        if step < 2:
            down = plus(down, terms[6 + step])
        if step == 0:
            up, down, later = lax.optimization_barrier((up, down, later))
        if step == 2:
            up, last = lax.optimization_barrier((up, last))
    return [terms[0], up, down], later, last


def collect_body(own, up, down, *outs):
    total = own[...].astype(F32) + up[...].astype(F32) + down[...].astype(F32)
    start = 0
    for out in outs:
        out[...] = total[:, start : start + out.shape[1]].astype(BF16)
        start += out.shape[1]


def across_z(terms):
    rows, columns = terms.shape
    rings = [[y * RING + z for z in range(RING)] for y in range(COLUMN)]
    terms = lax.all_to_all(terms, "seq", 0, 0, axis_index_groups=rings, tiled=True)
    return terms.reshape(RING, rows // RING, columns)


def along_z(value, step):
    pairs = [
        (y * RING + z, y * RING + (z + step) % RING) for y in range(COLUMN) for z in range(RING)
    ]
    return lax.ppermute(value, "seq", pairs)


def along_y(value, step):
    pairs = [
        (y * RING + z, (y + step) % COLUMN * RING + z) for y in range(COLUMN) for z in range(RING)
    ]
    return lax.ppermute(value, "seq", pairs)


def along_x(value, step):
    return lax.ppermute(value, "mp", [(x, (x + step) % 4) for x in range(4)])


def swapped(value):
    return lax.ppermute(value, "group", [(0, 1), (1, 0)])


def plus(*parts):
    total = parts[0].astype(F32)
    for part in parts[1:]:
        total = total + part.astype(F32)
    return total.astype(BF16)


def on_device(hidden, norm_gain, w_q, w_k, w_v, q_gain, k_gain, positions, reach, grad_out):
    place_x = lax.axis_index("mp").astype(jnp.int32)
    place = lax.axis_index("seq").astype(jnp.int32)
    place_y = place // RING
    rows, features = hidden.shape[1:]
    width = features * 4
    head = q_gain.shape[1]
    columns = w_q.shape[2]
    gain = norm_gain[0].reshape(1, width)
    local_gain = lax.dynamic_slice(gain, (0, place_x * features), (1, features))
    full = lax.all_gather(hidden[0], "mp", axis=1, tiled=True)
    sources = [gain, positions, reach, k_gain, q_gain, w_k[0], w_v[0], w_q[0]]
    normed, blocks, queries, raw, inverses = call(
        project_body,
        [
            shape((rows, width), BF16),
            shape((RING, 2 * rows + TAIL, head), BF16),
            shape((rows, columns + head), BF16),
            shape((rows, columns + 2 * head), F32),
            shape((rows, 128), F32),
        ],
        [full] + [pltpu.with_memory_space_constraint(value, pltpu.HBM) for value in sources],
        far=range(1, 9),
        scratch=[pltpu.VMEM(value.shape, value.dtype) for value in sources]
        + [pltpu.SemaphoreType.DMA((8,))],
        micros=4.0,
        name="project",
    )
    own_blocks = across_z(blocks.reshape(-1, head)).reshape(blocks.shape)
    queries = [queries] + [along_y(queries, step) for step in range(1, COLUMN)]
    ups = [grad_out[0]] + [along_y(grad_out[0], step) for step in range(1, COLUMN)]
    turned = call(
        turn_body,
        [shape((features, rows), BF16)] * COLUMN,
        [place_y.reshape(1), normed],
        smem=1,
        name="turn",
    )
    own_blocks, ups, turned = lax.optimization_barrier((own_blocks, ups, turned))
    other_blocks = swapped(own_blocks)
    sums, own_kept = forward(own_blocks, queries, ups, None)
    summed, stats, other_kept = forward(other_blocks, queries, ups, sums)
    finished = call(
        finish_body,
        [
            shape((COLUMN * rows, columns), BF16),
            shape((COLUMN * rows, columns), BF16),
            shape((COLUMN * rows, 128), F32),
        ]
        + [shape((rows, columns), BF16)] * COLUMN,
        [summed, stats] + [along_y(stats, step) for step in range(1, COLUMN)] + queries + ups,
        name="finish",
    )
    q_scaled, up_scaled, stats = finished[:3]
    outputs = finished[3:]
    stats, turned = lax.optimization_barrier((stats, turned))
    turned = [turned[0]] + [along_y(turned[step], step) for step in range(1, COLUMN)]
    other_terms, grad = backward(
        other_blocks, other_kept, up_scaled, q_scaled, stats, ups, None
    )
    grad, turned = lax.optimization_barrier((grad, turned))
    outs = backward(own_blocks, own_kept, up_scaled, q_scaled, stats, ups, grad)
    own_terms, query_grad = outs[0], list(outs[1:])
    own_terms = across_z(plus(own_terms, swapped(other_terms)))
    query_grad = [query_grad[0]] + [along_y(query_grad[step], -step) for step in range(1, COLUMN)]
    grads = call(
        grads_body,
        shape((rows, columns + 2 * head), BF16),
        query_grad + [own_terms, raw, inverses, q_gain, k_gain],
        name="grads",
    )
    all_grads = [grads] + [along_y(grads, step) for step in range(1, COLUMN)]
    feature_parts = call(
        feature_body,
        [shape((rows, features + 128), BF16)] * 4,
        [place_x.reshape(1), grads, raw, w_q[0], w_k[0], w_v[0]],
        smem=1,
        micros=5.0,
        name="feature",
    )
    first_part, all_grads = lax.optimization_barrier((feature_parts[0], all_grads))
    place_z = lax.rem(place, RING).reshape(1)
    terms = weight_terms(place_z, turned, all_grads)
    terms, sent = lax.optimization_barrier((terms, list(feature_parts[1:])))
    terms, outputs, local_gain = ring_sum(terms, outputs, local_gain)
    feature_parts = [first_part] + [along_x(sent[k - 1], k) for k in range(1, 4)]
    attended = plus(outputs[0], *[along_y(outputs[step], -step) for step in range(1, COLUMN)])
    input_grad = call(
        input_back_body,
        shape((rows, features), BF16),
        feature_parts + [hidden[0], inverses, local_gain],
        micros=8.0,
        name="input_back",
    )
    weight_rows = terms[0].shape[0]
    grad_wq, grad_wk, grad_wv = call(
        collect_body,
        [shape((weight_rows, size), BF16) for size in (columns, head, head)],
        terms,
        name="collect",
    )
    return (attended[None], input_grad[None], grad_wq[None], grad_wk[None], grad_wv[None])


def solution(mesh):
    return jax.shard_map(
        on_device,
        mesh=mesh,
        in_specs=(
            P("group", "seq", "mp"),
            P("group", None),
            P("group", None, "mp"),
            P("group", None, "mp"),
            P("group", None, "mp"),
            P("group", None),
            P("group", None),
            P("group", "seq"),
            P("group", "seq"),
            P("group", "seq", "mp"),
        ),
        out_specs=(P("group", "seq", "mp"),) * 5,
        check_vma=False,
    )
```

```python
import jax
import jax.numpy as jnp
from jax import lax
from jax.experimental import pallas as pl
from jax.experimental.pallas import tpu as pltpu
from jax.sharding import PartitionSpec as P

EPSILON = 1e-06
LOG2E = 1.4426950408889634
F32 = jnp.float32
BF16 = jnp.bfloat16
RING = 8
COLUMN = 4
TAIL = 16
VMEM = pl.BlockSpec(memory_space=pltpu.VMEM)
SMEM = pl.BlockSpec(memory_space=pltpu.SMEM)
FAR = pl.BlockSpec(memory_space=pltpu.HBM)


def nn(left, right):
    return lax.dot_general(left, right, (((1,), (0,)), ((), ())), preferred_element_type=F32)


def nt(left, right):
    return lax.dot_general(left, right, (((1,), (1,)), ((), ())), preferred_element_type=F32)


def tn(left, right):
    return lax.dot_general(left, right, (((0,), (0,)), ((), ())), preferred_element_type=F32)


def shape(dims, dtype):
    return jax.ShapeDtypeStruct(dims, dtype)


def call(body, out_shape, args, smem=0, far=(), scratch=(), micros=2.0, name=None):
    outs = out_shape if isinstance(out_shape, (list, tuple)) else [out_shape]
    return pl.pallas_call(
        body,
        out_shape=out_shape,
        in_specs=[
            SMEM if index < smem else FAR if index in far else VMEM for index in range(len(args))
        ],
        out_specs=[VMEM] * len(outs) if isinstance(out_shape, (list, tuple)) else VMEM,
        scratch_shapes=list(scratch),
        compiler_params=pltpu.CompilerParams(vmem_limit_bytes=16 * 1024 * 1024),
        cost_estimate=pl.CostEstimate(
            flops=int(micros * 1.15e9),
            bytes_accessed=0,
            transcendentals=0,
        ),
        name=name,
    )(*args)


def lanes_of(columns, rows, width=128):
    lane = lax.broadcasted_iota(jnp.int32, (rows, width), 1)
    packed = jnp.zeros((rows, width), F32)
    for index, column in enumerate(columns):
        packed = jnp.where(lane == index, column, packed)
    return packed


def project_body(full, *refs):
    far, near, refs = refs[:8], refs[-9:-1], list(refs[8:-9]) + [refs[-1]]
    normed, blocks, queries, raw, inverses, sems = refs
    gain, pos, reach, k_gain, q_gain, w_k, w_v, w_q = near
    copies = [
        pltpu.make_async_copy(source, target, sems.at[index])
        for index, (source, target) in enumerate(zip(far, near))
    ]
    for copy in copies:
        copy.start()
    values = full[...].astype(F32)
    rows, width = values.shape
    head = q_gain.shape[1]
    per_key = w_q.shape[1] // head
    inverse = lax.rsqrt(jnp.sum(values * values, axis=-1, keepdims=True) / width + EPSILON)
    for copy in copies[:5]:
        copy.wait()
    normed[...] = (values * inverse * gain[...]).astype(BF16)
    for copy in copies[5:]:
        copy.wait()
    k_raw = nn(normed[...], w_k[...])
    raw[:, per_key * head : (per_key + 1) * head] = k_raw
    k_inv = lax.rsqrt(jnp.mean(k_raw * k_raw, axis=-1, keepdims=True) + EPSILON)
    key_rows = (k_raw * k_inv * k_gain[...]).astype(BF16)
    v_raw = nn(normed[...], w_v[...])
    raw[:, (per_key + 1) * head :] = v_raw
    high = lax.shift_right_logical(pos[...], 6)
    row = lax.broadcasted_iota(jnp.int32, (TAIL, rows), 0)
    digits = jnp.where(row == 0, high, jnp.where(row == 1, pos[...] - high * 64, 0))
    for index in range(RING):
        blocks[index, :rows, :] = key_rows
        blocks[index, rows : 2 * rows, :] = v_raw.astype(BF16)
        blocks[index, 2 * rows :, :] = digits.astype(F32).astype(BF16)
    columns = []
    q_raw = nn(normed[...], w_q[...])
    raw[:, : per_key * head] = q_raw
    for index in range(per_key):
        part = q_raw[:, index * head : (index + 1) * head]
        inv = lax.rsqrt(jnp.mean(part * part, axis=-1, keepdims=True) + EPSILON)
        columns.append(inv)
        queries[:, index * head : (index + 1) * head] = (part * inv * q_gain[...]).astype(BF16)
    high = lax.shift_right_logical(reach[...], 6)
    row = lax.broadcasted_iota(jnp.int32, (rows, rows), 0)
    digits = jnp.where(row == 0, high, jnp.where(row == 1, reach[...] - high * 64, 0))
    queries[:, per_key * head :] = digits.astype(F32).T.astype(BF16)
    inverses[...] = lanes_of(columns + [k_inv, inverse], rows)


def turn_body(place, normed, *outs):
    count = len(outs)
    width = normed.shape[1] // count
    for index, out in enumerate(outs):
        start = pl.multiple_of(lax.rem(place[0] + index, count) * width, 128)
        out[...] = normed[:, pl.ds(start, width)].T


def stacked(refs, cols):
    return jnp.concatenate([ref[:, cols] for ref in refs], axis=0)


def key_tiles(blocks):
    token_rows = (blocks.shape[1] - TAIL) // 2
    for first in range(0, blocks.shape[0], 2):
        pair = range(first, first + 2)
        keys = jnp.concatenate([blocks[r, :token_rows, :] for r in pair], axis=0)
        values = jnp.concatenate([blocks[r, token_rows : 2 * token_rows, :] for r in pair], axis=0)
        places = []
        for r in pair:
            digits = blocks[r, 2 * token_rows :, :].astype(F32)
            places.append(digits[0:1] * 64.0 + digits[1:2])
        yield slice(first * token_rows, (first + 2) * token_rows), keys, values, jnp.concatenate(
            places, axis=1
        )


def forward_body(first, blocks, *refs):
    queries, refs = refs[:COLUMN], list(refs[COLUMN:])
    head = blocks.shape[2]
    width = queries[0].shape[1] - head
    rows = queries[0].shape[0] * COLUMN
    if first:
        sum_out, kept = refs
    else:
        ups, (sum_in, sum_out, stats, kept) = refs[:COLUMN], refs[COLUMN:]
    heads = width // head
    scale = head ** (-0.5) * LOG2E
    reach = stacked(queries, slice(width, width + head)).astype(F32)
    reach = reach[:, 0:1] * 64.0 + reach[:, 1:2]
    totals, dots = [], []
    for index in range(heads):
        cols = slice(index * head, (index + 1) * head)
        total_cols = slice(width + index * head, width + (index + 1) * head)
        query = stacked(queries, cols)
        summed = jnp.zeros((rows, head), F32) if first else sum_in[:, cols]
        total = jnp.zeros((rows, head), F32) if first else sum_in[:, total_cols]
        for span, keys, values, places in key_tiles(blocks):
            weights = jnp.where(places <= reach, jnp.exp2(nt(query, keys) * scale), 0.0)
            for r in range(weights.shape[1] // head):
                total = total + weights[:, r * head : (r + 1) * head]
            rounded = weights.astype(BF16)
            kept[index, :, span] = rounded
            summed = summed + nn(rounded, values)
        sum_out[:, cols] = summed
        if first:
            sum_out[:, total_cols] = total
        else:
            totals.append(jnp.sum(total, axis=-1, keepdims=True))
            up = stacked(ups, cols).astype(F32)
            dots.append(jnp.sum(up * summed, axis=-1, keepdims=True))
    if not first:
        stats[...] = lanes_of(dots + totals, rows).T[: 2 * heads]


def forward(blocks, queries, ups, sums):
    rows = queries[0].shape[0] * COLUMN
    head = blocks.shape[2]
    width = queries[0].shape[1] - head
    heads = width // head
    kept = shape((heads, rows, blocks.shape[0] * (blocks.shape[1] - TAIL) // 2), BF16)
    first = sums is None
    if first:
        out = [shape((rows, 2 * width), F32), kept]
        args = [blocks] + queries
    else:
        out = [shape((rows, width), F32), shape((2 * heads, rows), F32), kept]
        args = [blocks] + queries + ups + [sums]

    def body(*refs):
        forward_body(first, *refs)

    return call(body, out, args, micros=4.0, name="forward")


def finish_body(summed, *refs):
    stats, refs = refs[:COLUMN], refs[COLUMN:]
    queries, ups, refs = refs[:COLUMN], refs[COLUMN : 2 * COLUMN], refs[2 * COLUMN :]
    q_scaled, up_scaled, terms, outs = refs[0], refs[1], refs[2], refs[3:]
    rows, width = summed.shape
    part = rows // COLUMN
    heads = stats[0].shape[0] // 2
    head = width // heads
    scale = head ** (-0.5)
    joined = stats[0][...]
    for step in range(1, COLUMN):
        other = stats[step][...]
        cut = rows - step * part
        joined = joined + jnp.concatenate([other[:, cut:], other[:, :cut]], axis=1)
    fill = jnp.zeros((128 - 2 * heads, rows), F32)
    joined = jnp.concatenate([joined, fill], axis=0).T
    deltas, scales = [], []
    for index in range(heads):
        cols = slice(index * head, (index + 1) * head)
        inverse = 1.0 / joined[:, heads + index : heads + index + 1]
        deltas.append(joined[:, index : index + 1] * inverse)
        scales.append(inverse * scale)
        output = (summed[:, cols] * inverse).astype(BF16)
        for step, out in enumerate(outs):
            out[:, cols] = output[step * part : (step + 1) * part]
        up_scaled[:, cols] = (stacked(ups, cols).astype(F32) * inverse).astype(BF16)
        q_scaled[:, cols] = (stacked(queries, cols).astype(F32) * (inverse * scale)).astype(BF16)
    terms[...] = lanes_of(deltas + scales, rows)


def backward_body(last, blocks, kept, up_scaled, q_scaled, stats, *refs):
    ups, refs = refs[:COLUMN], list(refs[COLUMN:])
    grad_in = refs.pop(0) if last else None
    term, grad_out = refs[0], refs[1:]
    rows, width = q_scaled.shape
    part = rows // COLUMN
    head = blocks.shape[2]
    heads = width // head
    grads = [
        grad_in[:, h * head : (h + 1) * head] if last else jnp.zeros((rows, head), F32)
        for h in range(heads)
    ]
    for span, keys, values, _ in key_tiles(blocks):
        key_term = jnp.zeros((keys.shape[0], head), F32)
        value_term = jnp.zeros((keys.shape[0], head), F32)
        for index in range(heads):
            cols = slice(index * head, (index + 1) * head)
            weights = kept[index, :, span]
            prob_grad = nt(stacked(ups, cols), values)
            score_grad = (
                weights.astype(F32) * (prob_grad - stats[:, index : index + 1])
            ).astype(BF16)
            grads[index] = grads[index] + nn(score_grad, keys)
            key_term = key_term + tn(score_grad, q_scaled[:, cols])
            value_term = value_term + tn(weights, up_scaled[:, cols])
        term[span, :head] = key_term.astype(BF16)
        term[span, head:] = value_term.astype(BF16)
    for index in range(heads):
        cols = slice(index * head, (index + 1) * head)
        if last:
            grad = grads[index] * stats[:, heads + index : heads + index + 1]
            for step, out in enumerate(grad_out):
                out[:, cols] = grad[step * part : (step + 1) * part].astype(out.dtype)
        else:
            grad_out[0][:, cols] = grads[index]


def backward(blocks, kept, up_scaled, q_scaled, stats, ups, grad):
    rows, width = q_scaled.shape
    out = [shape((kept.shape[2], 2 * blocks.shape[2]), BF16)]
    last = grad is not None
    if last:
        out += [shape((rows // COLUMN, width), F32 if step == 0 else BF16) for step in range(COLUMN)]
    else:
        out += [shape((rows, width), F32)]
    args = [blocks, kept, up_scaled, q_scaled, stats] + ups + ([grad] if last else [])

    def body(*refs):
        backward_body(last, *refs)

    return call(body, out, args, micros=6.5, name="backward")


def back(upstream, hat, inverse, weight):
    scaled = weight * upstream
    return inverse * (scaled - hat * jnp.mean(scaled * hat, axis=-1, keepdims=True))


def grads_body(a, b, c, d, terms, raw, inverses, q_gain, k_gain, *refs):
    parts, (out, attended) = refs[:COLUMN], refs[COLUMN:]
    head = q_gain.shape[1]
    width = a.shape[1]
    heads = width // head
    for index in range(heads):
        cols = slice(index * head, (index + 1) * head)
        inv = inverses[:, index : index + 1]
        total = a[:, cols] + b[:, cols].astype(F32)
        total = total + c[:, cols].astype(F32) + d[:, cols].astype(F32)
        out[:, cols] = back(total, raw[:, cols] * inv, inv, q_gain[...]).astype(BF16)
    total = terms[0].astype(F32)
    for index in range(1, RING):
        total = total + terms[index].astype(F32)
    inv = inverses[:, heads : heads + 1]
    hat = raw[:, width : width + head] * inv
    out[:, width : width + head] = back(total[:, :head], hat, inv, k_gain[...]).astype(BF16)
    out[:, width + head :] = total[:, head:].astype(BF16)
    output = parts[0][...].astype(F32)
    for part in parts[1:]:
        output = output + part[...].astype(F32)
    attended[...] = output.astype(BF16)


def feature_body(place, grads, raw, w_q, w_k, w_v, *outs):
    count = len(outs)
    rows = grads.shape[0]
    head, width = w_k.shape[1], w_q.shape[1]
    features = w_q.shape[0] // count
    dot = jnp.sum(grads[...].astype(F32) * raw[...], axis=-1, keepdims=True)
    high = dot.astype(BF16).astype(F32)
    tail = lanes_of([high, dot - high], rows).astype(BF16)
    for index, out in enumerate(outs):
        start = pl.multiple_of(lax.rem(place[0] + index, count) * features, 128)
        part = nt(grads[:, :width], w_q[pl.ds(start, features), :])
        part = part + nt(grads[:, width : width + head], w_k[pl.ds(start, features), :])
        part = part + nt(grads[:, width + head :], w_v[pl.ds(start, features), :])
        out[:, :features] = part.astype(BF16)
        out[:, features:] = tail


def input_back_body(a, b, c, d, hidden, inverses, gain, out):
    features = hidden.shape[1]
    total = a[...].astype(F32) + b[...].astype(F32) + c[...].astype(F32) + d[...].astype(F32)
    dot = total[:, features : features + 1] + total[:, features + 1 : features + 2]
    mean = dot / (features * 4)
    inverse = inverses[:, 5:6]
    hat = hidden[...].astype(F32) * inverse
    out[...] = (inverse * (gain[...] * total[:, :features] - hat * mean)).astype(BF16)


def weight_body(place, *refs):
    sources, outs, product = refs[: 2 * COLUMN], refs[2 * COLUMN : -1], refs[-1]
    turned = jnp.concatenate([ref[...] for ref in sources[:COLUMN]], axis=1)
    grads = jnp.concatenate([ref[...] for ref in sources[COLUMN:]], axis=0)
    product[...] = nn(turned, grads).astype(BF16)
    rows = product.shape[0] // RING
    for index, out in enumerate(outs):
        start = pl.multiple_of(lax.rem(place[0] + index, RING) * rows, 16)
        out[...] = product[pl.ds(start, rows), :]


def weight_terms(place, turned, grads):
    rows, columns = turned[0].shape[0], grads[0].shape[1]
    return call(
        weight_body,
        [shape((rows // RING, columns), BF16)] * RING,
        [place] + turned + grads,
        smem=1,
        scratch=[pltpu.VMEM((rows, columns), BF16)],
        name="weight_terms",
    )


def ring_sum(terms):
    up, down = terms[4], terms[5]
    for step in range(4):
        up = along_z(up, 1)
        if step < 3:
            up = plus(up, terms[3 - step])
            down = along_z(down, -1)
        if step < 2:
            down = plus(down, terms[6 + step])
    return [terms[0], up, down]


def collect_body(own, up, down, *outs):
    total = own[...].astype(F32) + up[...].astype(F32) + down[...].astype(F32)
    start = 0
    for out in outs:
        out[...] = total[:, start : start + out.shape[1]].astype(BF16)
        start += out.shape[1]


def across_z(terms):
    rows, columns = terms.shape
    rings = [[y * RING + z for z in range(RING)] for y in range(COLUMN)]
    terms = lax.all_to_all(terms, "seq", 0, 0, axis_index_groups=rings, tiled=True)
    return terms.reshape(RING, rows // RING, columns)


def along_z(value, step):
    pairs = [
        (y * RING + z, y * RING + (z + step) % RING) for y in range(COLUMN) for z in range(RING)
    ]
    return lax.ppermute(value, "seq", pairs)


def along_y(value, step):
    pairs = [
        (y * RING + z, (y + step) % COLUMN * RING + z) for y in range(COLUMN) for z in range(RING)
    ]
    return lax.ppermute(value, "seq", pairs)


def along_x(value, step):
    return lax.ppermute(value, "mp", [(x, (x + step) % 4) for x in range(4)])


def swapped(value):
    return lax.ppermute(value, "group", [(0, 1), (1, 0)])


def plus(*parts):
    total = parts[0].astype(F32)
    for part in parts[1:]:
        total = total + part.astype(F32)
    return total.astype(BF16)


def on_device(hidden, norm_gain, w_q, w_k, w_v, q_gain, k_gain, positions, reach, grad_out):
    place_x = lax.axis_index("mp").astype(jnp.int32)
    place = lax.axis_index("seq").astype(jnp.int32)
    place_y = place // RING
    rows, features = hidden.shape[1:]
    width = features * 4
    head = q_gain.shape[1]
    columns = w_q.shape[2]
    gain = norm_gain[0].reshape(1, width)
    local_gain = lax.dynamic_slice(gain, (0, place_x * features), (1, features))
    full = lax.all_gather(hidden[0], "mp", axis=1, tiled=True)
    sources = [gain, positions, reach, k_gain, q_gain, w_k[0], w_v[0], w_q[0]]
    normed, blocks, queries, raw, inverses = call(
        project_body,
        [
            shape((rows, width), BF16),
            shape((RING, 2 * rows + TAIL, head), BF16),
            shape((rows, columns + head), BF16),
            shape((rows, columns + 2 * head), F32),
            shape((rows, 128), F32),
        ],
        [full] + [pltpu.with_memory_space_constraint(value, pltpu.HBM) for value in sources],
        far=range(1, 9),
        scratch=[pltpu.VMEM(value.shape, value.dtype) for value in sources]
        + [pltpu.SemaphoreType.DMA((8,))],
        micros=4.0,
        name="project",
    )
    own_blocks = across_z(blocks.reshape(-1, head)).reshape(blocks.shape)
    queries = [queries] + [along_y(queries, step) for step in range(1, COLUMN)]
    ups = [grad_out[0]] + [along_y(grad_out[0], step) for step in range(1, COLUMN)]
    turned = call(
        turn_body,
        [shape((features, rows), BF16)] * COLUMN,
        [place_y.reshape(1), normed],
        smem=1,
        name="turn",
    )
    own_blocks, ups, turned = lax.optimization_barrier((own_blocks, ups, turned))
    other_blocks = swapped(own_blocks)
    sums, own_kept = forward(own_blocks, queries, ups, None)
    summed, stats, other_kept = forward(other_blocks, queries, ups, sums)
    finished = call(
        finish_body,
        [
            shape((COLUMN * rows, columns), BF16),
            shape((COLUMN * rows, columns), BF16),
            shape((COLUMN * rows, 128), F32),
        ]
        + [shape((rows, columns), BF16)] * COLUMN,
        [summed, stats] + [along_y(stats, step) for step in range(1, COLUMN)] + queries + ups,
        name="finish",
    )
    q_scaled, up_scaled, stats = finished[:3]
    outputs = finished[3:]
    stats, turned = lax.optimization_barrier((stats, turned))
    turned = [turned[0]] + [along_y(turned[step], step) for step in range(1, COLUMN)]
    other_terms, grad = backward(
        other_blocks, other_kept, up_scaled, q_scaled, stats, ups, None
    )
    grad, turned = lax.optimization_barrier((grad, turned))
    outs = backward(own_blocks, own_kept, up_scaled, q_scaled, stats, ups, grad)
    own_terms, query_grad = outs[0], list(outs[1:])
    own_terms = plus(own_terms, swapped(other_terms))
    own_terms, outputs = lax.optimization_barrier((own_terms, outputs))
    own_terms = across_z(own_terms)
    query_grad = [query_grad[0]] + [along_y(query_grad[step], -step) for step in range(1, COLUMN)]
    outputs = [outputs[0]] + [along_y(outputs[step], -step) for step in range(1, COLUMN)]
    query_grad, outputs = lax.optimization_barrier((query_grad, outputs))
    grads, attended = call(
        grads_body,
        [shape((rows, columns + 2 * head), BF16), shape((rows, columns), BF16)],
        query_grad + [own_terms, raw, inverses, q_gain, k_gain] + outputs,
        name="grads",
    )
    all_grads = [grads] + [along_y(grads, step) for step in range(1, COLUMN)]
    feature_parts = call(
        feature_body,
        [shape((rows, features + 128), BF16)] * 4,
        [place_x.reshape(1), grads, raw, w_q[0], w_k[0], w_v[0]],
        smem=1,
        micros=5.0,
        name="feature",
    )
    first_part, all_grads = lax.optimization_barrier((feature_parts[0], all_grads))
    place_z = lax.rem(place, RING).reshape(1)
    terms = weight_terms(place_z, turned, all_grads)
    sent = feature_parts[1:]
    terms = ring_sum(terms)
    feature_parts = [first_part] + [along_x(sent[k - 1], k) for k in range(1, 4)]
    input_grad = call(
        input_back_body,
        shape((rows, features), BF16),
        feature_parts + [hidden[0], inverses, local_gain],
        micros=8.0,
        name="input_back",
    )
    weight_rows = terms[0].shape[0]
    grad_wq, grad_wk, grad_wv = call(
        collect_body,
        [shape((weight_rows, size), BF16) for size in (columns, head, head)],
        terms,
        name="collect",
    )
    return (attended[None], input_grad[None], grad_wq[None], grad_wk[None], grad_wv[None])


def solution(mesh):
    return jax.shard_map(
        on_device,
        mesh=mesh,
        in_specs=(
            P("group", "seq", "mp"),
            P("group", None),
            P("group", None, "mp"),
            P("group", None, "mp"),
            P("group", None, "mp"),
            P("group", None),
            P("group", None),
            P("group", "seq"),
            P("group", "seq"),
            P("group", "seq", "mp"),
        ),
        out_specs=(P("group", "seq", "mp"),) * 5,
        check_vma=False,
    )
```

```python
import jax
import jax.numpy as jnp
from jax import lax
from jax.experimental import pallas as pl
from jax.experimental.pallas import tpu as pltpu
from jax.sharding import PartitionSpec as P

EPSILON = 1e-06
LOG2E = 1.4426950408889634
F32 = jnp.float32
BF16 = jnp.bfloat16
RING = 8
COLUMN = 4
TAIL = 16
VMEM = pl.BlockSpec(memory_space=pltpu.VMEM)
SMEM = pl.BlockSpec(memory_space=pltpu.SMEM)
FAR = pl.BlockSpec(memory_space=pltpu.HBM)


def nn(left, right):
    return lax.dot_general(left, right, (((1,), (0,)), ((), ())), preferred_element_type=F32)


def nt(left, right):
    return lax.dot_general(left, right, (((1,), (1,)), ((), ())), preferred_element_type=F32)


def tn(left, right):
    return lax.dot_general(left, right, (((0,), (0,)), ((), ())), preferred_element_type=F32)


def shape(dims, dtype):
    return jax.ShapeDtypeStruct(dims, dtype)


def call(body, out_shape, args, smem=0, far=(), scratch=(), micros=2.0, name=None):
    outs = out_shape if isinstance(out_shape, (list, tuple)) else [out_shape]
    return pl.pallas_call(
        body,
        out_shape=out_shape,
        in_specs=[
            SMEM if index < smem else FAR if index in far else VMEM for index in range(len(args))
        ],
        out_specs=[VMEM] * len(outs) if isinstance(out_shape, (list, tuple)) else VMEM,
        scratch_shapes=list(scratch),
        compiler_params=pltpu.CompilerParams(vmem_limit_bytes=16 * 1024 * 1024),
        cost_estimate=pl.CostEstimate(
            flops=int(micros * 1.15e9),
            bytes_accessed=0,
            transcendentals=0,
        ),
        name=name,
    )(*args)


def lanes_of(columns, rows, width=128):
    lane = lax.broadcasted_iota(jnp.int32, (rows, width), 1)
    packed = jnp.zeros((rows, width), F32)
    for index, column in enumerate(columns):
        packed = jnp.where(lane == index, column, packed)
    return packed


def project_body(place, full, *refs):
    far, outs, near = refs[:8], refs[8:16], refs[16:24]
    normed, sems = refs[24:]
    blocks, queries, raw, inverses = outs[:4]
    gain, pos, reach, k_gain, q_gain, w_k, w_v, w_q = near
    copies = [
        pltpu.make_async_copy(source, target, sems.at[index])
        for index, (source, target) in enumerate(zip(far, near))
    ]
    for copy in copies:
        copy.start()
    values = full[...].astype(F32)
    rows, width = values.shape
    head = q_gain.shape[1]
    per_key = w_q.shape[1] // head
    inverse = lax.rsqrt(jnp.sum(values * values, axis=-1, keepdims=True) / width + EPSILON)
    for copy in copies[:5]:
        copy.wait()
    normed[...] = (values * inverse * gain[...]).astype(BF16)
    for copy in copies[5:]:
        copy.wait()
    k_raw = nn(normed[...], w_k[...])
    raw[:, per_key * head : (per_key + 1) * head] = k_raw
    k_inv = lax.rsqrt(jnp.mean(k_raw * k_raw, axis=-1, keepdims=True) + EPSILON)
    key_rows = (k_raw * k_inv * k_gain[...]).astype(BF16)
    v_raw = nn(normed[...], w_v[...])
    raw[:, (per_key + 1) * head :] = v_raw
    high = lax.shift_right_logical(pos[...], 6)
    row = lax.broadcasted_iota(jnp.int32, (TAIL, rows), 0)
    digits = jnp.where(row == 0, high, jnp.where(row == 1, pos[...] - high * 64, 0))
    for index in range(RING):
        blocks[index, :rows, :] = key_rows
        blocks[index, rows : 2 * rows, :] = v_raw.astype(BF16)
        blocks[index, 2 * rows :, :] = digits.astype(F32).astype(BF16)
    columns = []
    q_raw = nn(normed[...], w_q[...])
    raw[:, : per_key * head] = q_raw
    for index in range(per_key):
        part = q_raw[:, index * head : (index + 1) * head]
        inv = lax.rsqrt(jnp.mean(part * part, axis=-1, keepdims=True) + EPSILON)
        columns.append(inv)
        queries[:, index * head : (index + 1) * head] = (part * inv * q_gain[...]).astype(BF16)
    high = lax.shift_right_logical(reach[...], 6)
    row = lax.broadcasted_iota(jnp.int32, (rows, rows), 0)
    digits = jnp.where(row == 0, high, jnp.where(row == 1, reach[...] - high * 64, 0))
    queries[:, per_key * head :] = digits.astype(F32).T.astype(BF16)
    inverses[...] = lanes_of(columns + [k_inv, inverse], rows)
    part = width // COLUMN
    for index, out in enumerate(outs[4:]):
        start = pl.multiple_of(lax.rem(place[0] + index, COLUMN) * part, 128)
        out[...] = normed[:, pl.ds(start, part)].T


def stacked(refs, cols):
    return jnp.concatenate([ref[:, cols] for ref in refs], axis=0)


def key_tiles(blocks):
    token_rows = (blocks.shape[1] - TAIL) // 2
    for first in range(0, blocks.shape[0], 2):
        pair = range(first, first + 2)
        keys = jnp.concatenate([blocks[r, :token_rows, :] for r in pair], axis=0)
        values = jnp.concatenate([blocks[r, token_rows : 2 * token_rows, :] for r in pair], axis=0)
        places = []
        for r in pair:
            digits = blocks[r, 2 * token_rows :, :].astype(F32)
            places.append(digits[0:1] * 64.0 + digits[1:2])
        yield slice(first * token_rows, (first + 2) * token_rows), keys, values, jnp.concatenate(
            places, axis=1
        )


def forward_body(first, blocks, *refs):
    queries, refs = refs[:COLUMN], list(refs[COLUMN:])
    head = blocks.shape[2]
    width = queries[0].shape[1] - head
    rows = queries[0].shape[0] * COLUMN
    if first:
        sum_out, kept = refs
    else:
        ups, (sum_in, sum_out, stats, kept) = refs[:COLUMN], refs[COLUMN:]
    heads = width // head
    scale = head ** (-0.5) * LOG2E
    reach = stacked(queries, slice(width, width + head)).astype(F32)
    reach = reach[:, 0:1] * 64.0 + reach[:, 1:2]
    totals, dots = [], []
    for index in range(heads):
        cols = slice(index * head, (index + 1) * head)
        total_cols = slice(width + index * head, width + (index + 1) * head)
        query = stacked(queries, cols)
        summed = jnp.zeros((rows, head), F32) if first else sum_in[:, cols]
        total = jnp.zeros((rows, head), F32) if first else sum_in[:, total_cols]
        for span, keys, values, places in key_tiles(blocks):
            weights = jnp.where(places <= reach, jnp.exp2(nt(query, keys) * scale), 0.0)
            for r in range(weights.shape[1] // head):
                total = total + weights[:, r * head : (r + 1) * head]
            rounded = weights.astype(BF16)
            kept[index, :, span] = rounded
            summed = summed + nn(rounded, values)
        sum_out[:, cols] = summed
        if first:
            sum_out[:, total_cols] = total
        else:
            totals.append(jnp.sum(total, axis=-1, keepdims=True))
            up = stacked(ups, cols).astype(F32)
            dots.append(jnp.sum(up * summed, axis=-1, keepdims=True))
    if not first:
        stats[...] = lanes_of(dots + totals, rows).T[: 2 * heads]


def forward(blocks, queries, ups, sums):
    rows = queries[0].shape[0] * COLUMN
    head = blocks.shape[2]
    width = queries[0].shape[1] - head
    heads = width // head
    kept = shape((heads, rows, blocks.shape[0] * (blocks.shape[1] - TAIL) // 2), BF16)
    first = sums is None
    if first:
        out = [shape((rows, 2 * width), F32), kept]
        args = [blocks] + queries
    else:
        out = [shape((rows, width), F32), shape((2 * heads, rows), F32), kept]
        args = [blocks] + queries + ups + [sums]

    def body(*refs):
        forward_body(first, *refs)

    return call(body, out, args, micros=4.0, name="forward")


def finish_body(summed, *refs):
    stats, refs = refs[:COLUMN], refs[COLUMN:]
    queries, ups, refs = refs[:COLUMN], refs[COLUMN : 2 * COLUMN], refs[2 * COLUMN :]
    q_scaled, up_scaled, terms, outs = refs[0], refs[1], refs[2], refs[3:]
    rows, width = summed.shape
    part = rows // COLUMN
    heads = stats[0].shape[0] // 2
    head = width // heads
    scale = head ** (-0.5)
    joined = stats[0][...]
    for step in range(1, COLUMN):
        other = stats[step][...]
        cut = rows - step * part
        joined = joined + jnp.concatenate([other[:, cut:], other[:, :cut]], axis=1)
    fill = jnp.zeros((128 - 2 * heads, rows), F32)
    joined = jnp.concatenate([joined, fill], axis=0).T
    deltas, scales = [], []
    for index in range(heads):
        cols = slice(index * head, (index + 1) * head)
        inverse = 1.0 / joined[:, heads + index : heads + index + 1]
        deltas.append(joined[:, index : index + 1] * inverse)
        scales.append(inverse * scale)
        output = (summed[:, cols] * inverse).astype(BF16)
        for step, out in enumerate(outs):
            out[:, cols] = output[step * part : (step + 1) * part]
        up_scaled[:, cols] = (stacked(ups, cols).astype(F32) * inverse).astype(BF16)
        q_scaled[:, cols] = (stacked(queries, cols).astype(F32) * (inverse * scale)).astype(BF16)
    terms[...] = lanes_of(deltas + scales, rows)


def backward_body(last, blocks, kept, up_scaled, q_scaled, stats, *refs):
    ups, refs = refs[:COLUMN], list(refs[COLUMN:])
    grad_in = refs.pop(0) if last else None
    term, grad_out = refs[0], refs[1:]
    rows, width = q_scaled.shape
    part = rows // COLUMN
    head = blocks.shape[2]
    heads = width // head
    grads = [
        grad_in[:, h * head : (h + 1) * head] if last else jnp.zeros((rows, head), F32)
        for h in range(heads)
    ]
    for span, keys, values, _ in key_tiles(blocks):
        key_term = jnp.zeros((keys.shape[0], head), F32)
        value_term = jnp.zeros((keys.shape[0], head), F32)
        for index in range(heads):
            cols = slice(index * head, (index + 1) * head)
            weights = kept[index, :, span]
            prob_grad = nt(stacked(ups, cols), values)
            score_grad = (
                weights.astype(F32) * (prob_grad - stats[:, index : index + 1])
            ).astype(BF16)
            grads[index] = grads[index] + nn(score_grad, keys)
            key_term = key_term + tn(score_grad, q_scaled[:, cols])
            value_term = value_term + tn(weights, up_scaled[:, cols])
        term[span, :head] = key_term.astype(BF16)
        term[span, head:] = value_term.astype(BF16)
    for index in range(heads):
        cols = slice(index * head, (index + 1) * head)
        if last:
            grad = grads[index] * stats[:, heads + index : heads + index + 1]
            for step, out in enumerate(grad_out):
                out[:, cols] = grad[step * part : (step + 1) * part].astype(out.dtype)
        else:
            grad_out[0][:, cols] = grads[index]


def backward(blocks, kept, up_scaled, q_scaled, stats, ups, grad):
    rows, width = q_scaled.shape
    out = [shape((kept.shape[2], 2 * blocks.shape[2]), BF16)]
    last = grad is not None
    if last:
        out += [shape((rows // COLUMN, width), F32 if step == 0 else BF16) for step in range(COLUMN)]
    else:
        out += [shape((rows, width), F32)]
    args = [blocks, kept, up_scaled, q_scaled, stats] + ups + ([grad] if last else [])

    def body(*refs):
        backward_body(last, *refs)

    return call(body, out, args, micros=6.5, name="backward")


def back(upstream, hat, inverse, weight):
    scaled = weight * upstream
    return inverse * (scaled - hat * jnp.mean(scaled * hat, axis=-1, keepdims=True))


def grads_body(a, b, c, d, terms, raw, inverses, q_gain, k_gain, *refs):
    parts, (out, attended) = refs[:COLUMN], refs[COLUMN:]
    head = q_gain.shape[1]
    width = a.shape[1]
    heads = width // head
    for index in range(heads):
        cols = slice(index * head, (index + 1) * head)
        inv = inverses[:, index : index + 1]
        total = a[:, cols] + b[:, cols].astype(F32)
        total = total + c[:, cols].astype(F32) + d[:, cols].astype(F32)
        out[:, cols] = back(total, raw[:, cols] * inv, inv, q_gain[...]).astype(BF16)
    total = terms[0].astype(F32)
    for index in range(1, RING):
        total = total + terms[index].astype(F32)
    inv = inverses[:, heads : heads + 1]
    hat = raw[:, width : width + head] * inv
    out[:, width : width + head] = back(total[:, :head], hat, inv, k_gain[...]).astype(BF16)
    out[:, width + head :] = total[:, head:].astype(BF16)
    output = parts[0][...].astype(F32)
    for part in parts[1:]:
        output = output + part[...].astype(F32)
    attended[...] = output.astype(BF16)


def feature_body(place, grads, raw, w_q, w_k, w_v, *outs):
    count = len(outs)
    rows = grads.shape[0]
    head, width = w_k.shape[1], w_q.shape[1]
    features = w_q.shape[0] // count
    dot = jnp.sum(grads[...].astype(F32) * raw[...], axis=-1, keepdims=True)
    high = dot.astype(BF16).astype(F32)
    tail = lanes_of([high, dot - high], rows).astype(BF16)
    for index, out in enumerate(outs):
        start = pl.multiple_of(lax.rem(place[0] + index, count) * features, 128)
        part = nt(grads[:, :width], w_q[pl.ds(start, features), :])
        part = part + nt(grads[:, width : width + head], w_k[pl.ds(start, features), :])
        part = part + nt(grads[:, width + head :], w_v[pl.ds(start, features), :])
        out[:, :features] = part.astype(BF16)
        out[:, features:] = tail


def input_back_body(a, b, c, d, hidden, inverses, gain, out):
    features = hidden.shape[1]
    total = a[...].astype(F32) + b[...].astype(F32) + c[...].astype(F32) + d[...].astype(F32)
    dot = total[:, features : features + 1] + total[:, features + 1 : features + 2]
    mean = dot / (features * 4)
    inverse = inverses[:, 5:6]
    hat = hidden[...].astype(F32) * inverse
    out[...] = (inverse * (gain[...] * total[:, :features] - hat * mean)).astype(BF16)


def weight_body(place, *refs):
    sources, outs, product = refs[: 2 * COLUMN], refs[2 * COLUMN : -1], refs[-1]
    turned = jnp.concatenate([ref[...] for ref in sources[:COLUMN]], axis=1)
    grads = jnp.concatenate([ref[...] for ref in sources[COLUMN:]], axis=0)
    product[...] = nn(turned, grads).astype(BF16)
    rows = product.shape[0] // RING
    for index, out in enumerate(outs):
        start = pl.multiple_of(lax.rem(place[0] + index, RING) * rows, 16)
        out[...] = product[pl.ds(start, rows), :]


def weight_terms(place, turned, grads):
    rows, columns = turned[0].shape[0], grads[0].shape[1]
    return call(
        weight_body,
        [shape((rows // RING, columns), BF16)] * RING,
        [place] + turned + grads,
        smem=1,
        scratch=[pltpu.VMEM((rows, columns), BF16)],
        name="weight_terms",
    )


def ring_sum(terms):
    up, down = terms[4], terms[5]
    for step in range(4):
        up = along_z(up, 1)
        if step < 3:
            up = plus(up, terms[3 - step])
            down = along_z(down, -1)
        if step < 2:
            down = plus(down, terms[6 + step])
    return [terms[0], up, down]


def collect_body(own, up, down, *outs):
    total = own[...].astype(F32) + up[...].astype(F32) + down[...].astype(F32)
    start = 0
    for out in outs:
        out[...] = total[:, start : start + out.shape[1]].astype(BF16)
        start += out.shape[1]


def across_z(terms):
    rows, columns = terms.shape
    rings = [[y * RING + z for z in range(RING)] for y in range(COLUMN)]
    terms = lax.all_to_all(terms, "seq", 0, 0, axis_index_groups=rings, tiled=True)
    return terms.reshape(RING, rows // RING, columns)


def along_z(value, step):
    pairs = [
        (y * RING + z, y * RING + (z + step) % RING) for y in range(COLUMN) for z in range(RING)
    ]
    return lax.ppermute(value, "seq", pairs)


def along_y(value, step):
    pairs = [
        (y * RING + z, (y + step) % COLUMN * RING + z) for y in range(COLUMN) for z in range(RING)
    ]
    return lax.ppermute(value, "seq", pairs)


def along_x(value, step):
    return lax.ppermute(value, "mp", [(x, (x + step) % 4) for x in range(4)])


def swapped(value):
    return lax.ppermute(value, "group", [(0, 1), (1, 0)])


def plus(*parts):
    total = parts[0].astype(F32)
    for part in parts[1:]:
        total = total + part.astype(F32)
    return total.astype(BF16)


def on_device(hidden, norm_gain, w_q, w_k, w_v, q_gain, k_gain, positions, reach, grad_out):
    place_x = lax.axis_index("mp").astype(jnp.int32)
    place = lax.axis_index("seq").astype(jnp.int32)
    place_y = place // RING
    rows, features = hidden.shape[1:]
    width = features * 4
    head = q_gain.shape[1]
    columns = w_q.shape[2]
    gain = norm_gain[0].reshape(1, width)
    local_gain = lax.dynamic_slice(gain, (0, place_x * features), (1, features))
    full = lax.all_gather(hidden[0], "mp", axis=1, tiled=True)
    sources = [gain, positions, reach, k_gain, q_gain, w_k[0], w_v[0], w_q[0]]
    projected = call(
        project_body,
        [
            shape((RING, 2 * rows + TAIL, head), BF16),
            shape((rows, columns + head), BF16),
            shape((rows, columns + 2 * head), F32),
            shape((rows, 128), F32),
        ]
        + [shape((features, rows), BF16)] * COLUMN,
        [place_y.reshape(1), full]
        + [pltpu.with_memory_space_constraint(value, pltpu.HBM) for value in sources],
        smem=1,
        far=range(2, 10),
        scratch=[pltpu.VMEM(value.shape, value.dtype) for value in sources]
        + [pltpu.VMEM((rows, width), BF16), pltpu.SemaphoreType.DMA((8,))],
        micros=4.0,
        name="project",
    )
    blocks, queries, raw, inverses = projected[:4]
    turned = list(projected[4:])
    own_blocks = across_z(blocks.reshape(-1, head)).reshape(blocks.shape)
    queries = [queries] + [along_y(queries, step) for step in range(1, COLUMN)]
    ups = [grad_out[0]] + [along_y(grad_out[0], step) for step in range(1, COLUMN)]
    own_blocks, ups = lax.optimization_barrier((own_blocks, ups))
    other_blocks = swapped(own_blocks)
    sums, own_kept = forward(own_blocks, queries, ups, None)
    summed, stats, other_kept = forward(other_blocks, queries, ups, sums)
    all_stats = [stats] + [along_y(stats, step) for step in range(1, COLUMN)]
    all_stats[1], turned = lax.optimization_barrier((all_stats[1], turned))
    turned = [turned[0]] + [along_y(turned[step], step) for step in range(1, COLUMN)]
    finished = call(
        finish_body,
        [
            shape((COLUMN * rows, columns), BF16),
            shape((COLUMN * rows, columns), BF16),
            shape((COLUMN * rows, 128), F32),
        ]
        + [shape((rows, columns), BF16)] * COLUMN,
        [summed] + all_stats + queries + ups,
        name="finish",
    )
    q_scaled, up_scaled, stats = finished[:3]
    outputs = finished[3:]
    other_terms, grad = backward(
        other_blocks, other_kept, up_scaled, q_scaled, stats, ups, None
    )
    grad, turned = lax.optimization_barrier((grad, turned))
    outs = backward(own_blocks, own_kept, up_scaled, q_scaled, stats, ups, grad)
    own_terms, query_grad = outs[0], list(outs[1:])
    own_terms = plus(own_terms, swapped(other_terms))
    own_terms, outputs = lax.optimization_barrier((own_terms, outputs))
    own_terms = across_z(own_terms)
    query_grad = [query_grad[0]] + [along_y(query_grad[step], -step) for step in range(1, COLUMN)]
    outputs = [outputs[0]] + [along_y(outputs[step], -step) for step in range(1, COLUMN)]
    query_grad, outputs = lax.optimization_barrier((query_grad, outputs))
    grads, attended = call(
        grads_body,
        [shape((rows, columns + 2 * head), BF16), shape((rows, columns), BF16)],
        query_grad + [own_terms, raw, inverses, q_gain, k_gain] + outputs,
        name="grads",
    )
    all_grads = [grads] + [along_y(grads, step) for step in range(1, COLUMN)]
    feature_parts = call(
        feature_body,
        [shape((rows, features + 128), BF16)] * 4,
        [place_x.reshape(1), grads, raw, w_q[0], w_k[0], w_v[0]],
        smem=1,
        micros=5.0,
        name="feature",
    )
    first_part, all_grads = lax.optimization_barrier((feature_parts[0], all_grads))
    place_z = lax.rem(place, RING).reshape(1)
    terms = weight_terms(place_z, turned, all_grads)
    sent = feature_parts[1:]
    terms = ring_sum(terms)
    feature_parts = [first_part] + [along_x(sent[k - 1], k) for k in range(1, 4)]
    input_grad = call(
        input_back_body,
        shape((rows, features), BF16),
        feature_parts + [hidden[0], inverses, local_gain],
        micros=8.0,
        name="input_back",
    )
    weight_rows = terms[0].shape[0]
    grad_wq, grad_wk, grad_wv = call(
        collect_body,
        [shape((weight_rows, size), BF16) for size in (columns, head, head)],
        terms,
        name="collect",
    )
    return (attended[None], input_grad[None], grad_wq[None], grad_wk[None], grad_wv[None])


def solution(mesh):
    return jax.shard_map(
        on_device,
        mesh=mesh,
        in_specs=(
            P("group", "seq", "mp"),
            P("group", None),
            P("group", None, "mp"),
            P("group", None, "mp"),
            P("group", None, "mp"),
            P("group", None),
            P("group", None),
            P("group", "seq"),
            P("group", "seq"),
            P("group", "seq", "mp"),
        ),
        out_specs=(P("group", "seq", "mp"),) * 5,
        check_vma=False,
    )
```
